32 devices in a mesh: dp: 4 (over y, x), section: 2 (over core), shard: 4 (over z).
Axes of the slice: x: 2, y: 2, z: 4, core: 2. Of those that a mesh axis runs over, the one named last changes fastest.
Arguments:
- boundary: bfloat16 [2, 24576, 512], P('section', ('dp', 'shard')), may hold values from -6 to 6
- segment_ids: int32 [24576], P(('dp', 'shard')), may hold values from 0 to 2, as said below
- token_valid: int32 [24576], P(('dp', 'shard')), may hold values from 0 to 1, as said below
- attention_gain: bfloat16 [2, 512], P('section', 'shard'), may hold values from 0.5 to 1.5
- attention_bias: bfloat16 [2, 512], P('section', 'shard'), may hold values from -1.796875 to 1.796875
- query_weight: bfloat16 [2, 512, 512], P('section', 'shard'), may hold values from -0.25 to 0.25
- key_weight: bfloat16 [2, 512, 512], P('section', 'shard'), may hold values from -0.25 to 0.25
- value_weight: bfloat16 [2, 512, 512], P('section', 'shard'), may hold values from -0.25 to 0.25
- key_conv: bfloat16 [2, 512, 3, 512], P('section', 'shard'), may hold values from -0.15625 to 0.15625
- value_conv: bfloat16 [2, 512, 3, 512], P('section', 'shard'), may hold values from -0.15625 to 0.15625
- out_weight: bfloat16 [2, 512, 512], P('section', 'shard'), may hold values from -1 to 1
- feed_gain: bfloat16 [2, 512], P('section', 'shard'), may hold values from 0.5 to 1.5
- feed_bias: bfloat16 [2, 512], P('section', 'shard'), may hold values from -1.796875 to 1.796875
- up_weight: bfloat16 [2, 512, 2048], P('section', 'shard'), may hold values from -0.25 to 0.25
- down_weight: bfloat16 [2, 2048, 512], P('section', 'shard'), may hold values from -0.125 to 0.125
Outputs:
- section_ends: bfloat16 [2, 24576, 512], P('section', ('dp', 'shard'))
- attention_gain_grad: float32 [2, 512], P('section', 'shard')
- attention_bias_grad: float32 [2, 512], P('section', 'shard')
- query_weight_grad: float32 [2, 512, 512], P('section', 'shard')
- key_weight_grad: float32 [2, 512, 512], P('section', 'shard')
- value_weight_grad: float32 [2, 512, 512], P('section', 'shard')
- key_conv_grad: float32 [2, 512, 3, 512], P('section', 'shard')
- value_conv_grad: float32 [2, 512, 3, 512], P('section', 'shard')
- out_weight_grad: float32 [2, 512, 512], P('section', 'shard')
- feed_gain_grad: float32 [2, 512], P('section', 'shard')
- feed_bias_grad: float32 [2, 512], P('section', 'shard')
- up_weight_grad: float32 [2, 512, 2048], P('section', 'shard')
- down_weight_grad: float32 [2, 2048, 512], P('section', 'shard')
The draws below stay inside these ranges and needn't reach their ends.
Inputs may be any that keep to these rules, and one draw needn't show every extreme that they name: `segment_ids`: within each row of 768 tokens the ids never fall; the first token has id 0 and the last id 2. `token_valid`: within each row of 768 tokens the ones come first, then between 1 and 192 zeros.
All inputs are finite; a program needn't handle non-finite values.
Results may differ from the reference program's by a relative error of at most 0.025.
Values may be sent and summed in bfloat16 or wider, within the bound.
No kernel may reach another device: no remote copies, remote signals or barrier semaphores. Data moves between devices by JAX's collectives and lax.ppermute only.
A program may use at most 192 MiB of HBM per device.

```python
import jax
import jax.numpy as jnp
from jax import lax

D = 512
H = 8
HD = 64
FF = 2048
BLK = 256
LEN = 768
TOKENS = 24576


def draw_segment_ids(key, part):
    key = jax.random.fold_in(key, 17)
    first_key, second_key = jax.random.split(key)
    row_count = TOKENS // LEN
    first_cut = jax.random.randint(first_key, (row_count, 1), 1, LEN)
    second_cut = jax.random.randint(second_key, (row_count, 1), 1, LEN)
    position = jnp.arange(LEN, dtype=jnp.int32)[None, :]
    segments = (position >= first_cut).astype(jnp.int32) + (position >= second_cut).astype(jnp.int32)
    return segments.reshape(-1)


def draw_token_valid(key, part):
    key = jax.random.fold_in(key, 29)
    row_count = TOKENS // LEN
    padding = jax.random.randint(key, (row_count, 1), 1, LEN // 4 + 1)
    position = jnp.arange(LEN, dtype=jnp.int32)[None, :]
    return (position < LEN - padding).astype(jnp.int32).reshape(-1)


def levels(own_key, extent, cuts, least, high):
    level = 1.0
    for dim, parts in cuts:
        heights = jax.random.uniform(jax.random.fold_in(jax.random.fold_in(own_key, 6), dim), (parts,), jnp.float32, least / len(cuts), high / len(cuts))
        level = level * jnp.repeat(jnp.exp(heights), extent[dim] // parts).reshape((-1,) + (1,) * (len(extent) - 1 - dim))
    return level


def noise(own_key, shape, width, reach, pieces=(), held_as=jnp.bfloat16):
    level = levels(own_key, shape, pieces, -0.22, 0.18) if pieces else 1.0
    values = jax.random.normal(own_key, shape, jnp.float32) * width * level
    return jnp.minimum(jnp.maximum(values, -reach), reach).astype(held_as)


def setup_inputs(seed: int = 0) -> dict:
    keys = jax.random.split(jax.random.key(seed), 16)
    return {
        "boundary": noise(keys[0], (2, TOKENS, D), 1.0, 6.0, ((0, 2), (1, 16))),
        "segment_ids": draw_segment_ids(jax.random.fold_in(keys[15], 71), 0),
        "token_valid": draw_token_valid(jax.random.fold_in(keys[15], 71), 0),
        "attention_gain": jnp.clip(1.0 + 0.1 * jax.random.normal(keys[3], (2, D), jnp.float32), 0.5, 1.5).astype(jnp.bfloat16),
        "attention_bias": noise(keys[4], (2, D), 0.3, 1.796875, ((0, 2), (1, 4))),
        "query_weight": noise(keys[5], (2, D, D), D ** -0.5, 0.25, ((0, 2), (1, 4))),
        "key_weight": noise(keys[6], (2, D, D), D ** -0.5, 0.25, ((0, 2), (1, 4))),
        "value_weight": noise(keys[7], (2, D, D), D ** -0.5, 0.25, ((0, 2), (1, 4))),
        "key_conv": noise(keys[8], (2, D, 3, D), (3 * D) ** -0.5, 0.15625, ((0, 2), (1, 4))),
        "value_conv": noise(keys[9], (2, D, 3, D), (3 * D) ** -0.5, 0.15625, ((0, 2), (1, 4))),
        "out_weight": noise(keys[10], (2, D, D), (D // 16) ** -0.5, 1.0, ((0, 2), (1, 4))),
        "feed_gain": jnp.clip(1.0 + 0.1 * jax.random.normal(keys[11], (2, D), jnp.float32), 0.5, 1.5).astype(jnp.bfloat16),
        "feed_bias": noise(keys[12], (2, D), 0.3, 1.796875, ((0, 2), (1, 4))),
        "up_weight": noise(keys[13], (2, D, FF), D ** -0.5, 0.25, ((0, 2), (1, 4))),
        "down_weight": noise(keys[14], (2, FF, D), FF ** -0.5, 0.125, ((0, 2), (1, 4))),
    }


@jax.custom_vjp
def low(v):
    return lax.optimization_barrier(v.astype(jnp.bfloat16)).astype(jnp.float32)

@jax.custom_vjp
def low_back(v):
    return v

def low_keep(v):
    return (low(v), None)

def low_pass(kept, grad):
    return (grad,)

def back_keep(v):
    return (v, None)

def back_low(kept, grad):
    return (low(grad),)
low.defvjp(low_keep, low_pass)
low_back.defvjp(back_keep, back_low)
EPSILON = 1e-05
NEGATIVE = -1e+30
HIGHEST = lax.Precision.HIGHEST

def normalize(hidden, norm_gain, norm_shift):
    centred = hidden - lax.optimization_barrier(jnp.mean(hidden, axis=-1, keepdims=True))
    spread = lax.optimization_barrier(jnp.mean(centred * centred, axis=-1, keepdims=True))
    return centred * lax.rsqrt(spread + EPSILON) * norm_gain + norm_shift

def product(former, latter):
    return jnp.dot(former, latter, precision=HIGHEST)

def geometry(segments, validity, block_len):
    windows = segments.shape[0] // 3
    seg_taps = segments.reshape(windows, 3)
    valid_taps = validity.reshape(windows, 3)
    seg_anchor = seg_taps[:, 2]
    tap_mask = (seg_taps == seg_anchor[:, None]) & (valid_taps == 1)
    anchor = jnp.arange(windows, dtype=jnp.int32) * 3 + 2
    position = jnp.arange(segments.shape[0], dtype=jnp.int32)
    allowed = (anchor[None, :] <= position[:, None]) & (seg_anchor[None, :] == segments[:, None])
    allowed = allowed & (valid_taps[:, 2][None, :] == 1) & (anchor[None, :] // block_len == position[:, None] // block_len)
    return (tap_mask, allowed)

def run_layer(hidden, segments, validity, weights, block_len):
    attention_gain, attention_bias, query_weight, key_weight, value_weight, key_conv, value_conv, out_weight, feed_gain, feed_bias, up_weight, down_weight = weights
    length = hidden.shape[0]
    windows = length // 3
    tap_mask, allowed = geometry(segments, validity, block_len)
    tap_float = tap_mask.astype(jnp.float32)[:, :, None]
    normed = low(normalize(hidden, attention_gain, attention_bias))
    query_rows = low(low_back(product(normed, query_weight)))
    key_rows = low(low_back(product(normed, key_weight)))
    value_rows = low(low_back(product(normed, value_weight)))
    key_taps = key_rows.reshape(windows, 3, D) * tap_float
    value_taps = value_rows.reshape(windows, 3, D) * tap_float
    packed_keys = low(low_back(jnp.einsum('jti,ito->jo', key_taps, key_conv, precision=HIGHEST)))
    packed_values = low(low_back(jnp.einsum('jti,ito->jo', value_taps, value_conv, precision=HIGHEST)))
    scores = jnp.einsum('thd,jhd->htj', query_rows.reshape(length, H, HD), packed_keys.reshape(windows, H, HD), precision=HIGHEST)
    scores = low_back(scores * HD ** (-0.5))
    masked = jnp.where(allowed[None], scores, NEGATIVE)
    top_score = jnp.maximum(lax.optimization_barrier(jnp.max(masked, axis=-1, keepdims=True)), 0.0)
    numerator = jnp.where(allowed[None], jnp.exp(masked - top_score), 0.0)
    attn_probs = low(numerator / (jnp.exp(-top_score) + lax.optimization_barrier(jnp.sum(numerator, axis=-1, keepdims=True))))
    mixed_heads = jnp.einsum('htj,jhd->thd', attn_probs, packed_values.reshape(windows, H, HD), precision=HIGHEST)
    mixed_heads = low(low_back(mixed_heads.reshape(length, D)))
    middle = hidden + low_back(product(mixed_heads, out_weight))
    normed_two = low(normalize(middle, feed_gain, feed_bias))
    activated = low(jax.nn.gelu(low_back(product(normed_two, up_weight)), approximate=False))
    return middle + low_back(product(activated, down_weight))

def row_forward(params, row_input, segments, validity):
    lower = jax.tree.map(lambda stacked: stacked[0], params)
    upper = jax.tree.map(lambda stacked: stacked[1], params)
    between = low(low_back(run_layer(row_input, segments, validity, lower, BLK)))
    return run_layer(between, segments, validity, upper, LEN)

def reference(boundary, segment_ids, token_valid, attention_gain, attention_bias, query_weight, key_weight, value_weight, key_conv, value_conv, out_weight, feed_gain, feed_bias, up_weight, down_weight):
    row_count = boundary.shape[1] // LEN
    inputs = boundary[0].astype(jnp.float32).reshape(row_count, LEN, D)
    cotangent = boundary[1].astype(jnp.float32).reshape(row_count, LEN, D)
    segments = segment_ids.reshape(row_count, LEN)
    validity = token_valid.reshape(row_count, LEN)
    params = tuple((weight.astype(jnp.float32) for weight in (attention_gain, attention_bias, query_weight, key_weight, value_weight, key_conv, value_conv, out_weight, feed_gain, feed_bias, up_weight, down_weight)))
    checked = jax.checkpoint(row_forward)

    def forward(rows_in, weights):

        def one_row(entry_row):
            return checked(weights, entry_row[0], entry_row[1], entry_row[2])
        return lax.map(one_row, (rows_in, segments, validity))
    outputs, pullback = jax.vjp(forward, inputs, params)
    grad_inputs, grad_params = pullback(cotangent)
    section_ends = jnp.stack([grad_inputs.reshape(-1, D), outputs.reshape(-1, D)]).astype(jnp.bfloat16)
    return (section_ends, grad_params[0], grad_params[1], grad_params[2], grad_params[3], grad_params[4], grad_params[5], grad_params[6], grad_params[7], grad_params[8], grad_params[9], grad_params[10], grad_params[11])
```

```python
import functools
import jax
import jax.numpy as jnp
from jax import lax
from jax.experimental import pallas as pl
from jax.experimental.pallas import tpu as pltpu
from jax.sharding import PartitionSpec as P

D = 512
H = 8
HD = 64
FF = 2048
BLK = 256
LEN = 768
WIN = LEN // 3
EPSILON = 1e-05
NEGATIVE = -1e30
F32 = jnp.float32
BF16 = jnp.bfloat16
LOG2E = 1.4426950408889634
VMEM = pl.BlockSpec(memory_space=pltpu.VMEM)


def nn(a, b):
    return lax.dot_general(a, b, (((1,), (0,)), ((), ())), preferred_element_type=F32)


def nt(a, b):
    return lax.dot_general(a, b, (((1,), (1,)), ((), ())), preferred_element_type=F32)


def tn(a, b):
    return lax.dot_general(a, b, (((0,), (0,)), ((), ())), preferred_element_type=F32)


def norm_parts(hidden):
    centred = hidden - jnp.mean(hidden, axis=-1, keepdims=True)
    spread = jnp.mean(centred * centred, axis=-1, keepdims=True)
    scale = lax.rsqrt(spread + EPSILON)
    return centred * scale, scale


def norm_back(grad, hat, scale, gain):
    inner = grad * gain
    mean_one = jnp.mean(inner, axis=-1, keepdims=True)
    mean_two = jnp.mean(inner * hat, axis=-1, keepdims=True)
    return scale * (inner - mean_one - hat * mean_two)


def gelu_both(z):
    x = jnp.abs(z) * 0.7071067811865476
    d = 1.0 + 0.3275911 * x
    t = 1.0 / d
    e = jnp.exp2(z * z * (-0.5 * LOG2E))
    poly = t * (0.5 * 0.254829592 + t * (0.5 * -0.284496736 + t * (0.5 * 1.421413741 + t * (0.5 * -1.453152027 + t * (0.5 * 1.061405429)))))
    tail = poly * e
    phi = jnp.where(z < 0.0, tail, 1.0 - tail)
    return z * phi, phi + z * (e * 0.3989422804014327)


def head_mask(rows):
    lane = lax.broadcasted_iota(jnp.int32, (rows, 256), 1) // HD
    return [lane == i for i in range(4)]


def attn_fwd(h_ref, bias_ref, tap_ref, gain_ref, shift_ref, wq_ref, wk_ref, wv_ref, kc_ref, vc_ref, wo_ref,
             h2_ref, q_ref, kt_ref, vt_ref, ck_ref, cv_ref, p_ref, ot_ref, n_ref):
    gain = gain_ref[...].astype(F32)
    shift = shift_ref[...].astype(F32)

    @pl.loop(0, 3)
    def _(t):
        rows = pl.ds(pl.multiple_of(t * WIN, WIN), WIN)
        hat, _s = norm_parts(h_ref[rows, :].astype(F32))
        n = (hat * gain + shift).astype(BF16)
        tap = tap_ref[rows, :]
        q_ref[rows, :] = nn(n, wq_ref[...]).astype(BF16)
        kt_ref[rows, :] = (nn(n, wk_ref[...]) * tap).astype(BF16)
        vt_ref[rows, :] = (nn(n, wv_ref[...]) * tap).astype(BF16)

    ck = sum(nn(kt_ref[t * WIN:(t + 1) * WIN, :], kc_ref[t]) for t in range(3))
    ck_ref[...] = ck.astype(BF16)
    cv = sum(nn(vt_ref[t * WIN:(t + 1) * WIN, :], vc_ref[t]) for t in range(3))
    cv_ref[...] = cv.astype(BF16)
    masks = head_mask(WIN)
    zero = jnp.zeros((WIN, 256), BF16)

    @pl.loop(0, 3)
    def _(t):
        rows = pl.ds(pl.multiple_of(t * WIN, WIN), WIN)
        bias = bias_ref[:, rows]
        for g in range(2):
            cols = slice(g * 256, g * 256 + 256)
            qg = q_ref[rows, cols]
            total = None
            for i in range(4):
                ckm = jnp.where(masks[i], ck_ref[:, cols], zero)
                s = nt(ckm, qg) * (0.125 * LOG2E) + bias
                top = jnp.maximum(jnp.max(s, axis=0, keepdims=True), 0.0)
                num = jnp.exp2(s - top)
                den = jnp.exp2(-top) + jnp.sum(num, axis=0, keepdims=True)
                p = (num * (1.0 / den)).astype(BF16)
                p_ref[g * 4 + i, :, rows] = p
                cvm = jnp.where(masks[i], cv_ref[:, cols], zero)
                part = tn(cvm, p)
                total = part if total is None else total + part
            ot_ref[cols, rows] = total.astype(BF16)

    @pl.loop(0, 3)
    def _(t):
        rows = pl.ds(pl.multiple_of(t * WIN, WIN), WIN)
        h2_ref[rows, :] = h_ref[rows, :].astype(F32) + tn(ot_ref[:, rows], wo_ref[...])


def feed_fwd(h2_ref, gain_ref, shift_ref, wu_ref, wd_ref, y_ref, a_ref, gd_ref):
    gain = gain_ref[...].astype(F32)
    shift = shift_ref[...].astype(F32)

    @pl.loop(0, 3)
    def _(t):
        rows = pl.ds(pl.multiple_of(t * WIN, WIN), WIN)
        h2 = h2_ref[rows, :]
        hat, _s = norm_parts(h2)
        n = (hat * gain + shift).astype(BF16)
        total = h2
        for c in range(4):
            cols = slice(c * 512, c * 512 + 512)
            act, slope = gelu_both(nn(n, wu_ref[:, cols]))
            act = act.astype(BF16)
            a_ref[rows, cols] = act
            gd_ref[rows, cols] = slope.astype(BF16)
            total = total + nn(act, wd_ref[cols, :])
        y_ref[rows, :] = total.astype(BF16)


ROW = ((LEN, D), BF16)
ROWF = ((LEN, D), F32)
WIN_ = ((WIN, D), BF16)
SQ = ((D, D), BF16)
CV = ((3, D, D), BF16)
VEC = ((1, D), F32)


def slot_of(piece, replica, core, bits):
    rel = piece ^ replica
    return sum(((rel >> k) & 1) << (bits - 1 - k) for k in range(bits)) if core == 0 else rel


def send_halves(idx_ref, first, second, keep_ref, send_ref, sems):
    core = idx_ref[1]
    copies = []
    for here in range(2):
        pairs = [(src, keep_ref if here == half else send_ref, dst)
                 for half, items in ((0, first), (1, second)) for src, dst in items]

        @pl.when(core == here)
        def _():
            for i, (src, out, dst) in enumerate(pairs):
                pltpu.make_async_copy(src, out.at[dst], sems.at[i]).start()
        copies = pairs
    return copies


def wait_halves(copies, keep_ref, sems):
    for i, (src, out, dst) in enumerate(copies):
        pltpu.make_async_copy(src, keep_ref.at[dst], sems.at[i]).wait()


def fill_vectors(vec_ref, rows):
    vec_ref[...] = jnp.zeros_like(vec_ref)
    parts, block = vec_ref.shape[0], D // vec_ref.shape[0]
    for z in range(parts):
        for i, row in enumerate(rows):
            vec_ref[z, i:i + 1, :block] = row[:, z * block:(z + 1) * block].astype(BF16)


def feed_bwd(idx_ref, gout_ref, h2_ref, gain_ref, shift_ref, wu_ref, wd_ref, a_ref, gd_ref,
             gh2_ref, keep_ref, send_ref, gz_ref, n_ref, gwu_ref, gwd_ref, vec_ref, gg_ref, gb_ref, sems):
    gain = gain_ref[...].astype(F32)
    shift = shift_ref[...].astype(F32)
    gg_ref[...] = jnp.zeros_like(gg_ref)
    gb_ref[...] = jnp.zeros_like(gb_ref)

    @pl.loop(0, 3)
    def _(t):
        rows = pl.ds(pl.multiple_of(t * WIN, WIN), WIN)
        gout = gout_ref[rows, :]
        hat, scale = norm_parts(h2_ref[rows, :])
        n_ref[rows, :] = (hat * gain + shift).astype(BF16)
        gn = None
        for c in range(4):
            cols = slice(c * 512, c * 512 + 512)
            gz = (nt(gout, wd_ref[cols, :]) * gd_ref[rows, cols].astype(F32)).astype(BF16)
            gz_ref[rows, cols] = gz
            part = nt(gz, wu_ref[:, cols])
            gn = part if gn is None else gn + part
        gg_ref[...] += jnp.sum(gn * hat, axis=0, keepdims=True)
        gb_ref[...] += jnp.sum(gn, axis=0, keepdims=True)
        gh2_ref[rows, :] = gout.astype(F32) + norm_back(gn, hat, scale, gain)

    parts, quarters = gwu_ref.shape[0], keep_ref.shape[0]
    block = D // parts
    fill_vectors(vec_ref, [gg_ref[...], gb_ref[...]])

    @pl.loop(0, 4)
    def _(c):
        cols = pl.ds(pl.multiple_of(c * 512, 512), 512)
        here = pl.ds(c * (parts // 4), parts // 4)
        gwd_ref[here] = tn(a_ref[:, cols], gout_ref[...]).astype(BF16).reshape(parts // 4, 4 * block, D)
        gwu_ref[:, :, cols] = tn(n_ref[...], gz_ref[:, cols]).astype(BF16).reshape(parts, block, 512)

    first, second = [], []
    bits = quarters.bit_length() - 1
    wide = FF // quarters
    for q in range(quarters):
        slot = slot_of(q, idx_ref[0], 0, bits)
        first.append((gwd_ref.at[:, :, q * 128:q * 128 + 128], (slot, slice(None), pl.ds(0, 4 * block))))
        first.append((vec_ref, (slot, slice(None), pl.ds(4 * block, 16))))
        slot = slot_of(q, idx_ref[0], 1, bits)
        for i in range(wide // 128):
            second.append((gwu_ref.at[:, :, q * wide + i * 128:q * wide + i * 128 + 128],
                           (slot, slice(None), pl.ds(i * block, block))))
        second.append((vec_ref, (slot, slice(None), pl.ds(4 * block, 16))))
    wait_halves(send_halves(idx_ref, first, second, keep_ref, send_ref, sems), keep_ref, sems)


def attn_bwd(idx_ref, gh2_ref, h_ref, tap_ref, gain_ref, shift_ref, wq_ref, wk_ref, wv_ref, kc_ref, vc_ref, wo_ref,
             q_ref, kt_ref, vt_ref, ck_ref, cv_ref, p_ref, ot_ref,
             gh_ref, keep_ref, send_ref,
             gob_ref, go_ref, gq_ref, gk_ref, gv_ref, gck_ref, gcv_ref, n_ref, gw_ref, vec_ref, gg_ref, gb_ref, sems):
    gain = gain_ref[...].astype(F32)
    shift = shift_ref[...].astype(F32)
    gg_ref[...] = jnp.zeros_like(gg_ref)
    gb_ref[...] = jnp.zeros_like(gb_ref)
    gck_ref[...] = jnp.zeros_like(gck_ref)
    gcv_ref[...] = jnp.zeros_like(gcv_ref)
    parts, quarters = gw_ref.shape[1], keep_ref.shape[0]
    block = D // parts
    shaped = (parts, block, D)

    @pl.loop(0, 3)
    def _(t):
        rows = pl.ds(pl.multiple_of(t * WIN, WIN), WIN)
        gob = gh2_ref[rows, :].astype(BF16)
        gob_ref[rows, :] = gob
        go_ref[rows, :] = nt(gob, wo_ref[...]).astype(BF16)

    gw_ref[6] = nn(ot_ref[...], gob_ref[...]).astype(BF16).reshape(shaped)
    masks = head_mask(WIN)
    zero = jnp.zeros((WIN, 256), BF16)

    @pl.loop(0, 3)
    def _(t):
        rows = pl.ds(pl.multiple_of(t * WIN, WIN), WIN)
        for g in range(2):
            cols = slice(g * 256, g * 256 + 256)
            gog = go_ref[rows, cols]
            qg = q_ref[rows, cols]
            gq = None
            for i in range(4):
                cvm = jnp.where(masks[i], cv_ref[:, cols], zero)
                ckm = jnp.where(masks[i], ck_ref[:, cols], zero)
                gp = nt(cvm, gog)
                pb = p_ref[g * 4 + i, :, rows]
                p = pb.astype(F32)
                pg = p * gp
                gs = (pg - p * jnp.sum(pg, axis=0, keepdims=True)).astype(BF16)
                gcv_ref[:, cols] += jnp.where(masks[i], nn(pb, gog), 0.0)
                gck_ref[:, cols] += jnp.where(masks[i], nn(gs, qg), 0.0)
                part = tn(gs, ckm)
                gq = part if gq is None else gq + part
            gq_ref[rows, cols] = (gq * 0.125).astype(BF16)

    gck = (gck_ref[...] * 0.125).astype(BF16)
    gcv = gcv_ref[...].astype(BF16)
    for t in range(3):
        rows = slice(t * WIN, t * WIN + WIN)
        tap = tap_ref[rows, :]
        gk_ref[rows, :] = (nt(gck, kc_ref[t]) * tap).astype(BF16)
        gv_ref[rows, :] = (nt(gcv, vc_ref[t]) * tap).astype(BF16)
        gw_ref[2 + t] = tn(kt_ref[rows, :], gck).astype(BF16).reshape(shaped)
        gw_ref[7 + t] = tn(vt_ref[rows, :], gcv).astype(BF16).reshape(shaped)

    @pl.loop(0, 3)
    def _(t):
        rows = pl.ds(pl.multiple_of(t * WIN, WIN), WIN)
        hat, scale = norm_parts(h_ref[rows, :].astype(F32))
        n_ref[rows, :] = (hat * gain + shift).astype(BF16)
        gn = nt(gq_ref[rows, :], wq_ref[...]) + nt(gk_ref[rows, :], wk_ref[...]) + nt(gv_ref[rows, :], wv_ref[...])
        gg_ref[...] += jnp.sum(gn * hat, axis=0, keepdims=True)
        gb_ref[...] += jnp.sum(gn, axis=0, keepdims=True)
        gh_ref[rows, :] = (gh2_ref[rows, :] + norm_back(gn, hat, scale, gain)).astype(BF16)

    fill_vectors(vec_ref, [gg_ref[...], gb_ref[...]])
    across = n_ref[...].T
    gw_ref[0] = nn(across, gq_ref[...]).astype(BF16).reshape(shaped)
    gw_ref[1] = nn(across, gk_ref[...]).astype(BF16).reshape(shaped)
    gw_ref[5] = nn(across, gv_ref[...]).astype(BF16).reshape(shaped)

    halves = [], []
    bits = quarters.bit_length() - 1
    for q in range(quarters):
        for half in range(2):
            slot = slot_of(q, idx_ref[0], half, bits)
            for u in range(5):
                halves[half].append((gw_ref.at[half * 5 + u, :, :, q * 128:q * 128 + 128],
                                     (slot, slice(None), pl.ds(u * block, block))))
            halves[half].append((vec_ref, (slot, slice(None), pl.ds(5 * block, 16))))
    wait_halves(send_halves(idx_ref, halves[0], halves[1], keep_ref, send_ref, sems), keep_ref, sems)


def geometry(segments, validity, block_len):
    seg = segments.reshape(WIN, 3)
    val = validity.reshape(WIN, 3)
    anchor_seg = seg[:, 2]
    tap = ((seg == anchor_seg[:, None]) & (val == 1)).astype(F32).T.reshape(LEN, 1)
    seg_t = seg.T.reshape(LEN)
    position = (jnp.arange(WIN, dtype=jnp.int32)[None, :] * 3 + jnp.arange(3, dtype=jnp.int32)[:, None]).reshape(LEN)
    anchor = jnp.arange(WIN, dtype=jnp.int32) * 3 + 2
    allowed = (anchor[:, None] <= position[None, :]) & (anchor_seg[:, None] == seg_t[None, :])
    allowed = allowed & (val[:, 2][:, None] == 1) & (anchor[:, None] // block_len == position[None, :] // block_len)
    return tap, jnp.where(allowed, 0.0, NEGATIVE).astype(F32)


def tap_major(x):
    return x.reshape(WIN, 3, -1).transpose(1, 0, 2).reshape(LEN, -1)


def row_major(x):
    return x.reshape(3, WIN, -1).transpose(1, 0, 2).reshape(LEN, -1)


ANY = pl.BlockSpec(memory_space=pl.ANY)
SMEM = pl.BlockSpec(memory_space=pltpu.SMEM)


def place_shards(idx_ref, *refs):
    pieces, out_ref, sems = refs[:-2], refs[-2], refs[-1]
    n = len(pieces)
    copies = [pltpu.make_async_copy(piece, out_ref.at[lax.rem(idx_ref[2] + n - k, n)], sems.at[k])
              for k, piece in enumerate(pieces)]
    for copy in copies:
        copy.start()
    for copy in copies:
        copy.wait()


def relative(index, core, bits):
    back = sum(((index >> k) & 1) << (bits - 1 - k) for k in range(bits))
    return jnp.where(core == 0, back, index)


def assemble(units, quarters, idx_ref, *refs):
    own, other = refs[:quarters], refs[quarters:2 * quarters]
    outs, sems = refs[2 * quarters:-1], refs[-1]
    core, replica = idx_ref[1], idx_ref[0]
    bits = quarters.bit_length() - 1
    block = outs[0].shape[-2] if len(outs) > 2 else outs[1].shape[-2]
    made = []
    for here in range(2):
        made = []
        for half in range(2):
            for m in range(quarters):
                piece = (own if half == here else other)[m]
                made += units(half, piece, outs, replica ^ relative(m, half, bits), block)

        @pl.when(core == here)
        def _():
            for i, (src, dst) in enumerate(made):
                pltpu.make_async_copy(src, dst, sems.at[i]).start()
    for i, (src, dst) in enumerate(made):
        pltpu.make_async_copy(src, dst, sems.at[i]).wait()


def lanes(quarter, width):
    return pl.ds(pl.multiple_of(quarter * width, 128), 128)


def attn_units(half, piece, outs, quarter, block):
    cols = lanes(quarter, 128)
    targets = ([outs[0], outs[1]] + [outs[4].at[t] for t in range(3)],
               [outs[2], outs[3]] + [outs[5].at[t] for t in range(3)])[half]
    return [(piece.at[:, pl.ds(u * block, block), :], target.at[:, :, cols]) for u, target in enumerate(targets)]


def feed_units(half, piece, outs, quarter, block):
    if half == 0:
        return [(piece, outs[0].at[:, :, lanes(quarter, 128)])]
    return [(piece.at[:, pl.ds(i * block, block), :],
             outs[1].at[:, :, pl.ds(pl.multiple_of(quarter * 512 + i * 128, 128), 128)]) for i in range(4)]


def add_halves(order, idx_ref, keep_a, keep_b, recv_a, recv_b, out_a, out_b):
    out_a[...] = (keep_a[...].astype(F32) + recv_a[...].astype(F32)).astype(BF16)
    out_b[...] = (keep_b[...].astype(F32) + recv_b[...].astype(F32)).astype(BF16)


def add_split(idx, keep, recv, in_shard_order):
    m, rows, _ = keep.shape
    half = m // 2
    bits = m.bit_length() - 1

    def where(i, idx_ref):
        if in_shard_order:
            return sum(((i >> k) & 1) << (bits - 1 - k) for k in range(bits)) ^ idx_ref[2]
        return i

    block = (1, rows, 128)
    low = pl.BlockSpec(block, lambda i, s: (where(i, s), 0, 0))
    high = pl.BlockSpec(block, lambda i, s: (where(i + half, s), 0, 0))
    out = pl.BlockSpec(block, lambda i, s: (i, 0, 0))
    return pl.pallas_call(
        functools.partial(add_halves, in_shard_order),
        grid_spec=pltpu.PrefetchScalarGridSpec(
            num_scalar_prefetch=1, grid=(half,), in_specs=[low, high, low, high], out_specs=[out, out]),
        out_shape=[jax.ShapeDtypeStruct((half, rows, 128), BF16)] * 2,
        cost_estimate=pl.CostEstimate(flops=m * rows * 128, bytes_accessed=m * rows * 128 * 6, transcendentals=0),
        name="add_split",
    )(idx, keep, keep, recv, recv)


def unpack(units, quarters, idx_ref, *refs):
    layers = (refs[:2 * quarters], refs[2 * quarters:4 * quarters])
    outs, held, sems = refs[4 * quarters:-2], refs[-2], refs[-1]
    core, replica = idx_ref[1], idx_ref[0]
    bits = quarters.bit_length() - 1
    for here in range(2):
        @pl.when(core == here)
        def _():
            for m in range(quarters):
                for side in range(2):
                    source = layers[here][m if side == here else quarters + m]
                    pltpu.make_async_copy(source, held.at[side, replica ^ relative(m, side, bits)],
                                          sems.at[side * quarters + m]).start()
    for m in range(quarters):
        for side in range(2):
            pltpu.make_async_copy(layers[0][m], held.at[side, m], sems.at[side * quarters + m]).wait()
    units(held, outs)


def attn_unpack(held, outs):
    block = outs[0].shape[0]
    for q in range(held.shape[1]):
        cols = slice(q * 128, q * 128 + 128)
        for half in range(2):
            for u in range(5):
                value = held[half, q, u * block:(u + 1) * block, :].astype(F32)
                if u < 2:
                    outs[half * 2 + u][:, cols] = value
                else:
                    outs[4 + half][u - 2, :, cols] = value


def feed_unpack(held, outs):
    block = outs[1].shape[0]
    for q in range(held.shape[1]):
        outs[0][:, q * 128:q * 128 + 128] = held[0, q, :4 * block, :].astype(F32)
        for i in range(4):
            cols = slice(q * 512 + i * 128, q * 512 + i * 128 + 128)
            outs[1][:, cols] = held[1, q, i * block:(i + 1) * block, :].astype(F32)


def plain(kernel, in_specs, outs, out_specs, scratch, name, us, *args):
    return pl.pallas_call(
        kernel,
        out_shape=[jax.ShapeDtypeStruct(s, d) for s, d in outs],
        in_specs=in_specs,
        out_specs=out_specs,
        scratch_shapes=scratch,
        compiler_params=pltpu.CompilerParams(vmem_limit_bytes=56 * 2**20),
        cost_estimate=pl.CostEstimate(flops=int(us * 1.1e9), bytes_accessed=2**20, transcendentals=0),
        name=name,
    )(*args)


def swap_cores(value):
    return lax.ppermute(value, "section", [(0, 1), (1, 0)])


def dp_swap(value, step, bits):
    route = []
    for replica in range(2**bits):
        for core in range(2):
            bit = step if core == 0 else bits - 1 - step
            route.append((replica * 2 + core, (replica ^ (1 << bit)) * 2 + core))
    return lax.ppermute(value, ("dp", "section"), route)


def spread(piece, bits):
    pieces = [piece]
    for step in reversed(range(bits)):
        pieces += [dp_swap(held, step, bits) for held in pieces]
    return pieces


def shard_gather(idx, piece, n):
    if n > 8:
        return lax.all_gather(piece, "shard", axis=0)
    pieces = [piece] + [lax.ppermute(piece, "shard", [(i, (i + k) % n) for i in range(n)]) for k in range(1, n)]
    return plain(place_shards, [SMEM] + [ANY] * n, [((n,) + piece.shape, BF16)], [VMEM],
                 [pltpu.SemaphoreType.DMA((n,))], "place_shards", 1, idx, *pieces)[0]


def gather_weights(idx, piece, n, bits, units, outs, name):
    here = shard_gather(idx, piece, n)
    own = spread(here, bits)
    other = [swap_cores(held) for held in own]
    count = 2 ** bits * 10
    made = plain(functools.partial(assemble, units, 2**bits), [SMEM] + [ANY] * (2 * len(own)),
                 [(s, BF16) for s in outs], [VMEM] * len(outs), [pltpu.SemaphoreType.DMA((count,))], name, 2,
                 idx, *own, *other)
    return here, made


def reduce_grads(idx, keep, send, n, bits):
    rows = keep.shape[2]
    shape = (-1, rows, 128)
    recv = swap_cores(send).reshape(shape)
    keep = keep.reshape(shape)
    for step in range(bits):
        keep, send = add_split(idx, keep, recv, False)
        recv = dp_swap(send, step, bits)
    ordered = True
    for step in range(n.bit_length() - 1):
        keep, send = add_split(idx, keep, recv, ordered)
        recv = lax.ppermute(send, "shard", [(i, i ^ (1 << step)) for i in range(n)])
        ordered = False
    total = (keep[0].astype(F32) + recv[0].astype(F32)).astype(BF16)
    own = spread(total, bits)
    other = [swap_cores(held) for held in own]
    return own + other


def body(boundary, segment_ids, token_valid, attention_gain, attention_bias, query_weight, key_weight, value_weight,
         key_conv, value_conv, out_weight, feed_gain, feed_bias, up_weight, down_weight):
    core = lax.axis_index("section")
    replica = lax.axis_index("dp")
    first = core == 0
    quarters = lax.axis_size("dp")
    bits = quarters.bit_length() - 1
    n = lax.axis_size("shard")
    block = D // n
    idx = jnp.stack([replica, core, lax.axis_index("shard")]).astype(jnp.int32)

    own_rows = boundary[0].reshape(2, LEN, D)
    mine = lax.dynamic_index_in_dim(own_rows, core, 0, keepdims=False)
    theirs = swap_cores(lax.dynamic_index_in_dim(own_rows, 1 - core, 0, keepdims=False))
    h = tap_major(jnp.where(first, mine, theirs))
    cot = tap_major(jnp.where(first, theirs, mine))
    segments = lax.dynamic_index_in_dim(segment_ids.reshape(2, LEN), core, 0, keepdims=False)
    validity = lax.dynamic_index_in_dim(token_valid.reshape(2, LEN), core, 0, keepdims=False)

    def quarter(weight, width=128):
        return lax.dynamic_slice_in_dim(weight, replica * width, width, weight.ndim - 1)

    vectors = jnp.stack([attention_gain[0], attention_bias[0], feed_gain[0], feed_bias[0]])
    vectors = jnp.pad(vectors, ((0, 12), (0, 128 - block)))
    key_taps = quarter(key_conv[0]).transpose(1, 0, 2).reshape(3 * block, 128)
    value_taps = quarter(value_conv[0]).transpose(1, 0, 2).reshape(3 * block, 128)
    attn_halves = (jnp.concatenate([quarter(query_weight[0]), quarter(key_weight[0]), key_taps, vectors]),
                   jnp.concatenate([quarter(value_weight[0]), quarter(out_weight[0]), value_taps, vectors]))
    up_part = quarter(up_weight[0], 512).reshape(block, 4, 128).transpose(1, 0, 2).reshape(4 * block, 128)
    feed_halves = (quarter(down_weight[0]), up_part)
    pieces = []
    for halves in (attn_halves, feed_halves):
        kept = jnp.where(first, halves[0], halves[1])
        got = swap_cores(jnp.where(first, halves[1], halves[0]))
        pieces.append((jnp.where(first, kept, got), jnp.where(first, got, kept)))

    square, conv = (n, block, D), (3, n, block, D)
    layers = []
    for layer in range(2):
        here, attn = gather_weights(idx, pieces[0][layer], n, bits, attn_units, [square] * 4 + [conv] * 2, "assemble_attn")
        _, feed = gather_weights(idx, pieces[1][layer], n, bits, feed_units, [(n, 4 * block, D), (n, block, FF)],
                                 "assemble_feed")
        gains = here[:, 5 * block:5 * block + 4, :block].transpose(1, 0, 2).reshape(4, 1, D)
        wq, wk, wv, wo = [w.reshape(D, D) for w in attn[:4]]
        kc, vc = [w.reshape(3, D, D) for w in attn[4:]]
        layers.append((gains, (wq, wk, wv, kc, vc, wo), feed[1].reshape(D, FF), feed[0].reshape(FF, D)))

    saved = []
    for layer, length in ((0, BLK), (1, LEN)):
        gains, attn, up, down = layers[layer]
        tap, bias = geometry(segments, validity, length)
        h2, *kept = plain(attn_fwd, [VMEM] * 11, [ROWF, ROW, ROW, ROW, WIN_, WIN_, ((H, WIN, LEN), BF16), ((D, LEN), BF16)],
                          [VMEM] * 8, [pltpu.VMEM((LEN, D), BF16)], "attn_fwd", 14, h, bias, tap, gains[0], gains[1], *attn)
        y, act, slope = plain(feed_fwd, [VMEM] * 5, [ROW, ((LEN, FF), BF16), ((LEN, FF), BF16)], [VMEM] * 3, [],
                              "feed_fwd", 14, h2, gains[2], gains[3], up, down)
        saved.append((h, tap, h2, kept, act, slope))
        h = y
    result = h

    grad = cot
    reduced = [None, None]
    rows_attn, rows_feed = 5 * block + 16, 4 * block + 16
    for layer in (1, 0):
        gains, attn, up, down = layers[layer]
        h, tap, h2, kept, act, slope = saved[layer]
        shape = (quarters, n, rows_feed, 128)
        gh2, keep, send = plain(
            feed_bwd, [SMEM] + [VMEM] * 8, [ROWF, (shape, BF16), (shape, BF16)], [VMEM, ANY, ANY],
            [pltpu.VMEM((LEN, FF), BF16), pltpu.VMEM((LEN, D), BF16), pltpu.VMEM((n, block, FF), BF16),
             pltpu.VMEM((n, 4 * block, D), BF16), pltpu.VMEM((n, 16, 128), BF16), pltpu.VMEM((1, D), F32),
             pltpu.VMEM((1, D), F32), pltpu.SemaphoreType.DMA((quarters * 7,))],
            "feed_bwd", 16, idx, grad, h2, gains[2], gains[3], up, down, act, slope)
        feed_sums = reduce_grads(idx, keep, send, n, bits)
        shape = (quarters, n, rows_attn, 128)
        grad, keep, send = plain(
            attn_bwd, [SMEM] + [VMEM] * 18, [ROW, (shape, BF16), (shape, BF16)], [VMEM, ANY, ANY],
            [pltpu.VMEM((LEN, D), BF16)] * 5 + [pltpu.VMEM((WIN, D), F32)] * 2 + [pltpu.VMEM((LEN, D), BF16)]
            + [pltpu.VMEM((10, n, block, D), BF16), pltpu.VMEM((n, 16, 128), BF16), pltpu.VMEM((1, D), F32),
               pltpu.VMEM((1, D), F32), pltpu.SemaphoreType.DMA((quarters * 12,))],
            "attn_bwd", 19, idx, gh2, h, tap, gains[0], gains[1], *attn, *kept)
        attn_sums = reduce_grads(idx, keep, send, n, bits)
        reduced[layer] = (attn_sums, feed_sums)

    result, grad = row_major(result), row_major(grad)
    other = swap_cores(jnp.where(first, result, grad))
    ours = jnp.where(first, grad, result)
    section_ends = jnp.stack([jnp.where(first, ours, other), jnp.where(first, other, ours)]).reshape(1, 2 * LEN, D)

    def finish(which, units, outs, rows, name):
        return plain(functools.partial(unpack, units, quarters), [SMEM] + [ANY] * (4 * quarters),
                     [(s, F32) for s in outs], [VMEM] * len(outs),
                     [pltpu.VMEM((2, quarters, rows, 128), BF16), pltpu.SemaphoreType.DMA((2 * quarters,))],
                     name, 2, idx, *reduced[0][which], *reduced[1][which])

    gq, gk, gv, go, gkc, gvc = finish(0, attn_unpack, [(block, D)] * 4 + [(3, block, D)] * 2, rows_attn, "unpack_attn")
    gdown, gup = finish(1, feed_unpack, [(4 * block, D), (block, FF)], rows_feed, "unpack_feed")
    at, ft = 5 * block, 4 * block
    vec_attn = jnp.where(first, reduced[0][0][0][at:at + 2, :block], reduced[1][0][0][at:at + 2, :block]).astype(F32)
    vec_feed = jnp.where(first, reduced[0][1][0][ft:ft + 2, :block], reduced[1][1][0][ft:ft + 2, :block]).astype(F32)
    return (section_ends, vec_attn[0:1], vec_attn[1:2], gq[None], gk[None], gv[None], gkc.transpose(1, 0, 2)[None],
            gvc.transpose(1, 0, 2)[None], go[None], vec_feed[0:1], vec_feed[1:2], gup[None], gdown[None])


def solution(mesh):
    vector, matrix, conv = P("section", "shard"), P("section", "shard", None), P("section", "shard", None, None)
    rows, tokens = P("section", ("dp", "shard"), None), P(("dp", "shard"))
    weights = (vector, vector, matrix, matrix, matrix, conv, conv, matrix, vector, vector, matrix, matrix)
    return jax.shard_map(body, mesh=mesh, in_specs=(rows, tokens, tokens) + weights, out_specs=(rows,) + weights,
                         check_vma=False)
```

```python
import functools

import jax
import jax.numpy as jnp
from jax import lax
from jax.experimental import pallas as pl
from jax.experimental.pallas import tpu as pltpu
from jax.sharding import PartitionSpec as P

D = 512
H = 8
HD = 64
FF = 2048
BLK = 256
LEN = 768
WIN = LEN // 3
EPSILON = 1e-05
NEGATIVE = -1e30
F32 = jnp.float32
BF16 = jnp.bfloat16
LOG2E = 1.4426950408889634
VMEM = pl.BlockSpec(memory_space=pltpu.VMEM)
ANY = pl.BlockSpec(memory_space=pl.ANY)
SMEM = pl.BlockSpec(memory_space=pltpu.SMEM)
DMA = pltpu.SemaphoreType.DMA
VMEM_BYTES = 60 * 2**20
ROW = (LEN, D)
Q, K, KC, V, O, VC = 0, 1, 2, 5, 6, 7


def nn(a, b):
    return lax.dot_general(a, b, (((1,), (0,)), ((), ())), preferred_element_type=F32)


def nt(a, b):
    return lax.dot_general(a, b, (((1,), (1,)), ((), ())), preferred_element_type=F32)


def tn(a, b):
    return lax.dot_general(a, b, (((0,), (0,)), ((), ())), preferred_element_type=F32)


def norm_parts(hidden):
    centred = hidden - jnp.mean(hidden, axis=-1, keepdims=True)
    spread = jnp.mean(centred * centred, axis=-1, keepdims=True)
    scale = lax.rsqrt(spread + EPSILON)
    return centred * scale, scale


def norm_back(grad, hat, scale, gain):
    inner = grad * gain
    mean_one = jnp.mean(inner, axis=-1, keepdims=True)
    mean_two = jnp.mean(inner * hat, axis=-1, keepdims=True)
    return scale * (inner - mean_one - hat * mean_two)


def gelu_both(z):
    phi = 0.5 + 0.5 * lax.erf(z * 0.7071067811865476)
    density = jnp.exp2(z * z * (-0.5 * LOG2E)) * 0.3989422804014327
    return z * phi, phi + z * density


def head_mask(rows):
    lane = lax.broadcasted_iota(jnp.int32, (rows, 256), 1) // HD
    return [lane == i for i in range(4)]


def relative(index, core, bits):
    return sum(((index >> k) & 1) << (bits - 1 - k) for k in range(bits)) if core == 0 else index


class Moves:
    def __init__(self, sems):
        self.sems, self.items = sems, []

    def start(self, src, dst):
        copy = pltpu.make_async_copy(src, dst, self.sems.at[len(self.items)])
        copy.start()
        self.items.append(copy)
        return copy

    def wait(self):
        for copy in self.items:
            copy.wait()


def fetch_pieces(idx_ref, own, other, units, sems):
    core, replica = idx_ref[1], idx_ref[0]
    bits = len(own).bit_length() - 1
    for here in range(2):
        made = []
        for half in range(2):
            for m in range(len(own)):
                piece = (own if half == here else other)[m]
                made += units(half, piece, replica ^ relative(m, half, bits))

        @pl.when(core == here)
        def _():
            for i, (src, dst) in enumerate(made):
                pltpu.make_async_copy(src, dst, sems.at[i]).start()
    return [pltpu.make_async_copy(src, dst, sems.at[i]) for i, (src, dst) in enumerate(made)]


def send_halves(idx_ref, halves, keep_ref, send_ref, sems, base=0):
    core = idx_ref[1]
    for here in range(2):
        @pl.when(core == here)
        def _():
            i = base
            for half in range(2):
                for src, dst in halves[half]:
                    out = keep_ref if here == half else send_ref
                    pltpu.make_async_copy(src, out.at[dst], sems.at[i]).start()
                    i += 1
    items = halves[0] + halves[1]
    return [pltpu.make_async_copy(src, keep_ref.at[dst], sems.at[base + i]) for i, (src, dst) in enumerate(items)]


def fill_vectors(vec_ref, rows):
    vec_ref[...] = jnp.zeros_like(vec_ref)
    parts, block = vec_ref.shape[0], D // vec_ref.shape[0]
    for z in range(parts):
        for i, row in enumerate(rows):
            vec_ref[z, i:i + 1, :block] = row[:, z * block:(z + 1) * block].astype(BF16)


def wait_all(copies):
    for copy in copies:
        copy.wait()


def attn_fwd(quarters, at, idx_ref, h_ref, bias_ref, tap_ref, gain_ref, shift_ref, *refs):
    own, other = refs[:quarters], refs[quarters:2 * quarters]
    (h2_ref, q_out, kt_out, vt_out, ck_out, cv_out, p_out, ot_out, w_out,
     w_ref, q_ref, kt_ref, vt_ref, ck_ref, cv_ref, p_ref, ot_ref, n_ref, across_ref, in_sems, out_sems) = refs[2 * quarters:]
    block = w_ref.shape[2]

    def units(half, piece, quarter):
        cols = pl.ds(pl.multiple_of(quarter * 128, 128), 128)
        return [(piece.at[:, pl.ds(at + u * block, block), :], w_ref.at[half * 5 + u, :, :, cols]) for u in range(5)]

    fetched = fetch_pieces(idx_ref, own, other, units, in_sems)
    out = Moves(out_sems)

    def weight(u):
        return w_ref[u].reshape(D, D)

    hat, _s = norm_parts(h_ref[...].astype(F32))
    n_ref[...] = (hat * gain_ref[...].astype(F32) + shift_ref[...].astype(F32)).astype(BF16)
    wait_all(fetched)
    out.start(w_ref, w_out)
    tap = tap_ref[...]
    kt_ref[...] = (nn(n_ref[...], weight(K)) * tap).astype(BF16)
    vt_ref[...] = (nn(n_ref[...], weight(V)) * tap).astype(BF16)
    q_ref[...] = nn(n_ref[...], weight(Q)).astype(BF16)
    out.start(q_ref, q_out)
    out.start(kt_ref, kt_out)
    out.start(vt_ref, vt_out)
    ck_ref[...] = sum(nn(kt_ref[t * WIN:(t + 1) * WIN, :], weight(KC + t)) for t in range(3)).astype(BF16)
    cv_ref[...] = sum(nn(vt_ref[t * WIN:(t + 1) * WIN, :], weight(VC + t)) for t in range(3)).astype(BF16)
    out.start(ck_ref, ck_out)
    out.start(cv_ref, cv_out)
    masks = head_mask(WIN)
    zero = jnp.zeros((WIN, 256), BF16)
    for g in range(2):
        cols = slice(g * 256, g * 256 + 256)
        for i in range(4):
            across_ref[:, i * WIN:i * WIN + WIN] = jnp.where(masks[i], cv_ref[:, cols], zero).T
        for i in range(4):
            s = nt(jnp.where(masks[i], ck_ref[:, cols], zero), q_ref[:, cols]) * (0.125 * LOG2E) + bias_ref[...]
            top = jnp.maximum(jnp.max(s, axis=0, keepdims=True), 0.0)
            num = jnp.exp2(s - top)
            den = jnp.exp2(-top) + jnp.sum(num, axis=0, keepdims=True)
            p_ref[g * 4 + i] = (num * (1.0 / den)).astype(BF16)
        heads = pl.ds(g * 4, 4)
        out.start(p_ref.at[heads], p_out.at[heads])
        ot_ref[cols, :] = nn(across_ref[...], p_ref[heads].reshape(4 * WIN, LEN)).astype(BF16)
    out.start(ot_ref, ot_out)
    h2_ref[...] = h_ref[...].astype(F32) + tn(ot_ref[...], weight(O))
    out.wait()


def feed_fwd(quarters, at, idx_ref, h2_ref, gain_ref, shift_ref, *refs):
    own, other = refs[:quarters], refs[quarters:2 * quarters]
    (y_ref, a_out, gd_out, wu_out, wd_out, wu_ref, wd_ref, a_ref, gd_ref, n_ref, in_sems, out_sems) = refs[2 * quarters:]
    block = wu_ref.shape[1]

    def units(half, piece, quarter):
        if half == 0:
            return [(piece.at[:, pl.ds(at, 4 * block), :], wd_ref.at[:, :, pl.ds(pl.multiple_of(quarter * 128, 128), 128)])]
        return [(piece.at[:, pl.ds(at + i * block, block), :],
                 wu_ref.at[:, :, pl.ds(pl.multiple_of(quarter * 512 + i * 128, 128), 128)]) for i in range(4)]

    fetched = fetch_pieces(idx_ref, own, other, units, in_sems)
    hat, _s = norm_parts(h2_ref[...])
    n_ref[...] = (hat * gain_ref[...].astype(F32) + shift_ref[...].astype(F32)).astype(BF16)
    wait_all(fetched)
    out = Moves(out_sems)
    out.start(wu_ref, wu_out)
    out.start(wd_ref, wd_out)
    chunks = [slice(c * 512, c * 512 + 512) for c in range(4)]

    def up(c):
        return nn(n_ref[...], wu_ref[:, :, chunks[c]].reshape(D, 512))

    total = h2_ref[...]
    z = up(0)
    for c in range(4):
        later = up(c + 1) if c < 3 else None
        act, slope = gelu_both(z)
        act = act.astype(BF16)
        a_ref[:, chunks[c]] = act
        gd_ref[:, chunks[c]] = slope.astype(BF16)
        out.start(a_ref.at[:, chunks[c]], a_out.at[:, chunks[c]])
        out.start(gd_ref.at[:, chunks[c]], gd_out.at[:, chunks[c]])
        total = total + nn(act, wd_ref[...].reshape(FF, D)[chunks[c], :])
        z = later
    y_ref[...] = total.astype(BF16)
    out.wait()


def feed_bwd(idx_ref, gout_ref, h2_ref, gain_ref, shift_ref, wu_in, wd_in, a_in, gd_in,
             gh2_ref, keep_ref, send_ref, wu_ref, wd_ref, a_ref, gd_ref, gz_ref, n_ref, gwu_ref, gwd_ref, vec_ref,
             in_sems, sems):
    arriving = Moves(in_sems)
    for src, dst in ((a_in, a_ref), (wd_in, wd_ref), (gd_in, gd_ref), (wu_in, wu_ref)):
        arriving.start(src, dst)
    parts, quarters = gwu_ref.shape[0], keep_ref.shape[0]
    block = D // parts
    bits = quarters.bit_length() - 1
    wide = FF // quarters
    gain = gain_ref[...].astype(F32)
    hat, scale = norm_parts(h2_ref[...])
    n_ref[...] = (hat * gain + shift_ref[...].astype(F32)).astype(BF16)
    arriving.items[0].wait()
    gwd_ref[...] = tn(a_ref[...], gout_ref[...]).astype(BF16).reshape(parts, 4 * block, D)
    slots = [[relative(q ^ idx_ref[0], half, bits) for half in range(2)] for q in range(quarters)]
    down = [(gwd_ref.at[:, :, q * 128:q * 128 + 128], (slots[q][0], slice(None), pl.ds(0, 4 * block)))
            for q in range(quarters)]
    copies = send_halves(idx_ref, (down, []), keep_ref, send_ref, sems)
    wait_all(arriving.items[1:3])
    for c in range(4):
        cols = slice(c * 512, c * 512 + 512)
        gz_ref[:, cols] = (nt(gout_ref[...], wd_ref[cols, :]) * gd_ref[:, cols].astype(F32)).astype(BF16)
    arriving.items[3].wait()
    gwu_ref[...] = tn(n_ref[...], gz_ref[...]).astype(BF16).reshape(parts, block, FF)
    up = [(gwu_ref.at[:, :, q * wide + i * 128:q * wide + i * 128 + 128],
           (slots[q][1], slice(None), pl.ds(i * block, block))) for q in range(quarters) for i in range(wide // 128)]
    copies += send_halves(idx_ref, ([], up), keep_ref, send_ref, sems, len(copies))
    gn = nt(gz_ref[...], wu_ref[...])
    hat, scale = norm_parts(h2_ref[...])
    fill_vectors(vec_ref, [jnp.sum(gn * hat, axis=0, keepdims=True), jnp.sum(gn, axis=0, keepdims=True)])
    vectors = [[(vec_ref, (slots[q][half], slice(None), pl.ds(4 * block, 16))) for q in range(quarters)]
               for half in range(2)]
    copies += send_halves(idx_ref, vectors, keep_ref, send_ref, sems, len(copies))
    gh2_ref[...] = gout_ref[...].astype(F32) + norm_back(gn, hat, scale, gain)
    wait_all(copies)


def attn_bwd(idx_ref, gh2_ref, tap_ref, w_in, q_in, kt_in, vt_in, ck_ref, cv_ref, p_in,
             gq_out, gk_out, gv_out, keep_ref, send_ref,
             w_ref, q_ref, kt_ref, vt_ref, p_ref, go_ref, gq_ref, gk_ref, gv_ref, gck_ref, gcv_ref, gw_ref, gs_ref, across_ref,
             in_sems, out_sems, sems):
    arriving = Moves(in_sems)
    arriving.start(w_in.at[O], w_ref.at[6])
    arriving.start(q_in, q_ref)
    arriving.start(p_in, p_ref)
    arriving.start(w_in.at[pl.ds(KC, 3)], w_ref.at[pl.ds(0, 3)])
    arriving.start(w_in.at[pl.ds(VC, 3)], w_ref.at[pl.ds(3, 3)])
    arriving.start(kt_in, kt_ref)
    arriving.start(vt_in, vt_ref)
    out = Moves(out_sems)
    parts, quarters = gw_ref.shape[1], keep_ref.shape[0]
    block = D // parts
    shaped = (parts, block, D)
    wait_all(arriving.items[:1])
    go_ref[...] = nt(gh2_ref[...].astype(BF16), w_ref[6].reshape(D, D)).astype(BF16)
    masks = head_mask(WIN)
    zero = jnp.zeros((WIN, 256), BF16)
    wait_all(arriving.items[1:3])

    def own_lanes(stacked):
        return sum(jnp.where(masks[i], stacked[i * WIN:(i + 1) * WIN, :], 0.0) for i in range(4))

    for g in range(2):
        cols = slice(g * 256, g * 256 + 256)
        for i in range(4):
            across_ref[:, i * WIN:i * WIN + WIN] = jnp.where(masks[i], ck_ref[:, cols], zero).T
        for i in range(4):
            gp = nt(jnp.where(masks[i], cv_ref[:, cols], zero), go_ref[:, cols])
            p = p_ref[g * 4 + i].astype(F32)
            pg = p * gp
            gs_ref[i * WIN:i * WIN + WIN, :] = (pg - p * jnp.sum(pg, axis=0, keepdims=True)).astype(BF16)
        stacked = p_ref[pl.ds(g * 4, 4)].reshape(4 * WIN, LEN)
        gcv_ref[:, cols] = own_lanes(nn(stacked, go_ref[:, cols])).astype(BF16)
        gck_ref[:, cols] = (own_lanes(nn(gs_ref[...], q_ref[:, cols])) * 0.125).astype(BF16)
        gq_ref[:, cols] = (nn(across_ref[...], gs_ref[...]) * 0.125).astype(BF16).T

    out.start(gq_ref, gq_out)
    gck, gcv = gck_ref[...], gcv_ref[...]
    wait_all(arriving.items[3:])
    for t in range(3):
        rows = slice(t * WIN, t * WIN + WIN)
        gw_ref[t] = tn(kt_ref[rows, :], gck).astype(BF16).reshape(shaped)
        gw_ref[3 + t] = tn(vt_ref[rows, :], gcv).astype(BF16).reshape(shaped)

    halves = [], []
    bits = quarters.bit_length() - 1
    for q in range(quarters):
        for half in range(2):
            slot = relative(q ^ idx_ref[0], half, bits)
            for u in range(3):
                halves[half].append((gw_ref.at[half * 3 + u, :, :, q * 128:q * 128 + 128],
                                     (slot, slice(None), pl.ds(u * block, block))))
    copies = send_halves(idx_ref, halves, keep_ref, send_ref, sems)
    for t in range(3):
        rows = slice(t * WIN, t * WIN + WIN)
        tap = tap_ref[rows, :]
        gk_ref[rows, :] = (nt(gck, w_ref[t].reshape(D, D)) * tap).astype(BF16)
        gv_ref[rows, :] = (nt(gcv, w_ref[3 + t].reshape(D, D)) * tap).astype(BF16)
    out.start(gk_ref, gk_out)
    out.start(gv_ref, gv_out)
    wait_all(copies)
    out.wait()


def proj_bwd(idx_ref, gh2_ref, h_ref, gain_ref, shift_ref, w_in, gq_ref, gk_ref, gv_ref, ot_in,
             gh_ref, keep_ref, send_ref, w_ref, ot_ref, n_ref, gw_ref, vec_ref, in_sems, sems):
    arriving = Moves(in_sems)
    arriving.start(w_in.at[pl.ds(Q, 2)], w_ref.at[pl.ds(0, 2)])
    arriving.start(w_in.at[V], w_ref.at[2])
    arriving.start(ot_in, ot_ref)
    gain = gain_ref[...].astype(F32)
    parts, quarters = gw_ref.shape[1], keep_ref.shape[0]
    block = D // parts
    shaped = (parts, block, D)
    bits = quarters.bit_length() - 1
    slots = [[relative(q ^ idx_ref[0], half, bits) for half in range(2)] for q in range(quarters)]
    hat, scale = norm_parts(h_ref[...].astype(F32))
    n_ref[...] = (hat * gain + shift_ref[...].astype(F32)).astype(BF16)
    arriving.wait()
    gn = (nt(gq_ref[...], w_ref[0].reshape(D, D)) + nt(gk_ref[...], w_ref[1].reshape(D, D))
          + nt(gv_ref[...], w_ref[2].reshape(D, D)))
    fill_vectors(vec_ref, [jnp.sum(gn * hat, axis=0, keepdims=True), jnp.sum(gn, axis=0, keepdims=True)])
    vectors = [[(vec_ref, (slots[q][half], slice(None), pl.ds(2 * block, 16))) for q in range(quarters)]
               for half in range(2)]
    copies = send_halves(idx_ref, vectors, keep_ref, send_ref, sems)
    gh_ref[...] = (gh2_ref[...] + norm_back(gn, hat, scale, gain)).astype(BF16)
    gw_ref[3] = nn(ot_ref[...], gh2_ref[...].astype(BF16)).astype(BF16).reshape(shaped)
    across = n_ref[...].T
    for u, grad in enumerate((gq_ref, gk_ref, gv_ref)):
        gw_ref[u] = nn(across, grad[...]).astype(BF16).reshape(shaped)
    weights = [[(gw_ref.at[half * 2 + u, :, :, q * 128:q * 128 + 128], (slots[q][half], slice(None), pl.ds(u * block, block)))
                for q in range(quarters) for u in range(2)] for half in range(2)]
    copies += send_halves(idx_ref, weights, keep_ref, send_ref, sems, len(copies))
    wait_all(copies)


def place_shards(idx_ref, *refs):
    pieces, out_ref, sems = refs[:-2], refs[-2], refs[-1]
    n = len(pieces)
    copies = [pltpu.make_async_copy(piece, out_ref.at[lax.rem(idx_ref[2] + n - k, n)], sems.at[k])
              for k, piece in enumerate(pieces)]
    for copy in copies:
        copy.start()
    wait_all(copies)


def add_kernel(jobs, idx_ref, *refs):
    outs = refs[sum(2 * groups * chunks for groups, chunks in jobs):]
    at_in = at_out = 0
    for groups, chunks in jobs:
        at = 0
        for _ in range(chunks):
            for g in range(groups):
                keep, recv = refs[at_in], refs[at_in + 1]
                at_in += 2
                rows = keep.shape[1]
                outs[at_out + g][:, at:at + rows, :] = (keep[...].astype(F32) + recv[...].astype(F32)).astype(BF16)
            at += rows
        at_out += groups


def add_parts(idx, jobs, deps=()):
    sizes = [chunks[0][0].shape[0] // groups for chunks, groups, _ in jobs]
    steps = min(min(sizes), 4)
    in_specs, out_specs, shapes, args, plan = [], [], [], [], []
    for (chunks, groups, index), each in zip(jobs, sizes):
        lead = each // steps
        total = sum(keep.shape[1] for keep, _ in chunks)
        plan.append((groups, len(chunks)))
        for keep, recv in chunks:
            for g in range(groups):
                if index:
                    where = functools.partial(lambda g, i, s: (index(g, i, s), 0, 0), g)
                else:
                    where = functools.partial(lambda g, i, s: (i + g * steps, 0, 0), g)
                in_specs += [pl.BlockSpec((lead, keep.shape[1], 128), where)] * 2
                args += [keep, recv]
        out_specs += [pl.BlockSpec((lead, total, 128), lambda i, s: (i, 0, 0))] * groups
        shapes += [jax.ShapeDtypeStruct((each, total, 128), BF16)] * groups
    count = len(args)

    def with_deps(idx_ref, *refs):
        add_kernel(plan, idx_ref, *refs[:count], *refs[count + len(deps):])

    made = pl.pallas_call(
        with_deps,
        grid_spec=pltpu.PrefetchScalarGridSpec(
            num_scalar_prefetch=1, grid=(steps,), in_specs=in_specs + [ANY] * len(deps), out_specs=out_specs),
        out_shape=shapes,
        compiler_params=pltpu.CompilerParams(vmem_limit_bytes=VMEM_BYTES),
        cost_estimate=pl.CostEstimate(flops=4 * 10**9, bytes_accessed=2**20, transcendentals=0),
        name="add_parts",
    )(idx, *args, *deps)
    split, at = [], 0
    for groups, _ in plan:
        split.append(made[at:at + groups])
        at += groups
    return split


def unpack(quarters, rows, plans, units, idx_ref, *refs):
    outs, held, sems = refs[2 * quarters:-2], refs[-2], refs[-1]
    core, replica = idx_ref[1], idx_ref[0]
    for here in range(2):
        total, at = plans[here]

        @pl.when(core == here)
        def _():
            for k in range(quarters):
                for half in range(2):
                    start = at + (0 if half == here else total)
                    pltpu.make_async_copy(refs[here * quarters + k].at[pl.ds(start, rows), :],
                                          held.at[half, replica ^ k], sems.at[half * quarters + k]).start()
    for k in range(quarters):
        for half in range(2):
            pltpu.make_async_copy(refs[k].at[pl.ds(0, rows), :], held.at[half, k], sems.at[half * quarters + k]).wait()
    units(held, outs)


def proj_unpack(held, outs):
    block = outs[0].shape[0]
    for q in range(held.shape[1]):
        for u in range(4):
            outs[u][:, q * 128:q * 128 + 128] = held[u // 2, q, u % 2 * block:(u % 2 + 1) * block, :].astype(F32)


def conv_unpack(held, outs):
    block = outs[0].shape[1]
    for q in range(held.shape[1]):
        for half in range(2):
            for t in range(3):
                outs[half][t, :, q * 128:q * 128 + 128] = held[half, q, t * block:(t + 1) * block, :].astype(F32)


def feed_unpack(held, outs):
    block = outs[1].shape[0]
    for q in range(held.shape[1]):
        outs[0][:, q * 128:q * 128 + 128] = held[0, q, :4 * block, :].astype(F32)
        for i in range(4):
            cols = slice(q * 512 + i * 128, q * 512 + i * 128 + 128)
            outs[1][:, cols] = held[1, q, i * block:(i + 1) * block, :].astype(F32)


def plain(kernel, in_specs, outs, out_specs, scratch, name, us, *args, deps=()):
    count = len(args)

    def with_deps(*refs):
        kernel(*refs[:count], *refs[count + len(deps):])

    return pl.pallas_call(
        with_deps,
        out_shape=[jax.ShapeDtypeStruct(s, d) for s, d in outs],
        in_specs=list(in_specs) + [ANY] * len(deps),
        out_specs=out_specs,
        scratch_shapes=scratch,
        compiler_params=pltpu.CompilerParams(vmem_limit_bytes=VMEM_BYTES),
        cost_estimate=pl.CostEstimate(flops=int(us * 1.1e9), bytes_accessed=2**20, transcendentals=0),
        name=name,
    )(*args, *deps)


def geometry(segments, validity, block_len):
    seg = segments.reshape(WIN, 3)
    val = validity.reshape(WIN, 3)
    anchor_seg = seg[:, 2]
    tap = ((seg == anchor_seg[:, None]) & (val == 1)).astype(F32).T.reshape(LEN, 1)
    seg_t = seg.T.reshape(LEN)
    window = jnp.arange(WIN, dtype=jnp.int32)
    position = (window[None, :] * 3 + jnp.arange(3, dtype=jnp.int32)[:, None]).reshape(LEN)
    anchor = window * 3 + 2
    allowed = (anchor[:, None] <= position[None, :]) & (anchor_seg[:, None] == seg_t[None, :])
    allowed = allowed & (val[:, 2][:, None] == 1) & (anchor[:, None] // block_len == position[None, :] // block_len)
    return tap, jnp.where(allowed, 0.0, NEGATIVE).astype(F32)


def tap_major(x):
    return x.reshape(WIN, 3, -1).transpose(1, 0, 2).reshape(LEN, -1)


def row_major(x):
    return x.reshape(3, WIN, -1).transpose(1, 0, 2).reshape(LEN, -1)


def tie(value, *others):
    return lax.optimization_barrier((value,) + others)[0]


def swap_cores(value):
    return lax.ppermute(value, "section", [(0, 1), (1, 0)])


def dp_swap(value, step, bits):
    route = []
    for replica in range(2**bits):
        for core in range(2):
            bit = step if core == 0 else bits - 1 - step
            route.append((replica * 2 + core, (replica ^ (1 << bit)) * 2 + core))
    return lax.ppermute(value, ("dp", "section"), route)


def shard_gather(idx, piece, n, deps=()):
    if n > 8:
        return lax.all_gather(piece, "shard", axis=0)
    pieces = [piece] + [lax.ppermute(piece, "shard", [(i, (i + k) % n) for i in range(n)]) for k in range(1, n)]
    return plain(place_shards, [SMEM] + [ANY] * n, [((n,) + piece.shape, BF16)], [VMEM], [DMA((n,))],
                 "place_shards", 1, idx, *pieces, deps=deps)[0]


def shard_step(value, step, n):
    return lax.ppermute(value, "shard", [(i, i ^ (1 << step)) for i in range(n)])


def shard_order(bits):
    def index(g, i, idx_ref):
        place = i + g * (1 << (bits - 1))
        return sum(((place >> k) & 1) << (bits - 1 - k) for k in range(bits)) ^ idx_ref[2]
    return index


class Sums:
    def __init__(self, keep, recv):
        self.keep, self.recv = keep, recv


class Hops:
    def __init__(self, idx, n, bits):
        self.idx, self.n, self.bits, self.last = idx, n, bits, None

    def run(self, *jobs):
        n = self.n
        direct = n <= 8
        listed = []
        for chunks, what in jobs:
            pairs = [(c.keep, c.recv) for c in chunks]
            if what == "shard" and direct:
                listed.append((pairs, n, lambda g, i, s: lax.rem(s[2] + g, n)))
            elif what == "shard":
                listed.append((pairs, 2, shard_order(n.bit_length() - 1)))
            else:
                listed.append((pairs, 2, None))
        made = add_parts(self.idx, listed, () if self.last is None else (self.last,))
        self.last = made[0][0]
        results = []
        for (chunks, what), parts in zip(jobs, made):
            if what == "shard" and direct:
                got = [lax.ppermute(parts[k], "shard", [(i, (i + k) % n) for i in range(n)]) for k in range(1, n)]
                results.append(sum([parts[0].astype(F32)] + [g.astype(F32) for g in got])[0].astype(BF16))
            elif what == "shard":
                keep, recv = parts[0], shard_step(parts[1], 0, n)
                for step in range(1, n.bit_length() - 1):
                    (keep, send), = add_parts(self.idx, [([(keep, recv)], 2, None)])
                    recv = shard_step(send, step, n)
                results.append((keep[0].astype(F32) + recv[0].astype(F32)).astype(BF16))
            else:
                results.append(Sums(parts[0], dp_swap(parts[1], what, self.bits)))
        return results

    def collect(self, total, owner):
        total = tie(total, self.last)
        both = jnp.concatenate([total, lax.ppermute(total, "section", [(1 - owner, owner)])])
        quarters = 2**self.bits
        return [both] + [lax.ppermute(both, ("dp", "section"),
                                      [(2 * i + owner, 2 * (i ^ k) + owner) for i in range(quarters)])
                         for k in range(1, quarters)]


def body(boundary, segment_ids, token_valid, attention_gain, attention_bias, query_weight, key_weight, value_weight,
         key_conv, value_conv, out_weight, feed_gain, feed_bias, up_weight, down_weight):
    core = lax.axis_index("section")
    replica = lax.axis_index("dp")
    first = core == 0
    quarters = lax.axis_size("dp")
    bits = quarters.bit_length() - 1
    n = lax.axis_size("shard")
    block = D // n
    idx = jnp.stack([replica, core, lax.axis_index("shard")]).astype(jnp.int32)

    def quarter(weight, width=128):
        return lax.dynamic_slice_in_dim(weight, replica * width, width, weight.ndim - 1)

    vectors = jnp.stack([attention_gain[0], attention_bias[0], feed_gain[0], feed_bias[0]])
    vectors = jnp.pad(vectors, ((0, 12), (0, 128 - block)))
    key_taps = quarter(key_conv[0]).transpose(1, 0, 2).reshape(3 * block, 128)
    value_taps = quarter(value_conv[0]).transpose(1, 0, 2).reshape(3 * block, 128)
    attn_halves = (jnp.concatenate([quarter(query_weight[0]), quarter(key_weight[0]), key_taps, vectors]),
                   jnp.concatenate([quarter(value_weight[0]), quarter(out_weight[0]), value_taps, vectors]))
    up_part = quarter(up_weight[0], 512).reshape(block, 4, 128).transpose(1, 0, 2).reshape(4 * block, 128)
    feed_halves = (quarter(down_weight[0]), up_part)
    pieces = []
    for halves in (attn_halves, feed_halves):
        kept = jnp.where(first, halves[0], halves[1])
        got = swap_cores(jnp.where(first, halves[1], halves[0]))
        pieces.append((jnp.where(first, kept, got), jnp.where(first, got, kept)))

    own_rows = boundary[0].reshape(2, LEN, D)
    mine = lax.dynamic_index_in_dim(own_rows, core, 0, keepdims=False)
    theirs = swap_cores(lax.dynamic_index_in_dim(own_rows, 1 - core, 0, keepdims=False))
    h = tap_major(jnp.where(first, mine, theirs))
    cot = tap_major(jnp.where(first, theirs, mine))
    segments = lax.dynamic_index_in_dim(segment_ids.reshape(2, LEN), core, 0, keepdims=False)
    validity = lax.dynamic_index_in_dim(token_valid.reshape(2, LEN), core, 0, keepdims=False)

    square = (n, block, D)
    saved = []

    def run_attn_fwd(length, h, here, own, other, deps):
        gains = here[:, 5 * block:5 * block + 4, :block].transpose(1, 0, 2).reshape(4, 1, D)
        tap, bias = geometry(segments, validity, length)
        outs = [(ROW, F32), (ROW, BF16), (ROW, BF16), (ROW, BF16), ((WIN, D), BF16), ((WIN, D), BF16),
                ((H, WIN, LEN), BF16), ((D, LEN), BF16), ((10,) + square, BF16)]
        made = plain(
            functools.partial(attn_fwd, quarters, 0), [SMEM] + [VMEM] * 5 + [ANY] * (2 * quarters), outs,
            [VMEM] + [ANY] * 8,
            [pltpu.VMEM(outs[i][0], BF16) for i in (8, 1, 2, 3, 4, 5, 6, 7)]
            + [pltpu.VMEM(ROW, BF16), pltpu.VMEM((256, 4 * WIN), BF16), DMA((10 * quarters,)), DMA((9,))],
            "attn_fwd", 13, idx, h, bias, tap, gains[0], gains[1], *own, *other, deps=deps)
        return gains, tap, made

    def run_feed_fwd(h2, gains, own, other, at, deps):
        outs = [(ROW, BF16), ((LEN, FF), BF16), ((LEN, FF), BF16), ((n, block, FF), BF16), ((n, 4 * block, D), BF16)]
        y, act, slope, up, down = plain(
            functools.partial(feed_fwd, quarters, at), [SMEM] + [VMEM] * 3 + [ANY] * (2 * quarters), outs,
            [VMEM] + [ANY] * 4, [pltpu.VMEM(outs[i][0], BF16) for i in (3, 4, 1, 2)]
            + [pltpu.VMEM(ROW, BF16), DMA((5 * quarters,)), DMA((10,))],
            "feed_fwd", 13, idx, h2, gains[2], gains[3], *own, *other, deps=deps)
        return y, (act, slope, up.reshape(D, FF), down.reshape(FF, D))

    def spread_from(piece, last_after=None):
        pieces = [piece]
        for step in reversed(range(bits)):
            final = step == 0 and last_after is not None
            pieces += [dp_swap(tie(held, last_after) if final and at else held, step, bits)
                       for at, held in enumerate(list(pieces))]
        return pieces

    def between(own, after=()):
        after = list(after) + [None] * (len(own) - len(after))
        return [swap_cores(held if mark is None else tie(held, mark)) for held, mark in zip(own, after)]

    attn_here = shard_gather(idx, pieces[0][0], n)
    attn_own = spread_from(attn_here)
    feed_here = shard_gather(idx, tie(pieces[1][0], attn_here), n, tuple(attn_own[1:3]))
    feed_own = spread_from(feed_here)
    attn_other = between(attn_own)
    next_piece = jnp.concatenate([pieces[0][1], pieces[1][1]])
    next_here = shard_gather(idx, tie(next_piece, feed_here), n, tuple(attn_own[3:] + feed_own[1:3] + attn_other[:3]))
    gains, tap, made = run_attn_fwd(BLK, h, attn_here, attn_own, attn_other, (next_here,))
    h2 = made[0]
    next_own = spread_from(next_here, h2)
    feed_other = between(feed_own, [None] * 3 + [h2] * (quarters - 3))
    y, feed = run_feed_fwd(h2, gains, feed_own, feed_other, 0, ())
    saved.append((h, h2, gains, tap) + tuple(made[1:]) + feed)
    next_other = between(next_own, [h2] * 3 + [y] * (quarters - 3))
    h = y
    gains, tap, made = run_attn_fwd(LEN, h, next_here, next_own, next_other, ())
    result, feed = run_feed_fwd(made[0], gains, next_own, next_other, 5 * block + 16, ())
    saved.append((h, made[0], gains, tap) + tuple(made[1:]) + feed)

    rows_feed, rows_conv, rows_proj = 4 * block + 16, 3 * block, 2 * block + 16

    def halves_of(keep, send):
        recv = swap_cores(send)
        return Sums(keep.reshape((-1,) + keep.shape[2:]), recv.reshape((-1,) + recv.shape[2:]))

    def run_feed_bwd(layer, grad, deps=()):
        h, h2, gains, tap, q, kt, vt, ck, cv, p, ot, w, act, slope, up, down = saved[layer]
        shape = (quarters, n, rows_feed, 128)
        gh2, keep, send = plain(
            feed_bwd, [SMEM] + [VMEM] * 4 + [ANY] * 4, [(ROW, F32), (shape, BF16), (shape, BF16)], [VMEM, ANY, ANY],
            [pltpu.VMEM((D, FF), BF16), pltpu.VMEM((FF, D), BF16), pltpu.VMEM((LEN, FF), BF16),
             pltpu.VMEM((LEN, FF), BF16), pltpu.VMEM((LEN, FF), BF16), pltpu.VMEM(ROW, BF16),
             pltpu.VMEM((n, block, FF), BF16), pltpu.VMEM((n, 4 * block, D), BF16), pltpu.VMEM((n, 16, 128), BF16),
             DMA((4,)), DMA((quarters * 7,))],
            "feed_bwd", 13, idx, grad, h2, gains[2], gains[3], up, down, act, slope, deps=deps)
        return gh2, halves_of(keep, send)

    def run_attn_bwd(layer, gh2, deps=()):
        h, h2, gains, tap, q, kt, vt, ck, cv, p, ot, w, act, slope, up, down = saved[layer]
        shape = (quarters, n, rows_conv, 128)
        gq, gk, gv, keep, send = plain(
            attn_bwd, [SMEM, VMEM, VMEM] + [ANY] * 4 + [VMEM] * 2 + [ANY],
            [(ROW, BF16)] * 3 + [(shape, BF16), (shape, BF16)], [ANY] * 5,
            [pltpu.VMEM((7,) + square, BF16)] + [pltpu.VMEM(ROW, BF16)] * 3 + [pltpu.VMEM((H, WIN, LEN), BF16)]
            + [pltpu.VMEM(ROW, BF16)] * 4 + [pltpu.VMEM((WIN, D), BF16)] * 2
            + [pltpu.VMEM((6,) + square, BF16), pltpu.VMEM((4 * WIN, LEN), BF16), pltpu.VMEM((256, 4 * WIN), BF16), DMA((7,)), DMA((3,)), DMA((quarters * 6,))],
            "attn_bwd", 14, idx, gh2, tap, w, q, kt, vt, ck, cv, p, deps=deps)
        return gq, gk, gv, halves_of(keep, send)

    def run_proj_bwd(layer, gh2, gq, gk, gv, deps=()):
        h, h2, gains, tap, q, kt, vt, ck, cv, p, ot, w, act, slope, up, down = saved[layer]
        shape = (quarters, n, rows_proj, 128)
        grad, keep, send = plain(
            proj_bwd, [SMEM] + [VMEM] * 4 + [ANY] + [VMEM] * 3 + [ANY], [(ROW, BF16), (shape, BF16), (shape, BF16)],
            [VMEM, ANY, ANY],
            [pltpu.VMEM((3,) + square, BF16), pltpu.VMEM((D, LEN), BF16), pltpu.VMEM(ROW, BF16),
             pltpu.VMEM((4,) + square, BF16), pltpu.VMEM((n, 16, 128), BF16), DMA((3,)), DMA((quarters * 6,))],
            "proj_bwd", 7, idx, gh2, h, gains[0], gains[1], w, gq, gk, gv, ot, deps=deps)
        return grad, halves_of(keep, send)

    hops = Hops(idx, n, bits)
    gh2, feed_two = run_feed_bwd(1, cot)
    gq, gk, gv, conv_two = run_attn_bwd(1, gh2)
    hops.last = gq
    feed_two, = hops.run(([feed_two], 0))
    grad, proj_two = run_proj_bwd(1, gh2, gq, gk, gv, deps=(hops.last,))
    hops.last = grad
    feed_two, conv_two = hops.run(([feed_two], 1), ([conv_two], 0))
    gh2, feed_one = run_feed_bwd(0, grad, deps=(hops.last,))
    hops.last = gh2
    conv_two, = hops.run(([conv_two], 1))
    feed_two_sum, = hops.run(([feed_two], "shard"))
    gq, gk, gv, conv_one = run_attn_bwd(0, gh2, deps=(hops.last,))
    hops.last = gq
    mixed, = hops.run(([feed_one, proj_two], 0))
    conv_two_sum, = hops.run(([conv_two], "shard"))
    grad, proj_one = run_proj_bwd(0, gh2, gq, gk, gv, deps=(hops.last, feed_two_sum))
    hops.last = grad
    mixed, conv_one = hops.run(([mixed], 1), ([conv_one], 0))
    proj_one, = hops.run(([proj_one], 0))
    two_all = hops.collect(jnp.concatenate([feed_two_sum, conv_two_sum]), 1)
    mixed_sum, = hops.run(([mixed], "shard"))
    attn_one, = hops.run(([conv_one, proj_one], 1))
    attn_one_sum, = hops.run(([attn_one], "shard"))
    feed_one_all = hops.collect(mixed_sum[:rows_feed], 0)
    proj_two_all = hops.collect(mixed_sum[rows_feed:], 1)
    attn_one_all = hops.collect(attn_one_sum, 0)

    result, grad = row_major(result), row_major(grad)
    other = swap_cores(jnp.where(first, result, grad))
    ours = jnp.where(first, grad, result)
    section_ends = jnp.stack([jnp.where(first, ours, other), jnp.where(first, other, ours)]).reshape(1, 2 * LEN, D)

    def finish(zero, one, rows, units, outs, name):
        plans = tuple((arrays[0].shape[0] // 2, at) for arrays, at in (zero, one))
        return plain(functools.partial(unpack, quarters, rows, plans, units), [SMEM] + [ANY] * (2 * quarters),
                     [(s, F32) for s in outs], [VMEM] * len(outs),
                     [pltpu.VMEM((2, quarters, rows, 128), BF16), DMA((2 * quarters,))], name, 2, idx, *zero[0], *one[0])

    gdown, gup = finish((feed_one_all, 0), (two_all, 0), rows_feed, feed_unpack, [(4 * block, D), (block, FF)],
                        "unpack_feed")
    gkc, gvc = finish((attn_one_all, 0), (two_all, rows_feed), rows_conv, conv_unpack, [(3, block, D)] * 2, "unpack_conv")
    gq, gk, gv, go = finish((attn_one_all, rows_conv), (proj_two_all, 0), rows_proj, proj_unpack, [(block, D)] * 4,
                            "unpack_proj")

    def vectors_of(zero, one, at):
        return jnp.where(first, zero[0][at[0]:at[0] + 2, :block], one[0][at[1]:at[1] + 2, :block]).astype(F32)

    vec_attn = vectors_of(attn_one_all, proj_two_all, (rows_conv + 2 * block, 2 * block))
    vec_feed = vectors_of(feed_one_all, two_all, (4 * block, 4 * block))
    return (section_ends, vec_attn[0:1], vec_attn[1:2], gq[None], gk[None], gv[None], gkc.transpose(1, 0, 2)[None],
            gvc.transpose(1, 0, 2)[None], go[None], vec_feed[0:1], vec_feed[1:2], gup[None], gdown[None])


def solution(mesh):
    vector, matrix, conv = P("section", "shard"), P("section", "shard", None), P("section", "shard", None, None)
    rows, tokens = P("section", ("dp", "shard"), None), P(("dp", "shard"))
    weights = (vector, vector, matrix, matrix, matrix, conv, conv, matrix, vector, vector, matrix, matrix)
    return jax.shard_map(body, mesh=mesh, in_specs=(rows, tokens, tokens) + weights, out_specs=(rows,) + weights,
                         check_vma=False)
```

```python
import functools

import jax
import jax.numpy as jnp
from jax import lax
from jax.experimental import pallas as pl
from jax.experimental.pallas import tpu as pltpu
from jax.sharding import PartitionSpec as P

D = 512
H = 8
HD = 64
FF = 2048
BLK = 256
LEN = 768
WIN = LEN // 3
EPSILON = 1e-05
NEGATIVE = -1e30
F32 = jnp.float32
BF16 = jnp.bfloat16
LOG2E = 1.4426950408889634
VMEM = pl.BlockSpec(memory_space=pltpu.VMEM)
ANY = pl.BlockSpec(memory_space=pl.ANY)
SMEM = pl.BlockSpec(memory_space=pltpu.SMEM)
DMA = pltpu.SemaphoreType.DMA
ROW = (LEN, D)
Q, K, KC, V, O, VC = 0, 1, 2, 5, 6, 7


def nn(a, b):
    return lax.dot_general(a, b, (((1,), (0,)), ((), ())), preferred_element_type=F32)


def nt(a, b):
    return lax.dot_general(a, b, (((1,), (1,)), ((), ())), preferred_element_type=F32)


def tn(a, b):
    return lax.dot_general(a, b, (((0,), (0,)), ((), ())), preferred_element_type=F32)


def norm_parts(hidden):
    centred = hidden - jnp.mean(hidden, axis=-1, keepdims=True)
    spread = jnp.mean(centred * centred, axis=-1, keepdims=True)
    scale = lax.rsqrt(spread + EPSILON)
    return centred * scale, scale


def norm_back(grad, hat, scale, gain):
    inner = grad * gain
    mean_one = jnp.mean(inner, axis=-1, keepdims=True)
    mean_two = jnp.mean(inner * hat, axis=-1, keepdims=True)
    return scale * (inner - mean_one - hat * mean_two)


def gelu_both(z):
    phi = 0.5 + 0.5 * lax.erf(z * 0.7071067811865476)
    density = jnp.exp2(z * z * (-0.5 * LOG2E)) * 0.3989422804014327
    return z * phi, phi + z * density


def head_mask(rows):
    lane = lax.broadcasted_iota(jnp.int32, (rows, 256), 1) // HD
    return [lane == i for i in range(4)]


def relative(index, core, bits):
    return sum(((index >> k) & 1) << (bits - 1 - k) for k in range(bits)) if core == 0 else index


def to_taps(rows, staged_ref):
    for c in range(D // 128):
        staged_ref[c] = rows[:, c * 128:c * 128 + 128].astype(F32)
    return [jnp.concatenate([staged_ref[c, pl.ds(t, WIN, stride=3), :] for c in range(D // 128)], axis=1)
            for t in range(3)]


def to_rows(value, staged_ref):
    for c in range(D // 128):
        for t in range(3):
            staged_ref[c, pl.ds(t, WIN, stride=3), :] = value[t * WIN:(t + 1) * WIN, c * 128:c * 128 + 128]
    return jnp.concatenate([staged_ref[c] for c in range(D // 128)], axis=1)


class Moves:
    def __init__(self, sems):
        self.sems, self.items = sems, []

    def start(self, src, dst):
        copy = pltpu.make_async_copy(src, dst, self.sems.at[len(self.items)])
        copy.start()
        self.items.append(copy)
        return copy

    def wait(self):
        for copy in self.items:
            copy.wait()


def fetch_pieces(idx_ref, own, other, units, sems):
    core, replica = idx_ref[1], idx_ref[0]
    ordered = len(own) == 1
    quarters = own[0].shape[0] if ordered else len(own)
    bits = quarters.bit_length() - 1
    for here in range(2):
        made = []
        for half in range(2):
            side = own if half == here else other
            for m in range(quarters):
                piece = side[0].at[m] if ordered else side[m]
                made += units(half, piece, m if ordered else replica ^ relative(m, half, bits))

        @pl.when(core == here)
        def _():
            for i, (src, dst) in enumerate(made):
                pltpu.make_async_copy(src, dst, sems.at[i]).start()
    return [pltpu.make_async_copy(src, dst, sems.at[i]) for i, (src, dst) in enumerate(made)]


def send_halves(idx_ref, halves, keep_ref, send_ref, sems, base=0):
    core = idx_ref[1]
    for here in range(2):
        @pl.when(core == here)
        def _():
            i = base
            for half in range(2):
                for src, dst in halves[half]:
                    out = keep_ref if here == half else send_ref
                    pltpu.make_async_copy(src, out.at[dst], sems.at[i]).start()
                    i += 1
    items = halves[0] + halves[1]
    return [pltpu.make_async_copy(src, keep_ref.at[dst], sems.at[base + i]) for i, (src, dst) in enumerate(items)]


def fill_vectors(vec_ref, rows):
    vec_ref[...] = jnp.zeros_like(vec_ref)
    parts, block = vec_ref.shape[0], D // vec_ref.shape[0]
    for z in range(parts):
        for i, row in enumerate(rows):
            vec_ref[z, i:i + 1, :block] = row[:, z * block:(z + 1) * block].astype(BF16)


def wait_all(copies):
    for copy in copies:
        copy.wait()


def attn_fwd(count, in_rows, idx_ref, h_in, bias_ref, tap_ref, gain_ref, shift_ref, *refs):
    own, other = refs[:count], refs[count:2 * count]
    (h2_ref, h_ref, q_out, kt_out, vt_out, ck_out, cv_out, p_out, ot_out, w_out,
     w_ref, q_ref, kt_ref, vt_ref, ck_ref, cv_ref, p_ref, ot_ref, n_ref, across_ref, staged_ref, in_sems, out_sems) = refs[2 * count:]
    block = w_ref.shape[2]

    def units(half, piece, quarter):
        cols = pl.ds(pl.multiple_of(quarter * 128, 128), 128)
        return [(piece.at[:, pl.ds(u * block, block), :], w_ref.at[half * 5 + u, :, :, cols]) for u in range(5)]

    fetched = fetch_pieces(idx_ref, own, other, units, in_sems)
    out = Moves(out_sems)

    def weight(u):
        return w_ref[u].reshape(D, D)

    for t, rows in enumerate(to_taps(h_in[...], staged_ref) if in_rows else []):
        h_ref[t * WIN:(t + 1) * WIN, :] = rows.astype(BF16)
    if not in_rows:
        h_ref[...] = h_in[...]
    hat, _s = norm_parts(h_ref[...].astype(F32))
    n_ref[...] = (hat * gain_ref[...].astype(F32) + shift_ref[...].astype(F32)).astype(BF16)
    wait_all(fetched)
    out.start(w_ref, w_out)
    tap = tap_ref[...]
    kt_ref[...] = (nn(n_ref[...], weight(K)) * tap).astype(BF16)
    vt_ref[...] = (nn(n_ref[...], weight(V)) * tap).astype(BF16)
    q_ref[...] = nn(n_ref[...], weight(Q)).astype(BF16)
    out.start(q_ref, q_out)
    out.start(kt_ref, kt_out)
    out.start(vt_ref, vt_out)
    ck_ref[...] = sum(nn(kt_ref[t * WIN:(t + 1) * WIN, :], weight(KC + t)) for t in range(3)).astype(BF16)
    cv_ref[...] = sum(nn(vt_ref[t * WIN:(t + 1) * WIN, :], weight(VC + t)) for t in range(3)).astype(BF16)
    out.start(ck_ref, ck_out)
    out.start(cv_ref, cv_out)
    masks = head_mask(WIN)
    zero = jnp.zeros((WIN, 256), BF16)
    for g in range(2):
        cols = slice(g * 256, g * 256 + 256)
        for i in range(4):
            across_ref[:, i * WIN:i * WIN + WIN] = jnp.where(masks[i], cv_ref[:, cols], zero).T
        for i in range(4):
            s = nt(jnp.where(masks[i], ck_ref[:, cols], zero), q_ref[:, cols]) * (0.125 * LOG2E) + bias_ref[...]
            top = jnp.maximum(jnp.max(s, axis=0, keepdims=True), 0.0)
            num = jnp.exp2(s - top)
            den = jnp.exp2(-top) + jnp.sum(num, axis=0, keepdims=True)
            p_ref[g * 4 + i] = (num * (1.0 / den)).astype(BF16)
        heads = pl.ds(g * 4, 4)
        out.start(p_ref.at[heads], p_out.at[heads])
        ot_ref[cols, :] = nn(across_ref[...], p_ref[heads].reshape(4 * WIN, LEN)).astype(BF16)
    out.start(ot_ref, ot_out)
    h2_ref[...] = h_ref[...].astype(F32) + tn(ot_ref[...], weight(O))
    out.wait()


def feed_fwd(count, at, out_rows, idx_ref, h2_ref, gain_ref, shift_ref, *refs):
    own, other = refs[:count], refs[count:2 * count]
    (y_ref, a_out, gd_out, wu_out, wd_out, wu_ref, wd_ref, a_ref, gd_ref, n_ref, staged_ref, in_sems, out_sems) = refs[2 * count:]
    block = wu_ref.shape[1]

    def units(half, piece, quarter):
        if half == 0:
            return [(piece.at[:, pl.ds(at, 4 * block), :], wd_ref.at[:, :, pl.ds(pl.multiple_of(quarter * 128, 128), 128)])]
        return [(piece.at[:, pl.ds(at + i * block, block), :],
                 wu_ref.at[:, :, pl.ds(pl.multiple_of(quarter * 512 + i * 128, 128), 128)]) for i in range(4)]

    fetched = fetch_pieces(idx_ref, own, other, units, in_sems)
    hat, _s = norm_parts(h2_ref[...])
    n_ref[...] = (hat * gain_ref[...].astype(F32) + shift_ref[...].astype(F32)).astype(BF16)
    wait_all(fetched)
    out = Moves(out_sems)
    out.start(wu_ref, wu_out)
    out.start(wd_ref, wd_out)
    chunks = [slice(c * 512, c * 512 + 512) for c in range(4)]

    def up(c):
        return nn(n_ref[...], wu_ref[:, :, chunks[c]].reshape(D, 512))

    total = h2_ref[...]
    z = up(0)
    for c in range(4):
        later = up(c + 1) if c < 3 else None
        act, slope = gelu_both(z)
        act = act.astype(BF16)
        a_ref[:, chunks[c]] = act
        gd_ref[:, chunks[c]] = slope.astype(BF16)
        out.start(a_ref.at[:, chunks[c]], a_out.at[:, chunks[c]])
        out.start(gd_ref.at[:, chunks[c]], gd_out.at[:, chunks[c]])
        total = total + nn(act, wd_ref[...].reshape(FF, D)[chunks[c], :])
        z = later
    y_ref[...] = (to_rows(total, staged_ref) if out_rows else total).astype(BF16)
    out.wait()


def feed_bwd(in_rows, idx_ref, gout_in, h2_ref, gain_ref, shift_ref, wu_in, wd_in, a_in, gd_in,
             gh2_ref, keep_ref, send_ref, wu_ref, wd_ref, a_ref, gd_ref, gz_ref, n_ref, gwu_ref, gwd_ref, vec_ref,
             gout_ref, staged_ref, in_sems, sems):
    arriving = Moves(in_sems)
    for src, dst in ((a_in, a_ref), (wd_in, wd_ref), (gd_in, gd_ref), (wu_in, wu_ref)):
        arriving.start(src, dst)
    for t, rows in enumerate(to_taps(gout_in[...], staged_ref) if in_rows else []):
        gout_ref[t * WIN:(t + 1) * WIN, :] = rows.astype(BF16)
    if not in_rows:
        gout_ref[...] = gout_in[...]
    parts, quarters = gwu_ref.shape[0], keep_ref.shape[0]
    block = D // parts
    bits = quarters.bit_length() - 1
    wide = FF // quarters
    gain = gain_ref[...].astype(F32)
    hat, scale = norm_parts(h2_ref[...])
    n_ref[...] = (hat * gain + shift_ref[...].astype(F32)).astype(BF16)
    arriving.items[0].wait()
    gwd_ref[...] = tn(a_ref[...], gout_ref[...]).astype(BF16).reshape(parts, 4 * block, D)
    slots = [[relative(q ^ idx_ref[0], half, bits) for half in range(2)] for q in range(quarters)]
    down = [(gwd_ref.at[:, :, q * 128:q * 128 + 128], (slots[q][0], slice(None), pl.ds(0, 4 * block)))
            for q in range(quarters)]
    copies = send_halves(idx_ref, (down, []), keep_ref, send_ref, sems)
    wait_all(arriving.items[1:3])
    for c in range(4):
        cols = slice(c * 512, c * 512 + 512)
        gz_ref[:, cols] = (nt(gout_ref[...], wd_ref[cols, :]) * gd_ref[:, cols].astype(F32)).astype(BF16)
    arriving.items[3].wait()
    gwu_ref[...] = tn(n_ref[...], gz_ref[...]).astype(BF16).reshape(parts, block, FF)
    up = [(gwu_ref.at[:, :, q * wide + i * 128:q * wide + i * 128 + 128],
           (slots[q][1], slice(None), pl.ds(i * block, block))) for q in range(quarters) for i in range(wide // 128)]
    copies += send_halves(idx_ref, ([], up), keep_ref, send_ref, sems, len(copies))
    gn = nt(gz_ref[...], wu_ref[...])
    hat, scale = norm_parts(h2_ref[...])
    fill_vectors(vec_ref, [jnp.sum(gn * hat, axis=0, keepdims=True), jnp.sum(gn, axis=0, keepdims=True)])
    vectors = [[(vec_ref, (slots[q][half], slice(None), pl.ds(4 * block, 16))) for q in range(quarters)]
               for half in range(2)]
    copies += send_halves(idx_ref, vectors, keep_ref, send_ref, sems, len(copies))
    gh2_ref[...] = gout_ref[...].astype(F32) + norm_back(gn, hat, scale, gain)
    wait_all(copies)


def attn_bwd(idx_ref, gh2_ref, tap_ref, w_in, q_in, kt_in, vt_in, ck_ref, cv_ref, p_in,
             gq_out, gk_out, gv_out, keep_ref, send_ref,
             w_ref, q_ref, kt_ref, vt_ref, p_ref, go_ref, gq_ref, gk_ref, gv_ref, gck_ref, gcv_ref, gw_ref, gs_ref, across_ref,
             in_sems, out_sems, sems):
    arriving = Moves(in_sems)
    arriving.start(w_in.at[O], w_ref.at[6])
    arriving.start(q_in, q_ref)
    arriving.start(p_in, p_ref)
    arriving.start(w_in.at[pl.ds(KC, 3)], w_ref.at[pl.ds(0, 3)])
    arriving.start(w_in.at[pl.ds(VC, 3)], w_ref.at[pl.ds(3, 3)])
    arriving.start(kt_in, kt_ref)
    arriving.start(vt_in, vt_ref)
    out = Moves(out_sems)
    parts, quarters = gw_ref.shape[1], keep_ref.shape[0]
    block = D // parts
    shaped = (parts, block, D)
    wait_all(arriving.items[:1])
    go_ref[...] = nt(gh2_ref[...].astype(BF16), w_ref[6].reshape(D, D)).astype(BF16)
    masks = head_mask(WIN)
    zero = jnp.zeros((WIN, 256), BF16)
    wait_all(arriving.items[1:3])

    def own_lanes(stacked):
        return sum(jnp.where(masks[i], stacked[i * WIN:(i + 1) * WIN, :], 0.0) for i in range(4))

    for g in range(2):
        cols = slice(g * 256, g * 256 + 256)
        for i in range(4):
            across_ref[:, i * WIN:i * WIN + WIN] = jnp.where(masks[i], ck_ref[:, cols], zero).T
        for i in range(4):
            gp = nt(jnp.where(masks[i], cv_ref[:, cols], zero), go_ref[:, cols])
            p = p_ref[g * 4 + i].astype(F32)
            pg = p * gp
            gs_ref[i * WIN:i * WIN + WIN, :] = (pg - p * jnp.sum(pg, axis=0, keepdims=True)).astype(BF16)
        stacked = p_ref[pl.ds(g * 4, 4)].reshape(4 * WIN, LEN)
        gcv_ref[:, cols] = own_lanes(nn(stacked, go_ref[:, cols])).astype(BF16)
        gck_ref[:, cols] = (own_lanes(nn(gs_ref[...], q_ref[:, cols])) * 0.125).astype(BF16)
        gq_ref[:, cols] = (nn(across_ref[...], gs_ref[...]) * 0.125).astype(BF16).T

    out.start(gq_ref, gq_out)
    gck, gcv = gck_ref[...], gcv_ref[...]
    wait_all(arriving.items[3:])
    for t in range(3):
        rows = slice(t * WIN, t * WIN + WIN)
        gw_ref[t] = tn(kt_ref[rows, :], gck).astype(BF16).reshape(shaped)
        gw_ref[3 + t] = tn(vt_ref[rows, :], gcv).astype(BF16).reshape(shaped)

    halves = [], []
    bits = quarters.bit_length() - 1
    for q in range(quarters):
        for half in range(2):
            slot = relative(q ^ idx_ref[0], half, bits)
            for u in range(3):
                halves[half].append((gw_ref.at[half * 3 + u, :, :, q * 128:q * 128 + 128],
                                     (slot, slice(None), pl.ds(u * block, block))))
    copies = send_halves(idx_ref, halves, keep_ref, send_ref, sems)
    for t in range(3):
        rows = slice(t * WIN, t * WIN + WIN)
        tap = tap_ref[rows, :]
        gk_ref[rows, :] = (nt(gck, w_ref[t].reshape(D, D)) * tap).astype(BF16)
        gv_ref[rows, :] = (nt(gcv, w_ref[3 + t].reshape(D, D)) * tap).astype(BF16)
    out.start(gk_ref, gk_out)
    out.start(gv_ref, gv_out)
    wait_all(copies)
    out.wait()


def proj_bwd(out_rows, idx_ref, gh2_ref, h_ref, gain_ref, shift_ref, w_in, gq_ref, gk_ref, gv_ref, ot_in,
             gh_ref, keep_ref, send_ref, w_ref, ot_ref, n_ref, gw_ref, vec_ref, staged_ref, in_sems, sems):
    arriving = Moves(in_sems)
    arriving.start(w_in.at[pl.ds(Q, 2)], w_ref.at[pl.ds(0, 2)])
    arriving.start(w_in.at[V], w_ref.at[2])
    arriving.start(ot_in, ot_ref)
    gain = gain_ref[...].astype(F32)
    parts, quarters = gw_ref.shape[1], keep_ref.shape[0]
    block = D // parts
    shaped = (parts, block, D)
    bits = quarters.bit_length() - 1
    slots = [[relative(q ^ idx_ref[0], half, bits) for half in range(2)] for q in range(quarters)]
    hat, scale = norm_parts(h_ref[...].astype(F32))
    n_ref[...] = (hat * gain + shift_ref[...].astype(F32)).astype(BF16)
    arriving.wait()
    gn = (nt(gq_ref[...], w_ref[0].reshape(D, D)) + nt(gk_ref[...], w_ref[1].reshape(D, D))
          + nt(gv_ref[...], w_ref[2].reshape(D, D)))
    fill_vectors(vec_ref, [jnp.sum(gn * hat, axis=0, keepdims=True), jnp.sum(gn, axis=0, keepdims=True)])
    vectors = [[(vec_ref, (slots[q][half], slice(None), pl.ds(2 * block, 16))) for q in range(quarters)]
               for half in range(2)]
    copies = send_halves(idx_ref, vectors, keep_ref, send_ref, sems)
    gh = gh2_ref[...] + norm_back(gn, hat, scale, gain)
    gh_ref[...] = (to_rows(gh, staged_ref) if out_rows else gh).astype(BF16)
    gw_ref[3] = nn(ot_ref[...], gh2_ref[...].astype(BF16)).astype(BF16).reshape(shaped)
    across = n_ref[...].T
    for u, grad in enumerate((gq_ref, gk_ref, gv_ref)):
        gw_ref[u] = nn(across, grad[...]).astype(BF16).reshape(shaped)
    weights = [[(gw_ref.at[half * 2 + u, :, :, q * 128:q * 128 + 128], (slots[q][half], slice(None), pl.ds(u * block, block)))
                for q in range(quarters) for u in range(2)] for half in range(2)]
    copies += send_halves(idx_ref, weights, keep_ref, send_ref, sems, len(copies))
    wait_all(copies)


def place_shards(n, idx_ref, *refs):
    pieces, outs, sems = refs[:n], refs[n:-1], refs[-1]
    moves = Moves(sems)
    for k, piece in enumerate(pieces):
        at = 0
        for out in outs:
            rows = out.shape[1]
            moves.start(piece.at[pl.ds(at, rows), :], out.at[lax.rem(idx_ref[2] + n - k, n)])
            at += rows
    moves.wait()


def add_kernel(jobs, idx_ref, *refs):
    outs = refs[sum(2 * groups * chunks for groups, chunks in jobs):]
    at_in = at_out = 0
    for groups, chunks in jobs:
        at = 0
        for _ in range(chunks):
            for g in range(groups):
                keep, recv = refs[at_in], refs[at_in + 1]
                at_in += 2
                rows = keep.shape[1]
                outs[at_out + g][:, at:at + rows, :] = (keep[...].astype(F32) + recv[...].astype(F32)).astype(BF16)
            at += rows
        at_out += groups


def add_parts(idx, jobs, deps=()):
    sizes = [chunks[0][0].shape[0] // groups for chunks, groups, _ in jobs]
    steps = min(min(sizes), 4)
    in_specs, out_specs, shapes, args, plan = [], [], [], [], []
    for (chunks, groups, index), each in zip(jobs, sizes):
        lead = each // steps
        total = sum(keep.shape[1] for keep, _ in chunks)
        plan.append((groups, len(chunks)))
        for keep, recv in chunks:
            for g in range(groups):
                if index:
                    where = functools.partial(lambda g, i, s: (index(g, i, s), 0, 0), g)
                else:
                    where = functools.partial(lambda g, i, s: (i + g * steps, 0, 0), g)
                in_specs += [pl.BlockSpec((lead, keep.shape[1], 128), where)] * 2
                args += [keep, recv]
        out_specs += [pl.BlockSpec((lead, total, 128), lambda i, s: (i, 0, 0))] * groups
        shapes += [jax.ShapeDtypeStruct((each, total, 128), BF16)] * groups
    count = len(args)

    def with_deps(idx_ref, *refs):
        add_kernel(plan, idx_ref, *refs[:count], *refs[count + len(deps):])

    made = pl.pallas_call(
        with_deps,
        grid_spec=pltpu.PrefetchScalarGridSpec(
            num_scalar_prefetch=1, grid=(steps,), in_specs=in_specs + [ANY] * len(deps), out_specs=out_specs),
        out_shape=shapes,
        compiler_params=pltpu.CompilerParams(vmem_limit_bytes=16 * 2**20),
        cost_estimate=pl.CostEstimate(flops=int(0.5*1.1e9), bytes_accessed=1024, transcendentals=0),
        name="add_parts",
    )(idx, *args, *deps)
    split, at = [], 0
    for groups, _ in plan:
        split.append(made[at:at + groups])
        at += groups
    return split


def unpack(quarters, starts, idx_ref, *refs):
    outs, held, sems = refs[2 * quarters:-2], refs[-2], refs[-1]
    core, replica = idx_ref[1], idx_ref[0]
    rows = held.shape[2]
    for here in range(2):
        @pl.when(core == here)
        def _():
            for k in range(quarters):
                for half in range(2):
                    source = refs[(1 - here) * quarters + k].at[pl.ds(0 if half == here else rows, rows), :]
                    pltpu.make_async_copy(source, held.at[half, replica ^ k], sems.at[half * quarters + k]).start()
    for k in range(quarters):
        for half in range(2):
            pltpu.make_async_copy(refs[k].at[pl.ds(0, rows), :], held.at[half, k], sems.at[half * quarters + k]).wait()
    down, up, key_conv, value_conv = outs[:4]
    block = up.shape[0]
    feed, conv, proj = starts
    for q in range(quarters):
        cols = slice(q * 128, q * 128 + 128)
        down[:, cols] = held[0, q, feed:feed + 4 * block, :].astype(F32)
        for i in range(4):
            at = q * 512 + i * 128
            up[:, at:at + 128] = held[1, q, feed + i * block:feed + (i + 1) * block, :].astype(F32)
        for t in range(3):
            key_conv[t, :, cols] = held[0, q, conv + t * block:conv + (t + 1) * block, :].astype(F32)
            value_conv[t, :, cols] = held[1, q, conv + t * block:conv + (t + 1) * block, :].astype(F32)
        for u in range(4):
            at = proj + u % 2 * block
            outs[4 + u][:, cols] = held[u // 2, q, at:at + block, :].astype(F32)


def plain(kernel, in_specs, outs, out_specs, scratch, name, us, *args, deps=(), mib=16):
    count = len(args)

    def with_deps(*refs):
        kernel(*refs[:count], *refs[count + len(deps):])

    return pl.pallas_call(
        with_deps,
        out_shape=[jax.ShapeDtypeStruct(s, d) for s, d in outs],
        in_specs=list(in_specs) + [ANY] * len(deps),
        out_specs=out_specs,
        scratch_shapes=scratch,
        compiler_params=pltpu.CompilerParams(vmem_limit_bytes=mib * 2**20),
        cost_estimate=pl.CostEstimate(flops=int(us * 1 * 1.1e9), bytes_accessed=1024, transcendentals=0),
        name=name,
    )(*args, *deps)


def geometry(segments, validity, block_len):
    seg = segments.reshape(WIN, 3)
    val = validity.reshape(WIN, 3)
    anchor_seg = seg[:, 2]
    tap = ((seg == anchor_seg[:, None]) & (val == 1)).astype(F32).T.reshape(LEN, 1)
    seg_t = seg.T.reshape(LEN)
    window = jnp.arange(WIN, dtype=jnp.int32)
    position = (window[None, :] * 3 + jnp.arange(3, dtype=jnp.int32)[:, None]).reshape(LEN)
    anchor = window * 3 + 2
    allowed = (anchor[:, None] <= position[None, :]) & (anchor_seg[:, None] == seg_t[None, :])
    allowed = allowed & (val[:, 2][:, None] == 1) & (anchor[:, None] // block_len == position[None, :] // block_len)
    return tap, jnp.where(allowed, 0.0, NEGATIVE).astype(F32)


def tie(value, *others):
    return lax.optimization_barrier((value,) + others)[0]


def swap_cores(value):
    return lax.ppermute(value, "section", [(0, 1), (1, 0)])


def dp_swap(value, step, bits):
    route = []
    for replica in range(2**bits):
        for core in range(2):
            bit = step if core == 0 else bits - 1 - step
            route.append((replica * 2 + core, (replica ^ (1 << bit)) * 2 + core))
    return lax.ppermute(value, ("dp", "section"), route)


def shard_gather(idx, piece, n, deps=(), parts=None):
    parts = parts or [piece.shape[0]]
    if n > 8:
        whole = lax.all_gather(piece, "shard", axis=0)
        return [whole[:, sum(parts[:i]):sum(parts[:i + 1])] for i in range(len(parts))]
    pieces = [piece] + [lax.ppermute(piece, "shard", [(i, (i + k) % n) for i in range(n)]) for k in range(1, n)]
    return plain(functools.partial(place_shards, n), [SMEM] + [ANY] * n, [((n, rows, 128), BF16) for rows in parts],
                 [VMEM] * len(parts), [DMA((n * len(parts),))], "place_shards", 1, idx, *pieces, deps=deps)


def shard_step(value, step, n):
    return lax.ppermute(value, "shard", [(i, i ^ (1 << step)) for i in range(n)])


def shard_order(bits):
    def index(g, i, idx_ref):
        place = i + g * (1 << (bits - 1))
        return sum(((place >> k) & 1) << (bits - 1 - k) for k in range(bits)) ^ idx_ref[2]
    return index


class Sums:
    def __init__(self, keep, recv):
        self.keep, self.recv = keep, recv


class Hops:
    def __init__(self, idx, n, bits):
        self.idx, self.n, self.bits, self.last = idx, n, bits, None

    def run(self, *jobs, beside=(), deps=()):
        n = self.n
        direct = n <= 8
        listed = []
        for chunks, what in jobs:
            pairs = [(c.keep, c.recv) for c in chunks]
            if what == "all":
                listed.append((pairs, 1, None))
            elif what == "shard" and direct:
                listed.append((pairs, n, lambda g, i, s: lax.rem(s[2] + g, n)))
            elif what == "shard":
                listed.append((pairs, 2, shard_order(n.bit_length() - 1)))
            else:
                listed.append((pairs, 2, None))
        made = add_parts(self.idx, listed, tuple(deps) + (() if self.last is None else (self.last,)))
        self.last = made[0][0]
        results = []
        for (chunks, what), parts in zip(jobs, made):
            if what == "all":
                whole = parts[0].reshape((2**self.bits, n) + parts[0].shape[1:])
                results.append(lax.psum_scatter(lax.psum_scatter(whole, "dp", scatter_dimension=0), "shard",
                                                scatter_dimension=0))
            elif what == "shard" and direct:
                got = [lax.ppermute(parts[k], "shard", [(i, (i + k) % n) for i in range(n)]) for k in range(1, n)]
                got = [tie(g, *beside) for g in got] if beside else got
                results.append(sum([parts[0].astype(F32)] + [g.astype(F32) for g in got])[0].astype(BF16))
            elif what == "shard":
                keep, recv = parts[0], shard_step(parts[1], 0, n)
                for step in range(1, n.bit_length() - 1):
                    (keep, send), = add_parts(self.idx, [([(keep, recv)], 2, None)])
                    recv = shard_step(send, step, n)
                results.append((keep[0].astype(F32) + recv[0].astype(F32)).astype(BF16))
            else:
                results.append(Sums(parts[0], dp_swap(parts[1], what, self.bits)))
        return results

    def collect(self, total, owner):
        total = tie(total, self.last)
        both = jnp.concatenate([total, lax.ppermute(total, "section", [(1 - owner, owner)])])
        quarters = 2**self.bits
        return [both] + [lax.ppermute(both, ("dp", "section"),
                                      [(2 * i + owner, 2 * (i ^ k) + owner) for i in range(quarters)])
                         for k in range(1, quarters)]


def body(boundary, segment_ids, token_valid, attention_gain, attention_bias, query_weight, key_weight, value_weight,
         key_conv, value_conv, out_weight, feed_gain, feed_bias, up_weight, down_weight):
    core = lax.axis_index("section")
    replica = lax.axis_index("dp")
    first = core == 0
    quarters = lax.axis_size("dp")
    bits = quarters.bit_length() - 1
    n = lax.axis_size("shard")
    block = D // n
    idx = jnp.stack([replica, core, lax.axis_index("shard")]).astype(jnp.int32)

    def quarter(weight, width=128):
        return lax.dynamic_slice_in_dim(weight, replica * width, width, weight.ndim - 1)

    vectors = jnp.stack([attention_gain[0], attention_bias[0], feed_gain[0], feed_bias[0]])
    vectors = jnp.pad(vectors, ((0, 12), (0, 128 - block)))
    key_taps = quarter(key_conv[0]).transpose(1, 0, 2).reshape(3 * block, 128)
    value_taps = quarter(value_conv[0]).transpose(1, 0, 2).reshape(3 * block, 128)
    attn_halves = (jnp.concatenate([quarter(query_weight[0]), quarter(key_weight[0]), key_taps, vectors]),
                   jnp.concatenate([quarter(value_weight[0]), quarter(out_weight[0]), value_taps, vectors]))
    up_part = quarter(up_weight[0], 512).reshape(block, 4, 128).transpose(1, 0, 2).reshape(4 * block, 128)
    feed_halves = (quarter(down_weight[0]), up_part)
    pieces = []
    for halves in (attn_halves, feed_halves):
        kept = jnp.where(first, halves[0], halves[1])
        got = swap_cores(jnp.where(first, halves[1], halves[0]))
        pieces.append((jnp.where(first, kept, got), jnp.where(first, got, kept)))

    own_rows = boundary[0].reshape(2, LEN, D)
    mine = lax.dynamic_index_in_dim(own_rows, core, 0, keepdims=False)
    theirs = swap_cores(lax.dynamic_index_in_dim(own_rows, 1 - core, 0, keepdims=False))
    h = jnp.where(first, mine, theirs)
    cot = jnp.where(first, theirs, mine)
    segments = lax.dynamic_index_in_dim(segment_ids.reshape(2, LEN), core, 0, keepdims=False)
    validity = lax.dynamic_index_in_dim(token_valid.reshape(2, LEN), core, 0, keepdims=False)

    square = (n, block, D)
    saved = []

    def run_attn_fwd(length, h, here, own, other, deps):
        gains = here[:, 5 * block:5 * block + 4, :block].transpose(1, 0, 2).reshape(4, 1, D)
        tap, bias = geometry(segments, validity, length)
        outs = [(ROW, F32), (ROW, BF16), (ROW, BF16), (ROW, BF16), (ROW, BF16), ((WIN, D), BF16), ((WIN, D), BF16),
                ((H, WIN, LEN), BF16), ((D, LEN), BF16), ((10,) + square, BF16)]
        made = plain(
            functools.partial(attn_fwd, len(own), length == BLK), [SMEM] + [VMEM] * 5 + [ANY] * (2 * len(own)), outs,
            [VMEM] * 2 + [ANY] * 8,
            [pltpu.VMEM(outs[i][0], BF16) for i in (9, 2, 3, 4, 5, 6, 7, 8)]
            + [pltpu.VMEM(ROW, BF16), pltpu.VMEM((256, 4 * WIN), BF16), pltpu.VMEM((D // 128, LEN, 128), F32), DMA((10 * quarters,)), DMA((9,))],
            "attn_fwd", 13, idx, h, bias, tap, gains[0], gains[1], *own, *other, deps=deps, mib=56)
        return gains, tap, made

    def run_feed_fwd(h2, gains, own, other, at, deps):
        outs = [(ROW, BF16), ((LEN, FF), BF16), ((LEN, FF), BF16), ((n, block, FF), BF16), ((n, 4 * block, D), BF16)]
        y, act, slope, up, down = plain(
            functools.partial(feed_fwd, len(own), at, at > 0), [SMEM] + [VMEM] * 3 + [ANY] * (2 * len(own)), outs,
            [VMEM] + [ANY] * 4, [pltpu.VMEM(outs[i][0], BF16) for i in (3, 4, 1, 2)]
            + [pltpu.VMEM(ROW, BF16), pltpu.VMEM((D // 128, LEN, 128), F32), DMA((5 * quarters,)), DMA((10,))],
            "feed_fwd", 13, idx, h2, gains[2], gains[3], *own, *other, deps=deps, mib=56)
        return y, (act, slope, up.reshape(D, FF), down.reshape(FF, D))

    def spread(piece, last_after=None):
        pieces = [piece]
        for step in reversed(range(bits)):
            final = step == 0 and last_after is not None
            pieces += [dp_swap(tie(held, last_after) if final and at else held, step, bits)
                       for at, held in enumerate(list(pieces))]
        return pieces

    def between(own, after):
        return [swap_cores(held if mark is None else tie(held, mark)) for held, mark in zip(own, after)]

    attn_here, = shard_gather(idx, pieces[0][0], n)
    attn_own = spread(attn_here)
    feed_here, = shard_gather(idx, tie(pieces[1][0], attn_here), n, tuple(attn_own[1:3]))
    feed_own = spread(feed_here)
    attn_other = [swap_cores(held) for held in attn_own]
    next_piece = jnp.concatenate([pieces[0][1], pieces[1][1]])
    next_here, = shard_gather(idx, tie(next_piece, feed_here), n, tuple(attn_own[3:] + feed_own[1:3] + attn_other[:3]))
    gains, tap, made = run_attn_fwd(BLK, h, attn_here, attn_own, attn_other, (next_here,))
    h2 = made[0]
    next_own = spread(next_here, h2)
    feed_other = between(feed_own, [None] * 3 + [h2] * (quarters - 3))
    y, feed = run_feed_fwd(h2, gains, feed_own, feed_other, 0, ())
    saved.append((made[1], h2, gains, tap) + tuple(made[2:]) + feed)
    next_other = between(next_own, [h2] * 3 + [y] * (quarters - 3))
    gains, tap, made = run_attn_fwd(LEN, y, next_here, next_own, next_other, ())
    result, feed = run_feed_fwd(made[0], gains, next_own, next_other, 5 * block + 16, ())
    saved.append((made[1], made[0], gains, tap) + tuple(made[2:]) + feed)

    rows_feed, rows_conv, rows_proj = 4 * block + 16, 3 * block, 2 * block + 16

    def halves_of(keep, send):
        recv = swap_cores(send)
        return Sums(keep.reshape((-1,) + keep.shape[2:]), recv.reshape((-1,) + recv.shape[2:]))

    def run_feed_bwd(layer, grad, deps=()):
        h, h2, gains, tap, q, kt, vt, ck, cv, p, ot, w, act, slope, up, down = saved[layer]
        shape = (quarters, n, rows_feed, 128)
        gh2, keep, send = plain(
            functools.partial(feed_bwd, layer == 1), [SMEM] + [VMEM] * 4 + [ANY] * 4, [(ROW, F32), (shape, BF16), (shape, BF16)], [VMEM, ANY, ANY],
            [pltpu.VMEM((D, FF), BF16), pltpu.VMEM((FF, D), BF16), pltpu.VMEM((LEN, FF), BF16),
             pltpu.VMEM((LEN, FF), BF16), pltpu.VMEM((LEN, FF), BF16), pltpu.VMEM(ROW, BF16),
             pltpu.VMEM((n, block, FF), BF16), pltpu.VMEM((n, 4 * block, D), BF16), pltpu.VMEM((n, 16, 128), BF16),
             pltpu.VMEM(ROW, BF16), pltpu.VMEM((D // 128, LEN, 128), F32), DMA((4,)), DMA((quarters * 7,))],
            "feed_bwd", 13, idx, grad, h2, gains[2], gains[3], up, down, act, slope, deps=deps, mib=56)
        return gh2, halves_of(keep, send)

    def run_attn_bwd(layer, gh2, deps=()):
        h, h2, gains, tap, q, kt, vt, ck, cv, p, ot, w, act, slope, up, down = saved[layer]
        shape = (quarters, n, rows_conv, 128)
        gq, gk, gv, keep, send = plain(
            attn_bwd, [SMEM, VMEM, VMEM] + [ANY] * 4 + [VMEM] * 2 + [ANY],
            [(ROW, BF16)] * 3 + [(shape, BF16), (shape, BF16)], [ANY] * 5,
            [pltpu.VMEM((7,) + square, BF16)] + [pltpu.VMEM(ROW, BF16)] * 3 + [pltpu.VMEM((H, WIN, LEN), BF16)]
            + [pltpu.VMEM(ROW, BF16)] * 4 + [pltpu.VMEM((WIN, D), BF16)] * 2
            + [pltpu.VMEM((6,) + square, BF16), pltpu.VMEM((4 * WIN, LEN), BF16), pltpu.VMEM((256, 4 * WIN), BF16), DMA((7,)), DMA((3,)), DMA((quarters * 6,))],
            "attn_bwd", 14, idx, gh2, tap, w, q, kt, vt, ck, cv, p, deps=deps, mib=50)
        return gq, gk, gv, halves_of(keep, send)

    def run_proj_bwd(layer, gh2, gq, gk, gv, deps=()):
        h, h2, gains, tap, q, kt, vt, ck, cv, p, ot, w, act, slope, up, down = saved[layer]
        shape = (quarters, n, rows_proj, 128)
        grad, keep, send = plain(
            functools.partial(proj_bwd, layer == 0), [SMEM] + [VMEM] * 4 + [ANY] + [VMEM] * 3 + [ANY], [(ROW, BF16), (shape, BF16), (shape, BF16)],
            [VMEM, ANY, ANY],
            [pltpu.VMEM((3,) + square, BF16), pltpu.VMEM((D, LEN), BF16), pltpu.VMEM(ROW, BF16),
             pltpu.VMEM((4,) + square, BF16), pltpu.VMEM((n, 16, 128), BF16), pltpu.VMEM((D // 128, LEN, 128), F32), DMA((3,)), DMA((quarters * 6,))],
            "proj_bwd", 7, idx, gh2, h, gains[0], gains[1], w, gq, gk, gv, ot, deps=deps, mib=20)
        return grad, halves_of(keep, send)

    hops = Hops(idx, n, bits)
    gh2, feed_two = run_feed_bwd(1, cot)
    gq, gk, gv, conv_two = run_attn_bwd(1, gh2)
    hops.last = gq
    feed_two, = hops.run(([feed_two], 0))
    grad, proj_two = run_proj_bwd(1, gh2, gq, gk, gv, deps=(hops.last,))
    hops.last = grad
    conv_two, = hops.run(([conv_two], 0))
    gh2, feed_one = run_feed_bwd(0, grad, deps=(hops.last,))
    hops.last = gh2
    feed_two, proj_two = hops.run(([feed_two], 1), ([proj_two], 0))
    gq, gk, gv, conv_one = run_attn_bwd(0, gh2, deps=(hops.last,))
    hops.last = gq
    attn_two, feed_one = hops.run(([conv_two, proj_two], 1), ([feed_one], 0))
    grad, proj_one = run_proj_bwd(0, gh2, gq, gk, gv, deps=(hops.last,))
    hops.last = grad
    conv_one, = hops.run(([conv_one], 0))
    feed_one, = hops.run(([feed_one], 1))
    proj_one, = hops.run(([proj_one], 0))
    two, = hops.run(([feed_two, attn_two], "shard"))
    feed_one, = hops.run(([feed_one], "shard"))
    attn_one, = hops.run(([conv_one, proj_one], 1), deps=(two,))
    mark = hops.last
    two_all = hops.collect(two, 1)
    attn_one, = hops.run(([attn_one], "shard"), deps=(feed_one, two_all[0]), beside=two_all[1:])
    one_all = hops.collect(jnp.concatenate([feed_one, attn_one]), 0)

    result, grad = tie(result, mark), tie(grad, mark)
    other = swap_cores(jnp.where(first, result, grad))
    ours = jnp.where(first, grad, result)
    section_ends = jnp.stack([jnp.where(first, ours, other), jnp.where(first, other, ours)]).reshape(1, 2 * LEN, D)
    total = rows_feed + rows_conv + rows_proj
    shapes = [(4 * block, D), (block, FF), (3, block, D), (3, block, D)] + [(block, D)] * 4
    gdown, gup, gkc, gvc, gq, gk, gv, go = plain(
        functools.partial(unpack, quarters, (0, rows_feed, rows_feed + rows_conv)), [SMEM] + [ANY] * (2 * quarters),
        [(shape, F32) for shape in shapes], [VMEM] * 8,
        [pltpu.VMEM((2, quarters, total, 128), BF16), DMA((2 * quarters,))], "unpack", 4,
        idx, *two_all, *one_all, mib=20)

    def vectors_of(one, two):
        return jnp.where(first, one[:2, :block], two[:2, :block]).astype(F32)

    vec_feed = vectors_of(one_all[0][4 * block:], two_all[0][4 * block:])
    vec_attn = vectors_of(one_all[0][rows_feed + rows_conv + 2 * block:], two_all[0][rows_feed + rows_conv + 2 * block:])
    return (section_ends, vec_attn[0:1], vec_attn[1:2], gq[None], gk[None], gv[None], gkc.transpose(1, 0, 2)[None],
            gvc.transpose(1, 0, 2)[None], go[None], vec_feed[0:1], vec_feed[1:2], gup[None], gdown[None])


def solution(mesh):
    vector, matrix, conv = P("section", "shard"), P("section", "shard", None), P("section", "shard", None, None)
    rows, tokens = P("section", ("dp", "shard"), None), P(("dp", "shard"))
    weights = (vector, vector, matrix, matrix, matrix, conv, conv, matrix, vector, vector, matrix, matrix)
    return jax.shard_map(body, mesh=mesh, in_specs=(rows, tokens, tokens) + weights, out_specs=(rows,) + weights,
                         check_vma=False)
```

```python
import functools

import jax
import jax.numpy as jnp
from jax import lax
from jax.experimental import pallas as pl
from jax.experimental.pallas import tpu as pltpu
from jax.sharding import PartitionSpec as P

D = 512
H = 8
HD = 64
FF = 2048
BLK = 256
LEN = 768
WIN = LEN // 3
EPSILON = 1e-05
NEGATIVE = -1e30
F32 = jnp.float32
BF16 = jnp.bfloat16
LOG2E = 1.4426950408889634
VMEM = pl.BlockSpec(memory_space=pltpu.VMEM)
ANY = pl.BlockSpec(memory_space=pl.ANY)
SMEM = pl.BlockSpec(memory_space=pltpu.SMEM)
DMA = pltpu.SemaphoreType.DMA
ROW = (LEN, D)
Q, K, V, O, KC, VC = 0, 1, 2, 3, 4, 7
HALVES = (Q, K, KC, KC + 1, KC + 2), (V, O, VC, VC + 1, VC + 2)


def nn(a, b):
    return lax.dot_general(a, b, (((1,), (0,)), ((), ())), preferred_element_type=F32)


def nt(a, b):
    return lax.dot_general(a, b, (((1,), (1,)), ((), ())), preferred_element_type=F32)


def tn(a, b):
    return lax.dot_general(a, b, (((0,), (0,)), ((), ())), preferred_element_type=F32)


def norm_parts(hidden):
    centred = hidden - jnp.mean(hidden, axis=-1, keepdims=True)
    spread = jnp.mean(centred * centred, axis=-1, keepdims=True)
    scale = lax.rsqrt(spread + EPSILON)
    return centred * scale, scale


def norm_back(grad, hat, scale, gain):
    inner = grad * gain
    mean_one = jnp.mean(inner, axis=-1, keepdims=True)
    mean_two = jnp.mean(inner * hat, axis=-1, keepdims=True)
    return scale * (inner - mean_one - hat * mean_two)


def gelu_both(z):
    phi = 0.5 + 0.5 * lax.erf(z * 0.7071067811865476)
    density = jnp.exp2(z * z * (-0.5 * LOG2E)) * 0.3989422804014327
    return z * phi, phi + z * density


def head_mask(rows):
    lane = lax.broadcasted_iota(jnp.int32, (rows, 256), 1) // HD
    return [lane == i for i in range(4)]


def relative(index, core, bits):
    return sum(((index >> k) & 1) << (bits - 1 - k) for k in range(bits)) if core == 0 else index


def to_taps(rows, staged_ref):
    for c in range(D // 128):
        staged_ref[c] = rows[:, c * 128:c * 128 + 128].astype(F32)
    return [jnp.concatenate([staged_ref[c, pl.ds(t, WIN, stride=3), :] for c in range(D // 128)], axis=1)
            for t in range(3)]


def to_rows(value, staged_ref):
    for c in range(D // 128):
        for t in range(3):
            staged_ref[c, pl.ds(t, WIN, stride=3), :] = value[t * WIN:(t + 1) * WIN, c * 128:c * 128 + 128]
    return jnp.concatenate([staged_ref[c] for c in range(D // 128)], axis=1)


class Moves:
    def __init__(self, sems):
        self.sems, self.items = sems, []

    def start(self, src, dst):
        copy = pltpu.make_async_copy(src, dst, self.sems.at[len(self.items)])
        copy.start()
        self.items.append(copy)
        return copy

    def wait(self):
        for copy in self.items:
            copy.wait()


def fetch_pieces(idx_ref, own, other, units, sems):
    core, replica = idx_ref[1], idx_ref[0]
    ordered = len(own) == 1
    quarters = own[0].shape[0] if ordered else len(own)
    bits = quarters.bit_length() - 1
    for here in range(2):
        made = []
        for half in range(2):
            side = own if half == here else other
            for m in range(quarters):
                piece = side[0].at[m] if ordered else side[m]
                made += units(half, piece, m if ordered else replica ^ relative(m, half, bits))

        @pl.when(core == here)
        def _():
            for i, (src, dst) in enumerate(made):
                pltpu.make_async_copy(src, dst, sems.at[i]).start()
    return [pltpu.make_async_copy(src, dst, sems.at[i]) for i, (src, dst) in enumerate(made)]


def send_halves(idx_ref, halves, keep_ref, send_ref, sems, base=0):
    core = idx_ref[1]
    for here in range(2):
        @pl.when(core == here)
        def _():
            i = base
            for half in range(2):
                for src, dst in halves[half]:
                    out = keep_ref if here == half else send_ref
                    pltpu.make_async_copy(src, out.at[dst], sems.at[i]).start()
                    i += 1
    items = halves[0] + halves[1]
    return [pltpu.make_async_copy(src, keep_ref.at[dst], sems.at[base + i]) for i, (src, dst) in enumerate(items)]


def fill_vectors(vec_ref, rows):
    vec_ref[...] = jnp.zeros_like(vec_ref)
    parts, block = vec_ref.shape[0], D // vec_ref.shape[0]
    for z in range(parts):
        for i, row in enumerate(rows):
            vec_ref[z, i:i + 1, :block] = row[:, z * block:(z + 1) * block].astype(BF16)


def wait_all(copies):
    for copy in copies:
        copy.wait()


def attn_fwd(count, in_rows, idx_ref, h_in, bias_ref, tap_ref, gain_ref, shift_ref, *refs):
    own, other = refs[:count], refs[count:2 * count]
    (h2_ref, h_ref, q_out, kt_out, vt_out, ck_out, cv_out, p_out, ot_out, w_out, proj_out,
     w_ref, q_ref, kt_ref, vt_ref, ck_ref, cv_ref, p_ref, ot_ref, n_ref, across_ref, staged_ref, in_sems, out_sems) = refs[2 * count:]
    block = w_ref.shape[2]

    def units(half, piece, quarter):
        cols = pl.ds(pl.multiple_of(quarter * 128, 128), 128)
        return [(piece.at[:, pl.ds(u * block, block), :], w_ref.at[place, :, :, cols])
                for u, place in enumerate(HALVES[half])]

    fetched = fetch_pieces(idx_ref, own, other, units, in_sems)
    out = Moves(out_sems)

    def weight(u):
        return w_ref[u].reshape(D, D)

    for t, rows in enumerate(to_taps(h_in[...], staged_ref) if in_rows else []):
        h_ref[t * WIN:(t + 1) * WIN, :] = rows.astype(BF16)
    if not in_rows:
        h_ref[...] = h_in[...]
    hat, _s = norm_parts(h_ref[...].astype(F32))
    n_ref[...] = (hat * gain_ref[...].astype(F32) + shift_ref[...].astype(F32)).astype(BF16)
    wait_all(fetched)
    out.start(w_ref.at[pl.ds(O, 7)], w_out)
    out.start(w_ref.at[pl.ds(Q, 3)], proj_out)
    tap = tap_ref[...]
    kt_ref[...] = (nn(n_ref[...], weight(K)) * tap).astype(BF16)
    vt_ref[...] = (nn(n_ref[...], weight(V)) * tap).astype(BF16)
    q_ref[...] = nn(n_ref[...], weight(Q)).astype(BF16)
    out.start(q_ref, q_out)
    out.start(kt_ref, kt_out)
    out.start(vt_ref, vt_out)
    ck_ref[...] = sum(nn(kt_ref[t * WIN:(t + 1) * WIN, :], weight(KC + t)) for t in range(3)).astype(BF16)
    cv_ref[...] = sum(nn(vt_ref[t * WIN:(t + 1) * WIN, :], weight(VC + t)) for t in range(3)).astype(BF16)
    out.start(ck_ref, ck_out)
    out.start(cv_ref, cv_out)
    masks = head_mask(WIN)
    zero = jnp.zeros((WIN, 256), BF16)
    for g in range(2):
        cols = slice(g * 256, g * 256 + 256)
        for i in range(4):
            across_ref[:, i * WIN:i * WIN + WIN] = jnp.where(masks[i], cv_ref[:, cols], zero).T
        for i in range(4):
            s = nt(jnp.where(masks[i], ck_ref[:, cols], zero), q_ref[:, cols]) * (0.125 * LOG2E) + bias_ref[...]
            top = jnp.maximum(jnp.max(s, axis=0, keepdims=True), 0.0)
            num = jnp.exp2(s - top)
            den = jnp.exp2(-top) + jnp.sum(num, axis=0, keepdims=True)
            p_ref[g * 4 + i] = (num * (1.0 / den)).astype(BF16)
        heads = pl.ds(g * 4, 4)
        out.start(p_ref.at[heads], p_out.at[heads])
        ot_ref[cols, :] = nn(across_ref[...], p_ref[heads].reshape(4 * WIN, LEN)).astype(BF16)
    out.start(ot_ref, ot_out)
    h2_ref[...] = h_ref[...].astype(F32) + tn(ot_ref[...], weight(O))
    out.wait()


def feed_fwd(count, at, out_rows, idx_ref, h2_ref, gain_ref, shift_ref, *refs):
    own, other = refs[:count], refs[count:2 * count]
    (y_ref, a_out, gd_out, wu_out, wd_out, wu_ref, wd_ref, a_ref, gd_ref, n_ref, staged_ref, in_sems, out_sems) = refs[2 * count:]
    block = wu_ref.shape[1]

    def units(half, piece, quarter):
        if half == 0:
            return [(piece.at[:, pl.ds(at, 4 * block), :], wd_ref.at[:, :, pl.ds(pl.multiple_of(quarter * 128, 128), 128)])]
        return [(piece.at[:, pl.ds(at + i * block, block), :],
                 wu_ref.at[:, :, pl.ds(pl.multiple_of(quarter * 512 + i * 128, 128), 128)]) for i in range(4)]

    fetched = fetch_pieces(idx_ref, own, other, units, in_sems)
    hat, _s = norm_parts(h2_ref[...])
    n_ref[...] = (hat * gain_ref[...].astype(F32) + shift_ref[...].astype(F32)).astype(BF16)
    wait_all(fetched)
    out = Moves(out_sems)
    out.start(wu_ref, wu_out)
    out.start(wd_ref, wd_out)
    chunks = [slice(c * 512, c * 512 + 512) for c in range(4)]

    def up(c):
        return nn(n_ref[...], wu_ref[:, :, chunks[c]].reshape(D, 512))

    total = h2_ref[...]
    z = up(0)
    for c in range(4):
        later = up(c + 1) if c < 3 else None
        act, slope = gelu_both(z)
        act = act.astype(BF16)
        a_ref[:, chunks[c]] = act
        gd_ref[:, chunks[c]] = slope.astype(BF16)
        out.start(a_ref.at[:, chunks[c]], a_out.at[:, chunks[c]])
        out.start(gd_ref.at[:, chunks[c]], gd_out.at[:, chunks[c]])
        total = total + nn(act, wd_ref[...].reshape(FF, D)[chunks[c], :])
        z = later
    y_ref[...] = (to_rows(total, staged_ref) if out_rows else total).astype(BF16)
    out.wait()


def feed_back(idx_ref, gout_ref, h2_ref, gain_ref, wu, wd, a_ref, gd_ref, gh2_ref, keep_ref, send_ref, gz_ref,
              n_ref, gwu_ref, gwd_ref, vec_ref, sems, arrived):
    parts, quarters = gwu_ref.shape[0], keep_ref.shape[0]
    block = D // parts
    bits = quarters.bit_length() - 1
    wide = FF // quarters
    arrived(slice(0, 1))
    gwd_ref[...] = tn(a_ref[...], gout_ref[...]).astype(BF16).reshape(parts, 4 * block, D)
    slots = [[relative(q ^ idx_ref[0], half, bits) for half in range(2)] for q in range(quarters)]
    down = [(gwd_ref.at[:, :, q * 128:q * 128 + 128], (slots[q][0], slice(None), pl.ds(0, 4 * block)))
            for q in range(quarters)]
    copies = send_halves(idx_ref, (down, []), keep_ref, send_ref, sems)
    arrived(slice(1, 3))
    for c in range(4):
        cols = slice(c * 512, c * 512 + 512)
        gz_ref[:, cols] = (nt(gout_ref[...], wd[cols, :]) * gd_ref[:, cols].astype(F32)).astype(BF16)
    arrived(slice(3, 4))
    gwu_ref[...] = tn(n_ref[...], gz_ref[...]).astype(BF16).reshape(parts, block, FF)
    up = [(gwu_ref.at[:, :, q * wide + i * 128:q * wide + i * 128 + 128],
           (slots[q][1], slice(None), pl.ds(i * block, block))) for q in range(quarters) for i in range(wide // 128)]
    copies += send_halves(idx_ref, ([], up), keep_ref, send_ref, sems, len(copies))
    gn = nt(gz_ref[...], wu[...])
    hat, scale = norm_parts(h2_ref[...])
    fill_vectors(vec_ref, [jnp.sum(gn * hat, axis=0, keepdims=True), jnp.sum(gn, axis=0, keepdims=True)])
    vectors = [[(vec_ref, (slots[q][half], slice(None), pl.ds(4 * block, 16))) for q in range(quarters)]
               for half in range(2)]
    copies += send_halves(idx_ref, vectors, keep_ref, send_ref, sems, len(copies))
    gh2_ref[...] = gout_ref[...].astype(F32) + norm_back(gn, hat, scale, gain_ref[...].astype(F32))
    wait_all(copies)


def feed_both(count, at, idx_ref, h2_ref, gain_ref, shift_ref, gout_in, *refs):
    own, other = refs[:count], refs[count:2 * count]
    (y_ref, gh2_ref, keep_ref, send_ref, wu_ref, wd_ref, a_ref, gd_ref, gz_ref, n_ref, gwu_ref, gwd_ref, vec_ref,
     gout_ref, staged_ref, in_sems, sems) = refs[2 * count:]
    block = wu_ref.shape[1]

    def units(half, piece, quarter):
        if half == 0:
            return [(piece.at[:, pl.ds(at, 4 * block), :], wd_ref.at[:, :, pl.ds(pl.multiple_of(quarter * 128, 128), 128)])]
        return [(piece.at[:, pl.ds(at + i * block, block), :],
                 wu_ref.at[:, :, pl.ds(pl.multiple_of(quarter * 512 + i * 128, 128), 128)]) for i in range(4)]

    fetched = fetch_pieces(idx_ref, own, other, units, in_sems)
    for t, rows in enumerate(to_taps(gout_in[...], staged_ref)):
        gout_ref[t * WIN:(t + 1) * WIN, :] = rows.astype(BF16)
    hat, _s = norm_parts(h2_ref[...])
    n_ref[...] = (hat * gain_ref[...].astype(F32) + shift_ref[...].astype(F32)).astype(BF16)
    wait_all(fetched)
    chunks = [slice(c * 512, c * 512 + 512) for c in range(4)]

    def up(c):
        return nn(n_ref[...], wu_ref[:, :, chunks[c]].reshape(D, 512))

    total = h2_ref[...]
    z = up(0)
    for c in range(4):
        later = up(c + 1) if c < 3 else None
        act, slope = gelu_both(z)
        act = act.astype(BF16)
        a_ref[:, chunks[c]] = act
        gd_ref[:, chunks[c]] = slope.astype(BF16)
        total = total + nn(act, wd_ref[...].reshape(FF, D)[chunks[c], :])
        z = later
    y_ref[...] = to_rows(total, staged_ref).astype(BF16)
    feed_back(idx_ref, gout_ref, h2_ref, gain_ref, wu_ref[...].reshape(D, FF), wd_ref[...].reshape(FF, D), a_ref, gd_ref,
              gh2_ref, keep_ref, send_ref, gz_ref, n_ref, gwu_ref, gwd_ref, vec_ref, sems, lambda step: None)


def feed_bwd(in_rows, idx_ref, gout_in, h2_ref, gain_ref, shift_ref, wu_in, wd_in, a_in, gd_in,
             gh2_ref, keep_ref, send_ref, wu_ref, wd_ref, a_ref, gd_ref, gz_ref, n_ref, gwu_ref, gwd_ref, vec_ref,
             gout_ref, staged_ref, in_sems, sems):
    arriving = Moves(in_sems)
    for src, dst in ((a_in, a_ref), (wd_in, wd_ref), (gd_in, gd_ref), (wu_in, wu_ref)):
        arriving.start(src, dst)
    for t, rows in enumerate(to_taps(gout_in[...], staged_ref) if in_rows else []):
        gout_ref[t * WIN:(t + 1) * WIN, :] = rows.astype(BF16)
    if not in_rows:
        gout_ref[...] = gout_in[...]
    hat, scale = norm_parts(h2_ref[...])
    n_ref[...] = (hat * gain_ref[...].astype(F32) + shift_ref[...].astype(F32)).astype(BF16)
    feed_back(idx_ref, gout_ref, h2_ref, gain_ref, wu_ref, wd_ref, a_ref, gd_ref, gh2_ref, keep_ref, send_ref, gz_ref,
              n_ref, gwu_ref, gwd_ref, vec_ref, sems, lambda step: wait_all(arriving.items[step]))


def attn_bwd(idx_ref, gh2_ref, tap_ref, w_in, q_in, kt_in, vt_in, ck_ref, cv_ref, p_in,
             gq_out, gk_out, gv_out, keep_ref, send_ref,
             w_ref, q_ref, kt_ref, vt_ref, p_ref, go_ref, gq_ref, gk_ref, gv_ref, gck_ref, gcv_ref, gw_ref, gs_ref, across_ref,
             in_sems, out_sems, sems):
    arriving = Moves(in_sems)
    arriving.start(w_in.at[pl.ds(0, 1)], w_ref.at[pl.ds(6, 1)])
    arriving.start(q_in, q_ref)
    arriving.start(p_in, p_ref)
    arriving.start(w_in.at[pl.ds(1, 3)], w_ref.at[pl.ds(0, 3)])
    arriving.start(w_in.at[pl.ds(4, 3)], w_ref.at[pl.ds(3, 3)])
    arriving.start(kt_in, kt_ref)
    arriving.start(vt_in, vt_ref)
    out = Moves(out_sems)
    parts, quarters = gw_ref.shape[1], keep_ref.shape[0]
    block = D // parts
    shaped = (parts, block, D)
    wait_all(arriving.items[:1])
    go_ref[...] = nt(gh2_ref[...].astype(BF16), w_ref[6].reshape(D, D)).astype(BF16)
    masks = head_mask(WIN)
    zero = jnp.zeros((WIN, 256), BF16)
    wait_all(arriving.items[1:3])

    def own_lanes(stacked):
        return sum(jnp.where(masks[i], stacked[i * WIN:(i + 1) * WIN, :], 0.0) for i in range(4))

    for g in range(2):
        cols = slice(g * 256, g * 256 + 256)
        for i in range(4):
            across_ref[:, i * WIN:i * WIN + WIN] = jnp.where(masks[i], ck_ref[:, cols], zero).T
        for i in range(4):
            gp = nt(jnp.where(masks[i], cv_ref[:, cols], zero), go_ref[:, cols])
            p = p_ref[g * 4 + i].astype(F32)
            pg = p * gp
            gs_ref[i * WIN:i * WIN + WIN, :] = (pg - p * jnp.sum(pg, axis=0, keepdims=True)).astype(BF16)
        stacked = p_ref[pl.ds(g * 4, 4)].reshape(4 * WIN, LEN)
        gcv_ref[:, cols] = own_lanes(nn(stacked, go_ref[:, cols])).astype(BF16)
        gck_ref[:, cols] = (own_lanes(nn(gs_ref[...], q_ref[:, cols])) * 0.125).astype(BF16)
        gq_ref[:, cols] = (nn(across_ref[...], gs_ref[...]) * 0.125).astype(BF16).T

    out.start(gq_ref, gq_out)
    gck, gcv = gck_ref[...], gcv_ref[...]
    wait_all(arriving.items[3:])
    for t in range(3):
        rows = slice(t * WIN, t * WIN + WIN)
        gw_ref[t] = tn(kt_ref[rows, :], gck).astype(BF16).reshape(shaped)
        gw_ref[3 + t] = tn(vt_ref[rows, :], gcv).astype(BF16).reshape(shaped)

    halves = [], []
    bits = quarters.bit_length() - 1
    for q in range(quarters):
        for half in range(2):
            slot = relative(q ^ idx_ref[0], half, bits)
            for u in range(3):
                halves[half].append((gw_ref.at[half * 3 + u, :, :, q * 128:q * 128 + 128],
                                     (slot, slice(None), pl.ds(u * block, block))))
    copies = send_halves(idx_ref, halves, keep_ref, send_ref, sems)
    for t in range(3):
        rows = slice(t * WIN, t * WIN + WIN)
        tap = tap_ref[rows, :]
        gk_ref[rows, :] = (nt(gck, w_ref[t].reshape(D, D)) * tap).astype(BF16)
        gv_ref[rows, :] = (nt(gcv, w_ref[3 + t].reshape(D, D)) * tap).astype(BF16)
    out.start(gk_ref, gk_out)
    out.start(gv_ref, gv_out)
    wait_all(copies)
    out.wait()


def proj_bwd(out_rows, idx_ref, gh2_ref, h_ref, gain_ref, shift_ref, w_in, gq_ref, gk_ref, gv_ref, ot_in,
             gh_ref, keep_ref, send_ref, w_ref, ot_ref, n_ref, gw_ref, vec_ref, staged_ref, in_sems, sems):
    arriving = Moves(in_sems)
    arriving.start(w_in, w_ref)
    arriving.start(ot_in, ot_ref)
    gain = gain_ref[...].astype(F32)
    parts, quarters = gw_ref.shape[1], keep_ref.shape[0]
    block = D // parts
    shaped = (parts, block, D)
    bits = quarters.bit_length() - 1
    slots = [[relative(q ^ idx_ref[0], half, bits) for half in range(2)] for q in range(quarters)]
    hat, scale = norm_parts(h_ref[...].astype(F32))
    n_ref[...] = (hat * gain + shift_ref[...].astype(F32)).astype(BF16)
    arriving.wait()
    gn = (nt(gq_ref[...], w_ref[0].reshape(D, D)) + nt(gk_ref[...], w_ref[1].reshape(D, D))
          + nt(gv_ref[...], w_ref[2].reshape(D, D)))
    fill_vectors(vec_ref, [jnp.sum(gn * hat, axis=0, keepdims=True), jnp.sum(gn, axis=0, keepdims=True)])
    vectors = [[(vec_ref, (slots[q][half], slice(None), pl.ds(2 * block, 16))) for q in range(quarters)]
               for half in range(2)]
    copies = send_halves(idx_ref, vectors, keep_ref, send_ref, sems)
    gh = gh2_ref[...] + norm_back(gn, hat, scale, gain)
    gh_ref[...] = (to_rows(gh, staged_ref) if out_rows else gh).astype(BF16)
    gw_ref[3] = nn(ot_ref[...], gh2_ref[...].astype(BF16)).astype(BF16).reshape(shaped)
    across = n_ref[...].T
    for u, grad in enumerate((gq_ref, gk_ref, gv_ref)):
        gw_ref[u] = nn(across, grad[...]).astype(BF16).reshape(shaped)
    weights = [[(gw_ref.at[half * 2 + u, :, :, q * 128:q * 128 + 128], (slots[q][half], slice(None), pl.ds(u * block, block)))
                for q in range(quarters) for u in range(2)] for half in range(2)]
    copies += send_halves(idx_ref, weights, keep_ref, send_ref, sems, len(copies))
    wait_all(copies)


def place_shards(n, idx_ref, *refs):
    pieces, outs, sems = refs[:n], refs[n:-1], refs[-1]
    moves = Moves(sems)
    for k, piece in enumerate(pieces):
        at = 0
        for out in outs:
            rows = out.shape[1]
            moves.start(piece.at[pl.ds(at, rows), :], out.at[lax.rem(idx_ref[2] + n - k, n)])
            at += rows
    moves.wait()


def add_kernel(jobs, idx_ref, *refs):
    outs = refs[sum(2 * groups * chunks for groups, chunks in jobs):]
    at_in = at_out = 0
    for groups, chunks in jobs:
        at = 0
        for _ in range(chunks):
            for g in range(groups):
                keep, recv = refs[at_in], refs[at_in + 1]
                at_in += 2
                rows = keep.shape[1]
                outs[at_out + g][:, at:at + rows, :] = (keep[...].astype(F32) + recv[...].astype(F32)).astype(BF16)
            at += rows
        at_out += groups


def add_parts(idx, jobs, deps=(), us=0.1):
    sizes = [chunks[0][0].shape[0] // groups for chunks, groups, _ in jobs]
    ordered = [each for (_, _, index), each in zip(jobs, sizes) if index]
    steps = ordered[0] if ordered else min(min(sizes), 4)
    in_specs, out_specs, shapes, args, plan = [], [], [], [], []
    for (chunks, groups, index), each in zip(jobs, sizes):
        lead = each // steps
        total = sum(keep.shape[1] for keep, _ in chunks)
        plan.append((groups, len(chunks)))
        for keep, recv in chunks:
            for g in range(groups):
                if index:
                    where = functools.partial(lambda index, g, i, s: (index(g, i, s), 0, 0), index, g)
                else:
                    where = functools.partial(lambda g, i, s: (i + g * steps, 0, 0), g)
                in_specs += [pl.BlockSpec((lead, keep.shape[1], 128), where)] * 2
                args += [keep, recv]
        out_specs += [pl.BlockSpec((lead, total, 128), lambda i, s: (i, 0, 0))] * groups
        shapes += [jax.ShapeDtypeStruct((each, total, 128), BF16)] * groups
    count = len(args)

    def with_deps(idx_ref, *refs):
        add_kernel(plan, idx_ref, *refs[:count], *refs[count + len(deps):])

    made = pl.pallas_call(
        with_deps,
        grid_spec=pltpu.PrefetchScalarGridSpec(
            num_scalar_prefetch=1, grid=(steps,), in_specs=in_specs + [ANY] * len(deps), out_specs=out_specs),
        out_shape=shapes,
        compiler_params=pltpu.CompilerParams(vmem_limit_bytes=24 * 2**20),
        cost_estimate=pl.CostEstimate(flops=int(us * 1.1e9), bytes_accessed=1024, transcendentals=0),
        name="add_parts",
    )(idx, *args, *deps)
    split, at = [], 0
    for groups, _ in plan:
        split.append(made[at:at + groups])
        at += groups
    return split


def unpack(quarters, starts, idx_ref, *refs):
    outs, held, sems = refs[2 * quarters:-2], refs[-2], refs[-1]
    core, replica = idx_ref[1], idx_ref[0]
    rows = held.shape[2]
    for here in range(2):
        @pl.when(core == here)
        def _():
            for k in range(quarters):
                for half in range(2):
                    source = refs[(1 - here) * quarters + k].at[pl.ds(0 if half == here else rows, rows), :]
                    pltpu.make_async_copy(source, held.at[half, replica ^ k], sems.at[half * quarters + k]).start()
    for k in range(quarters):
        for half in range(2):
            pltpu.make_async_copy(refs[k].at[pl.ds(0, rows), :], held.at[half, k], sems.at[half * quarters + k]).wait()
    down, up, key_conv, value_conv = outs[:4]
    block = up.shape[0]
    feed, conv, proj = starts
    for q in range(quarters):
        cols = slice(q * 128, q * 128 + 128)
        down[:, cols] = held[0, q, feed:feed + 4 * block, :].astype(F32)
        for i in range(4):
            at = q * 512 + i * 128
            up[:, at:at + 128] = held[1, q, feed + i * block:feed + (i + 1) * block, :].astype(F32)
        for t in range(3):
            key_conv[t, :, cols] = held[0, q, conv + t * block:conv + (t + 1) * block, :].astype(F32)
            value_conv[t, :, cols] = held[1, q, conv + t * block:conv + (t + 1) * block, :].astype(F32)
        for u in range(4):
            at = proj + u % 2 * block
            outs[4 + u][:, cols] = held[u // 2, q, at:at + block, :].astype(F32)


def plain(kernel, in_specs, outs, out_specs, scratch, name, us, *args, deps=(), mib=16):
    count = len(args)

    def with_deps(*refs):
        kernel(*refs[:count], *refs[count + len(deps):])

    return pl.pallas_call(
        with_deps,
        out_shape=[jax.ShapeDtypeStruct(s, d) for s, d in outs],
        in_specs=list(in_specs) + [ANY] * len(deps),
        out_specs=out_specs,
        scratch_shapes=scratch,
        compiler_params=pltpu.CompilerParams(vmem_limit_bytes=mib * 2**20),
        cost_estimate=pl.CostEstimate(flops=int(us * 1.1e9), bytes_accessed=1024, transcendentals=0),
        name=name,
    )(*args, *deps)


def geometry(segments, validity, block_len):
    seg = segments.reshape(WIN, 3)
    val = validity.reshape(WIN, 3)
    anchor_seg = seg[:, 2]
    tap = ((seg == anchor_seg[:, None]) & (val == 1)).astype(F32).T.reshape(LEN, 1)
    seg_t = seg.T.reshape(LEN)
    window = jnp.arange(WIN, dtype=jnp.int32)
    position = (window[None, :] * 3 + jnp.arange(3, dtype=jnp.int32)[:, None]).reshape(LEN)
    anchor = window * 3 + 2
    allowed = (anchor[:, None] <= position[None, :]) & (anchor_seg[:, None] == seg_t[None, :])
    allowed = allowed & (val[:, 2][:, None] == 1) & (anchor[:, None] // block_len == position[None, :] // block_len)
    return tap, jnp.where(allowed, 0.0, NEGATIVE).astype(F32)


def tie(value, *others):
    return lax.optimization_barrier((value,) + others)[0]


def swap_cores(value):
    return lax.ppermute(value, "section", [(0, 1), (1, 0)])


def dp_swap(value, step, bits):
    route = []
    for replica in range(2**bits):
        for core in range(2):
            bit = step if core == 0 else bits - 1 - step
            route.append((replica * 2 + core, (replica ^ (1 << bit)) * 2 + core))
    return lax.ppermute(value, ("dp", "section"), route)


def shard_gather(idx, piece, n, deps=(), parts=None):
    parts = parts or [piece.shape[0]]
    if n > 8:
        whole = lax.all_gather(piece, "shard", axis=0)
        return [whole[:, sum(parts[:i]):sum(parts[:i + 1])] for i in range(len(parts))]
    pieces = [piece] + [lax.ppermute(piece, "shard", [(i, (i + k) % n) for i in range(n)]) for k in range(1, n)]
    return plain(functools.partial(place_shards, n), [SMEM] + [ANY] * n, [((n, rows, 128), BF16) for rows in parts],
                 [VMEM] * len(parts), [DMA((n * len(parts),))], "place_shards", 1, idx, *pieces, deps=deps)


def shard_step(value, step, n):
    return lax.ppermute(value, "shard", [(i, i ^ (1 << step)) for i in range(n)])


def shard_order(bits):
    def index(g, i, idx_ref):
        place = i + g * (1 << (bits - 1))
        return sum(((place >> k) & 1) << (bits - 1 - k) for k in range(bits)) ^ idx_ref[2]
    return index


class Sums:
    def __init__(self, keep, recv):
        self.keep, self.recv = keep, recv


class Hops:
    def __init__(self, idx, n, bits):
        self.idx, self.n, self.bits, self.last = idx, n, bits, None

    def run(self, *jobs, beside=(), deps=(), us=0.1):
        n = self.n
        direct = n <= 8
        listed = []
        for chunks, what in jobs:
            pairs = [(c.keep, c.recv) for c in chunks]
            if isinstance(what, tuple):
                listed.append((pairs, 2, shard_order(n.bit_length() - 1) if what[1] == 0 else None))
            elif what == "shard" and direct:
                listed.append((pairs, n, lambda g, i, s: lax.rem(s[2] + g, n)))
            elif what == "shard":
                listed.append((pairs, 2, shard_order(n.bit_length() - 1)))
            else:
                listed.append((pairs, 2, None))
        made = add_parts(self.idx, listed, tuple(deps) + (() if self.last is None else (self.last,)), us)
        self.last = made[0][0]
        results = []
        for (chunks, what), parts in zip(jobs, made):
            if isinstance(what, tuple):
                results.append(Sums(parts[0], shard_step(parts[1], what[1], n)))
            elif what == "shard" and direct:
                got = [lax.ppermute(parts[k], "shard", [(i, (i + k) % n) for i in range(n)]) for k in range(1, n)]
                got = [tie(g, *beside) for g in got] if beside else got
                results.append(sum([parts[0].astype(F32)] + [g.astype(F32) for g in got])[0].astype(BF16))
            elif what == "shard":
                keep, recv = parts[0], shard_step(parts[1], 0, n)
                for step in range(1, n.bit_length() - 1):
                    (keep, send), = add_parts(self.idx, [([(keep, recv)], 2, None)])
                    recv = shard_step(send, step, n)
                results.append((keep[0].astype(F32) + recv[0].astype(F32)).astype(BF16))
            else:
                results.append(Sums(parts[0], dp_swap(parts[1], what, self.bits)))
        return results

    def shard_steps(self, chunks, first=0):
        for step in range(first, self.n.bit_length() - 1):
            chunks, = self.run((chunks if isinstance(chunks, list) else [chunks], ("shard", step)))
        return chunks

    def total(self, sums):
        sums = Sums(tie(sums.keep, self.last), tie(sums.recv, self.last))
        return (sums.keep[0].astype(F32) + sums.recv[0].astype(F32)).astype(BF16)

    def collect(self, total, owner):
        total = tie(total, self.last)
        both = jnp.concatenate([total, lax.ppermute(total, "section", [(1 - owner, owner)])])
        quarters = 2**self.bits
        return [both] + [lax.ppermute(both, ("dp", "section"),
                                      [(2 * i + owner, 2 * (i ^ k) + owner) for i in range(quarters)])
                         for k in range(1, quarters)]


def body(boundary, segment_ids, token_valid, attention_gain, attention_bias, query_weight, key_weight, value_weight,
         key_conv, value_conv, out_weight, feed_gain, feed_bias, up_weight, down_weight):
    core = lax.axis_index("section")
    replica = lax.axis_index("dp")
    first = core == 0
    quarters = lax.axis_size("dp")
    bits = quarters.bit_length() - 1
    n = lax.axis_size("shard")
    block = D // n
    idx = jnp.stack([replica, core, lax.axis_index("shard")]).astype(jnp.int32)

    def quarter(weight, width=128):
        return lax.dynamic_slice_in_dim(weight, replica * width, width, weight.ndim - 1)

    vectors = jnp.stack([attention_gain[0], attention_bias[0], feed_gain[0], feed_bias[0]])
    vectors = jnp.pad(vectors, ((0, 12), (0, 128 - block)))
    key_taps = quarter(key_conv[0]).transpose(1, 0, 2).reshape(3 * block, 128)
    value_taps = quarter(value_conv[0]).transpose(1, 0, 2).reshape(3 * block, 128)
    attn_halves = (jnp.concatenate([quarter(query_weight[0]), quarter(key_weight[0]), key_taps, vectors]),
                   jnp.concatenate([quarter(value_weight[0]), quarter(out_weight[0]), value_taps, vectors]))
    up_part = quarter(up_weight[0], 512).reshape(block, 4, 128).transpose(1, 0, 2).reshape(4 * block, 128)
    feed_halves = (quarter(down_weight[0]), up_part)
    pieces = []
    for halves in (attn_halves, feed_halves):
        kept = jnp.where(first, halves[0], halves[1])
        got = swap_cores(jnp.where(first, halves[1], halves[0]))
        pieces.append((jnp.where(first, kept, got), jnp.where(first, got, kept)))

    own_rows = boundary[0].reshape(2, LEN, D)
    mine = lax.dynamic_index_in_dim(own_rows, core, 0, keepdims=False)
    theirs = swap_cores(lax.dynamic_index_in_dim(own_rows, 1 - core, 0, keepdims=False))
    h = jnp.where(first, mine, theirs)
    cot = jnp.where(first, theirs, mine)
    segments = lax.dynamic_index_in_dim(segment_ids.reshape(2, LEN), core, 0, keepdims=False)
    validity = lax.dynamic_index_in_dim(token_valid.reshape(2, LEN), core, 0, keepdims=False)

    square = (n, block, D)
    saved = []

    def run_attn_fwd(length, h, here, own, other, deps):
        gains = here[:, 5 * block:5 * block + 4, :block].transpose(1, 0, 2).reshape(4, 1, D)
        tap, bias = geometry(segments, validity, length)
        outs = [(ROW, F32), (ROW, BF16), (ROW, BF16), (ROW, BF16), (ROW, BF16), ((WIN, D), BF16), ((WIN, D), BF16),
                ((H, WIN, LEN), BF16), ((D, LEN), BF16), ((7,) + square, BF16), ((3,) + square, BF16)]
        made = plain(
            functools.partial(attn_fwd, len(own), length == BLK), [SMEM] + [VMEM] * 5 + [ANY] * (2 * len(own)), outs,
            [VMEM] * 2 + [ANY] * 9,
            [pltpu.VMEM((10,) + square, BF16)] + [pltpu.VMEM(outs[i][0], BF16) for i in (2, 3, 4, 5, 6, 7, 8)]
            + [pltpu.VMEM(ROW, BF16), pltpu.VMEM((256, 4 * WIN), BF16), pltpu.VMEM((D // 128, LEN, 128), F32), DMA((10 * quarters,)), DMA((10,))],
            "attn_fwd", 13, idx, h, bias, tap, gains[0], gains[1], *own, *other, deps=deps, mib=56)
        return gains, tap, made

    def run_feed_fwd(h2, gains, own, other, at, deps):
        outs = [(ROW, BF16), ((LEN, FF), BF16), ((LEN, FF), BF16), ((n, block, FF), BF16), ((n, 4 * block, D), BF16)]
        y, act, slope, up, down = plain(
            functools.partial(feed_fwd, len(own), at, at > 0), [SMEM] + [VMEM] * 3 + [ANY] * (2 * len(own)), outs,
            [VMEM] + [ANY] * 4, [pltpu.VMEM(outs[i][0], BF16) for i in (3, 4, 1, 2)]
            + [pltpu.VMEM(ROW, BF16), pltpu.VMEM((D // 128, LEN, 128), F32), DMA((5 * quarters,)), DMA((10,))],
            "feed_fwd", 13, idx, h2, gains[2], gains[3], *own, *other, deps=deps, mib=56)
        return y, (act, slope, up.reshape(D, FF), down.reshape(FF, D))

    def spread(piece, last_after=None):
        pieces = [piece]
        for step in reversed(range(bits)):
            final = step == 0 and last_after is not None
            pieces += [dp_swap(tie(held, last_after) if final and at else held, step, bits)
                       for at, held in enumerate(list(pieces))]
        return pieces

    def between(own, after):
        return [swap_cores(held if mark is None else tie(held, mark)) for held, mark in zip(own, after)]

    attn_here, = shard_gather(idx, pieces[0][0], n)
    attn_own = spread(attn_here)
    feed_here, = shard_gather(idx, tie(pieces[1][0], attn_here), n, tuple(attn_own[1:3]))
    feed_own = spread(feed_here)
    attn_other = [swap_cores(held) for held in attn_own]
    next_piece = jnp.concatenate([pieces[0][1], pieces[1][1]])
    next_here, = shard_gather(idx, tie(next_piece, feed_here), n, tuple(attn_own[3:] + feed_own[1:3] + attn_other[:3]))
    gains, tap, made = run_attn_fwd(BLK, h, attn_here, attn_own, attn_other, (next_here,))
    h2 = made[0]
    next_own = spread(next_here, h2)
    feed_other = between(feed_own, [None] * 3 + [h2] * (quarters - 3))
    y, feed = run_feed_fwd(h2, gains, feed_own, feed_other, 0, ())
    saved.append((made[1], h2, gains, tap) + tuple(made[2:]) + feed)
    next_other = between(next_own, [h2] * 3 + [y] * (quarters - 3))
    gains, tap, made = run_attn_fwd(LEN, y, next_here, next_own, next_other, ())
    saved.append((made[1], made[0], gains, tap) + tuple(made[2:]) + (None,) * 4)

    rows_feed, rows_conv, rows_proj = 4 * block + 16, 3 * block, 2 * block + 16

    def halves_of(keep, send):
        recv = swap_cores(send)
        return Sums(keep.reshape((-1,) + keep.shape[2:]), recv.reshape((-1,) + recv.shape[2:]))

    def run_feed_bwd(layer, grad, deps=()):
        h, h2, gains, tap, q, kt, vt, ck, cv, p, ot, w, w_proj, act, slope, up, down = saved[layer]
        shape = (quarters, n, rows_feed, 128)
        gh2, keep, send = plain(
            functools.partial(feed_bwd, layer == 1), [SMEM] + [VMEM] * 4 + [ANY] * 4, [(ROW, F32), (shape, BF16), (shape, BF16)], [VMEM, ANY, ANY],
            [pltpu.VMEM((D, FF), BF16), pltpu.VMEM((FF, D), BF16), pltpu.VMEM((LEN, FF), BF16),
             pltpu.VMEM((LEN, FF), BF16), pltpu.VMEM((LEN, FF), BF16), pltpu.VMEM(ROW, BF16),
             pltpu.VMEM((n, block, FF), BF16), pltpu.VMEM((n, 4 * block, D), BF16), pltpu.VMEM((n, 16, 128), BF16),
             pltpu.VMEM(ROW, BF16), pltpu.VMEM((D // 128, LEN, 128), F32), DMA((4,)), DMA((quarters * 7,))],
            "feed_bwd", 7, idx, grad, h2, gains[2], gains[3], up, down, act, slope, deps=deps, mib=56)
        return gh2, halves_of(keep, send)

    def run_feed_both(h2, gains, grad, own, other, at):
        shape = (quarters, n, rows_feed, 128)
        result, gh2, keep, send = plain(
            functools.partial(feed_both, len(own), at), [SMEM] + [VMEM] * 4 + [ANY] * (2 * len(own)),
            [(ROW, BF16), (ROW, F32), (shape, BF16), (shape, BF16)], [VMEM, VMEM, ANY, ANY],
            [pltpu.VMEM((n, block, FF), BF16), pltpu.VMEM((n, 4 * block, D), BF16)] + [pltpu.VMEM((LEN, FF), BF16)] * 3
            + [pltpu.VMEM(ROW, BF16), pltpu.VMEM((n, block, FF), BF16), pltpu.VMEM((n, 4 * block, D), BF16),
               pltpu.VMEM((n, 16, 128), BF16), pltpu.VMEM(ROW, BF16), pltpu.VMEM((D // 128, LEN, 128), F32),
               DMA((5 * quarters,)), DMA((quarters * 7,))],
            "feed_both", 20, idx, h2, gains[2], gains[3], grad, *own, *other, mib=56)
        return result, gh2, halves_of(keep, send)

    def run_attn_bwd(layer, gh2, deps=()):
        h, h2, gains, tap, q, kt, vt, ck, cv, p, ot, w, w_proj, act, slope, up, down = saved[layer]
        shape = (quarters, n, rows_conv, 128)
        gq, gk, gv, keep, send = plain(
            attn_bwd, [SMEM, VMEM, VMEM] + [ANY] * 4 + [VMEM] * 2 + [ANY],
            [(ROW, BF16)] * 3 + [(shape, BF16), (shape, BF16)], [ANY] * 5,
            [pltpu.VMEM((7,) + square, BF16)] + [pltpu.VMEM(ROW, BF16)] * 3 + [pltpu.VMEM((H, WIN, LEN), BF16)]
            + [pltpu.VMEM(ROW, BF16)] * 4 + [pltpu.VMEM((WIN, D), BF16)] * 2
            + [pltpu.VMEM((6,) + square, BF16), pltpu.VMEM((4 * WIN, LEN), BF16), pltpu.VMEM((256, 4 * WIN), BF16), DMA((7,)), DMA((3,)), DMA((quarters * 6,))],
            "attn_bwd", 7, idx, gh2, tap, w, q, kt, vt, ck, cv, p, deps=deps, mib=50)
        return gq, gk, gv, halves_of(keep, send)

    def run_proj_bwd(layer, gh2, gq, gk, gv, deps=()):
        h, h2, gains, tap, q, kt, vt, ck, cv, p, ot, w, w_proj, act, slope, up, down = saved[layer]
        shape = (quarters, n, rows_proj, 128)
        grad, keep, send = plain(
            functools.partial(proj_bwd, layer == 0), [SMEM] + [VMEM] * 4 + [ANY] + [VMEM] * 3 + [ANY], [(ROW, BF16), (shape, BF16), (shape, BF16)],
            [VMEM, ANY, ANY],
            [pltpu.VMEM((3,) + square, BF16), pltpu.VMEM((D, LEN), BF16), pltpu.VMEM(ROW, BF16),
             pltpu.VMEM((4,) + square, BF16), pltpu.VMEM((n, 16, 128), BF16), pltpu.VMEM((D // 128, LEN, 128), F32), DMA((3,)), DMA((quarters * 6,))],
            "proj_bwd", 6, idx, gh2, h, gains[0], gains[1], w_proj, gq, gk, gv, ot, deps=deps, mib=50)
        return grad, halves_of(keep, send)

    hops = Hops(idx, n, bits)
    result, gh2, feed_two = run_feed_both(saved[1][1], saved[1][2], cot, next_own, next_other, 5 * block + 16)
    gq, gk, gv, conv_two = run_attn_bwd(1, gh2)
    hops.last = gq
    feed_two, = hops.run(([feed_two], 0))
    grad, proj_two = run_proj_bwd(1, gh2, gq, gk, gv, deps=(hops.last,))
    hops.last = grad
    conv_two, = hops.run(([conv_two], 0))
    gh2, feed_one = run_feed_bwd(0, grad, deps=(hops.last,))
    hops.last = gh2
    feed_two, conv_two = hops.run(([feed_two], 1), ([conv_two], 1), us=24)
    mixed, = hops.run(([feed_one, proj_two], 0))
    gq, gk, gv, conv_one = run_attn_bwd(0, gh2, deps=(hops.last,))
    hops.last = gq
    grad, proj_one = run_proj_bwd(0, gh2, gq, gk, gv)
    hops.last = grad
    two, mixed = hops.run(([feed_two, conv_two], ("shard", 0)), ([mixed], 1), us=12)
    attn_one, = hops.run(([conv_one, proj_one], 0))
    two, = hops.run(([two], ("shard", 1)))
    mixed, = hops.run(([mixed], ("shard", 0)))
    attn_one, = hops.run(([attn_one], 1))
    mark = hops.last
    mixed, = hops.run(([mixed], ("shard", 1)), deps=(two.recv,))
    attn_one, = hops.run(([attn_one], "shard"))
    two, mixed = [hops.total(hops.shard_steps(x, 2)) for x in (two, mixed)]
    two_all = hops.collect(jnp.concatenate([two, mixed[rows_feed:]]), 1)
    one_all = hops.collect(jnp.concatenate([mixed[:rows_feed], tie(attn_one, *two_all[1:])]), 0)

    result, grad = tie(result, mark), tie(grad, mark)
    other = swap_cores(jnp.where(first, result, grad))
    ours = jnp.where(first, grad, result)
    section_ends = jnp.stack([jnp.where(first, ours, other), jnp.where(first, other, ours)]).reshape(1, 2 * LEN, D)
    total = rows_feed + rows_conv + rows_proj
    shapes = [(4 * block, D), (block, FF), (3, block, D), (3, block, D)] + [(block, D)] * 4
    gdown, gup, gkc, gvc, gq, gk, gv, go = plain(
        functools.partial(unpack, quarters, (0, rows_feed, rows_feed + rows_conv)), [SMEM] + [ANY] * (2 * quarters),
        [(shape, F32) for shape in shapes], [VMEM] * 8,
        [pltpu.VMEM((2, quarters, total, 128), BF16), DMA((2 * quarters,))], "unpack", 4,
        idx, *two_all, *one_all, mib=20)

    def vectors_of(one, two):
        return jnp.where(first, one[:2, :block], two[:2, :block]).astype(F32)

    vec_feed = vectors_of(one_all[0][4 * block:], two_all[0][4 * block:])
    vec_attn = vectors_of(one_all[0][rows_feed + rows_conv + 2 * block:], two_all[0][rows_feed + rows_conv + 2 * block:])
    return (section_ends, vec_attn[0:1], vec_attn[1:2], gq[None], gk[None], gv[None], gkc.transpose(1, 0, 2)[None],
            gvc.transpose(1, 0, 2)[None], go[None], vec_feed[0:1], vec_feed[1:2], gup[None], gdown[None])


def solution(mesh):
    vector, matrix, conv = P("section", "shard"), P("section", "shard", None), P("section", "shard", None, None)
    rows, tokens = P("section", ("dp", "shard"), None), P(("dp", "shard"))
    weights = (vector, vector, matrix, matrix, matrix, conv, conv, matrix, vector, vector, matrix, matrix)
    return jax.shard_map(body, mesh=mesh, in_specs=(rows, tokens, tokens) + weights, out_specs=(rows,) + weights,
                         check_vma=False)
```

```python
import functools

import jax
import jax.numpy as jnp
from jax import lax
from jax.experimental import pallas as pl
from jax.experimental.pallas import tpu as pltpu
from jax.sharding import PartitionSpec as P

D = 512
H = 8
HD = 64
FF = 2048
BLK = 256
LEN = 768
WIN = LEN // 3
EPSILON = 1e-05
NEGATIVE = -1e30
F32 = jnp.float32
BF16 = jnp.bfloat16
LOG2E = 1.4426950408889634
VMEM = pl.BlockSpec(memory_space=pltpu.VMEM)
ANY = pl.BlockSpec(memory_space=pl.ANY)
SMEM = pl.BlockSpec(memory_space=pltpu.SMEM)
DMA = pltpu.SemaphoreType.DMA
ROW = (LEN, D)
Q, K, V, O, KC, VC = 0, 1, 2, 3, 4, 7
HALVES = (Q, K, KC, KC + 1, KC + 2), (V, O, VC, VC + 1, VC + 2)


def nn(a, b):
    return lax.dot_general(a, b, (((1,), (0,)), ((), ())), preferred_element_type=F32)


def nt(a, b):
    return lax.dot_general(a, b, (((1,), (1,)), ((), ())), preferred_element_type=F32)


def tn(a, b):
    return lax.dot_general(a, b, (((0,), (0,)), ((), ())), preferred_element_type=F32)


def norm_parts(hidden):
    centred = hidden - jnp.mean(hidden, axis=-1, keepdims=True)
    spread = jnp.mean(centred * centred, axis=-1, keepdims=True)
    scale = lax.rsqrt(spread + EPSILON)
    return centred * scale, scale


def norm_back(grad, hat, scale, gain):
    inner = grad * gain
    mean_one = jnp.mean(inner, axis=-1, keepdims=True)
    mean_two = jnp.mean(inner * hat, axis=-1, keepdims=True)
    return scale * (inner - mean_one - hat * mean_two)


def gelu_both(z):
    phi = 0.5 + 0.5 * lax.erf(z * 0.7071067811865476)
    density = jnp.exp2(z * z * (-0.5 * LOG2E)) * 0.3989422804014327
    return z * phi, phi + z * density


def head_mask(rows):
    lane = lax.broadcasted_iota(jnp.int32, (rows, 256), 1) // HD
    return [lane == i for i in range(4)]


def relative(index, core, bits):
    return sum(((index >> k) & 1) << (bits - 1 - k) for k in range(bits)) if core == 0 else index


def to_taps(rows, staged_ref):
    for c in range(D // 128):
        staged_ref[c] = rows[:, c * 128:c * 128 + 128].astype(F32)
    return [jnp.concatenate([staged_ref[c, pl.ds(t, WIN, stride=3), :] for c in range(D // 128)], axis=1)
            for t in range(3)]


def to_rows(value, staged_ref):
    for c in range(D // 128):
        for t in range(3):
            staged_ref[c, pl.ds(t, WIN, stride=3), :] = value[t * WIN:(t + 1) * WIN, c * 128:c * 128 + 128]
    return jnp.concatenate([staged_ref[c] for c in range(D // 128)], axis=1)


class Moves:
    def __init__(self, sems):
        self.sems, self.items = sems, []

    def start(self, src, dst):
        copy = pltpu.make_async_copy(src, dst, self.sems.at[len(self.items)])
        copy.start()
        self.items.append(copy)
        return copy

    def wait(self):
        for copy in self.items:
            copy.wait()


def fetch_pieces(idx_ref, own, other, units, sems):
    core, replica = idx_ref[1], idx_ref[0]
    ordered = len(own) == 1
    quarters = own[0].shape[0] if ordered else len(own)
    bits = quarters.bit_length() - 1
    for here in range(2):
        made = []
        for half in range(2):
            side = own if half == here else other
            for m in range(quarters):
                piece = side[0].at[m] if ordered else side[m]
                made += units(half, piece, m if ordered else replica ^ relative(m, half, bits))

        @pl.when(core == here)
        def _():
            for i, (src, dst) in enumerate(made):
                pltpu.make_async_copy(src, dst, sems.at[i]).start()
    return [pltpu.make_async_copy(src, dst, sems.at[i]) for i, (src, dst) in enumerate(made)]


def send_halves(idx_ref, halves, keep_ref, send_ref, sems, base=0):
    core = idx_ref[1]
    for here in range(2):
        @pl.when(core == here)
        def _():
            i = base
            for half in range(2):
                for src, dst in halves[half]:
                    out = keep_ref if here == half else send_ref
                    pltpu.make_async_copy(src, out.at[dst], sems.at[i]).start()
                    i += 1
    items = halves[0] + halves[1]
    return [pltpu.make_async_copy(src, keep_ref.at[dst], sems.at[base + i]) for i, (src, dst) in enumerate(items)]


def fill_vectors(vec_ref, rows):
    vec_ref[...] = jnp.zeros_like(vec_ref)
    parts, block = vec_ref.shape[0], D // vec_ref.shape[0]
    for z in range(parts):
        for i, row in enumerate(rows):
            vec_ref[z, i:i + 1, :block] = row[:, z * block:(z + 1) * block].astype(BF16)


def wait_all(copies):
    for copy in copies:
        copy.wait()


def attn_fwd(count, in_rows, idx_ref, h_in, bias_ref, tap_ref, gain_ref, shift_ref, *refs):
    own, other = refs[:count], refs[count:2 * count]
    (h2_ref, h_ref, q_out, kt_out, vt_out, ck_out, cv_out, p_out, ot_out, w_out, proj_out,
     w_ref, q_ref, kt_ref, vt_ref, ck_ref, cv_ref, p_ref, ot_ref, n_ref, across_ref, staged_ref, in_sems, out_sems) = refs[2 * count:]
    block = w_ref.shape[2]

    def units(half, piece, quarter):
        cols = pl.ds(pl.multiple_of(quarter * 128, 128), 128)
        return [(piece.at[:, pl.ds(u * block, block), :], w_ref.at[place, :, :, cols])
                for u, place in enumerate(HALVES[half])]

    fetched = fetch_pieces(idx_ref, own, other, units, in_sems)
    out = Moves(out_sems)

    def weight(u):
        return w_ref[u].reshape(D, D)

    for t, rows in enumerate(to_taps(h_in[...], staged_ref) if in_rows else []):
        h_ref[t * WIN:(t + 1) * WIN, :] = rows.astype(BF16)
    if not in_rows:
        h_ref[...] = h_in[...]
    hat, _s = norm_parts(h_ref[...].astype(F32))
    n_ref[...] = (hat * gain_ref[...].astype(F32) + shift_ref[...].astype(F32)).astype(BF16)
    wait_all(fetched)
    out.start(w_ref.at[pl.ds(O, 7)], w_out)
    out.start(w_ref.at[pl.ds(Q, 3)], proj_out)
    tap = tap_ref[...]
    kt_ref[...] = (nn(n_ref[...], weight(K)) * tap).astype(BF16)
    vt_ref[...] = (nn(n_ref[...], weight(V)) * tap).astype(BF16)
    q_ref[...] = nn(n_ref[...], weight(Q)).astype(BF16)
    out.start(q_ref, q_out)
    out.start(kt_ref, kt_out)
    out.start(vt_ref, vt_out)
    ck_ref[...] = sum(nn(kt_ref[t * WIN:(t + 1) * WIN, :], weight(KC + t)) for t in range(3)).astype(BF16)
    cv_ref[...] = sum(nn(vt_ref[t * WIN:(t + 1) * WIN, :], weight(VC + t)) for t in range(3)).astype(BF16)
    out.start(ck_ref, ck_out)
    out.start(cv_ref, cv_out)
    masks = head_mask(WIN)
    zero = jnp.zeros((WIN, 256), BF16)
    for g in range(2):
        cols = slice(g * 256, g * 256 + 256)
        for i in range(4):
            across_ref[:, i * WIN:i * WIN + WIN] = jnp.where(masks[i], cv_ref[:, cols], zero).T
        for i in range(4):
            s = nt(jnp.where(masks[i], ck_ref[:, cols], zero), q_ref[:, cols]) * (0.125 * LOG2E) + bias_ref[...]
            top = jnp.maximum(jnp.max(s, axis=0, keepdims=True), 0.0)
            num = jnp.exp2(s - top)
            den = jnp.exp2(-top) + jnp.sum(num, axis=0, keepdims=True)
            p_ref[g * 4 + i] = (num * (1.0 / den)).astype(BF16)
        heads = pl.ds(g * 4, 4)
        out.start(p_ref.at[heads], p_out.at[heads])
        ot_ref[cols, :] = nn(across_ref[...], p_ref[heads].reshape(4 * WIN, LEN)).astype(BF16)
    out.start(ot_ref, ot_out)
    h2_ref[...] = h_ref[...].astype(F32) + tn(ot_ref[...], weight(O))
    out.wait()


def feed_fwd(count, at, out_rows, idx_ref, h2_ref, gain_ref, shift_ref, *refs):
    own, other = refs[:count], refs[count:2 * count]
    (y_ref, a_out, gd_out, wu_out, wd_out, wu_ref, wd_ref, a_ref, gd_ref, n_ref, staged_ref, in_sems, out_sems) = refs[2 * count:]
    block = wu_ref.shape[1]

    def units(half, piece, quarter):
        if half == 0:
            return [(piece.at[:, pl.ds(at, 4 * block), :], wd_ref.at[:, :, pl.ds(pl.multiple_of(quarter * 128, 128), 128)])]
        return [(piece.at[:, pl.ds(at + i * block, block), :],
                 wu_ref.at[:, :, pl.ds(pl.multiple_of(quarter * 512 + i * 128, 128), 128)]) for i in range(4)]

    fetched = fetch_pieces(idx_ref, own, other, units, in_sems)
    hat, _s = norm_parts(h2_ref[...])
    n_ref[...] = (hat * gain_ref[...].astype(F32) + shift_ref[...].astype(F32)).astype(BF16)
    wait_all(fetched)
    out = Moves(out_sems)
    out.start(wu_ref, wu_out)
    out.start(wd_ref, wd_out)
    chunks = [slice(c * 512, c * 512 + 512) for c in range(4)]

    def up(c):
        return nn(n_ref[...], wu_ref[:, :, chunks[c]].reshape(D, 512))

    total = h2_ref[...]
    z = up(0)
    for c in range(4):
        later = up(c + 1) if c < 3 else None
        act, slope = gelu_both(z)
        act = act.astype(BF16)
        a_ref[:, chunks[c]] = act
        gd_ref[:, chunks[c]] = slope.astype(BF16)
        out.start(a_ref.at[:, chunks[c]], a_out.at[:, chunks[c]])
        out.start(gd_ref.at[:, chunks[c]], gd_out.at[:, chunks[c]])
        total = total + nn(act, wd_ref[...].reshape(FF, D)[chunks[c], :])
        z = later
    y_ref[...] = (to_rows(total, staged_ref) if out_rows else total).astype(BF16)
    out.wait()


def feed_back(idx_ref, gout_ref, h2_ref, gain_ref, wu, wd, a_ref, gd_ref, gh2_ref, keep_ref, send_ref, gz_ref,
              n_ref, gwu_ref, gwd_ref, vec_ref, sems, arrived):
    parts, quarters = gwu_ref.shape[0], keep_ref.shape[0]
    block = D // parts
    bits = quarters.bit_length() - 1
    wide = FF // quarters
    arrived(slice(0, 1))
    gwd_ref[...] = tn(a_ref[...], gout_ref[...]).astype(BF16).reshape(parts, 4 * block, D)
    slots = [[relative(q ^ idx_ref[0], half, bits) for half in range(2)] for q in range(quarters)]
    down = [(gwd_ref.at[:, :, q * 128:q * 128 + 128], (slots[q][0], slice(None), pl.ds(0, 4 * block)))
            for q in range(quarters)]
    copies = send_halves(idx_ref, (down, []), keep_ref, send_ref, sems)
    arrived(slice(1, 3))
    for c in range(4):
        cols = slice(c * 512, c * 512 + 512)
        gz_ref[:, cols] = (nt(gout_ref[...], wd[cols, :]) * gd_ref[:, cols].astype(F32)).astype(BF16)
    arrived(slice(3, 4))
    gwu_ref[...] = tn(n_ref[...], gz_ref[...]).astype(BF16).reshape(parts, block, FF)
    up = [(gwu_ref.at[:, :, q * wide + i * 128:q * wide + i * 128 + 128],
           (slots[q][1], slice(None), pl.ds(i * block, block))) for q in range(quarters) for i in range(wide // 128)]
    copies += send_halves(idx_ref, ([], up), keep_ref, send_ref, sems, len(copies))
    gn = nt(gz_ref[...], wu[...])
    hat, scale = norm_parts(h2_ref[...])
    fill_vectors(vec_ref, [jnp.sum(gn * hat, axis=0, keepdims=True), jnp.sum(gn, axis=0, keepdims=True)])
    vectors = [[(vec_ref, (slots[q][half], slice(None), pl.ds(4 * block, 16))) for q in range(quarters)]
               for half in range(2)]
    copies += send_halves(idx_ref, vectors, keep_ref, send_ref, sems, len(copies))
    gh2_ref[...] = gout_ref[...].astype(F32) + norm_back(gn, hat, scale, gain_ref[...].astype(F32))
    wait_all(copies)


def feed_both(count, at, idx_ref, h2_ref, gain_ref, shift_ref, gout_in, *refs):
    own, other = refs[:count], refs[count:2 * count]
    (y_ref, gh2_ref, keep_ref, send_ref, wu_ref, wd_ref, a_ref, gd_ref, gz_ref, n_ref, gwu_ref, gwd_ref, vec_ref,
     gout_ref, staged_ref, in_sems, sems) = refs[2 * count:]
    block = wu_ref.shape[1]

    def units(half, piece, quarter):
        if half == 0:
            return [(piece.at[:, pl.ds(at, 4 * block), :], wd_ref.at[:, :, pl.ds(pl.multiple_of(quarter * 128, 128), 128)])]
        return [(piece.at[:, pl.ds(at + i * block, block), :],
                 wu_ref.at[:, :, pl.ds(pl.multiple_of(quarter * 512 + i * 128, 128), 128)]) for i in range(4)]

    fetched = fetch_pieces(idx_ref, own, other, units, in_sems)
    for t, rows in enumerate(to_taps(gout_in[...], staged_ref)):
        gout_ref[t * WIN:(t + 1) * WIN, :] = rows.astype(BF16)
    hat, _s = norm_parts(h2_ref[...])
    n_ref[...] = (hat * gain_ref[...].astype(F32) + shift_ref[...].astype(F32)).astype(BF16)
    wait_all(fetched)
    chunks = [slice(c * 512, c * 512 + 512) for c in range(4)]

    def up(c):
        return nn(n_ref[...], wu_ref[:, :, chunks[c]].reshape(D, 512))

    total = h2_ref[...]
    z = up(0)
    for c in range(4):
        later = up(c + 1) if c < 3 else None
        act, slope = gelu_both(z)
        act = act.astype(BF16)
        a_ref[:, chunks[c]] = act
        gd_ref[:, chunks[c]] = slope.astype(BF16)
        total = total + nn(act, wd_ref[...].reshape(FF, D)[chunks[c], :])
        z = later
    y_ref[...] = to_rows(total, staged_ref).astype(BF16)
    feed_back(idx_ref, gout_ref, h2_ref, gain_ref, wu_ref[...].reshape(D, FF), wd_ref[...].reshape(FF, D), a_ref, gd_ref,
              gh2_ref, keep_ref, send_ref, gz_ref, n_ref, gwu_ref, gwd_ref, vec_ref, sems, lambda step: None)


def feed_bwd(in_rows, idx_ref, gout_in, h2_ref, gain_ref, shift_ref, wu_in, wd_in, a_in, gd_in,
             gh2_ref, keep_ref, send_ref, wu_ref, wd_ref, a_ref, gd_ref, gz_ref, n_ref, gwu_ref, gwd_ref, vec_ref,
             gout_ref, staged_ref, in_sems, sems):
    arriving = Moves(in_sems)
    for src, dst in ((a_in, a_ref), (wd_in, wd_ref), (gd_in, gd_ref), (wu_in, wu_ref)):
        arriving.start(src, dst)
    for t, rows in enumerate(to_taps(gout_in[...], staged_ref) if in_rows else []):
        gout_ref[t * WIN:(t + 1) * WIN, :] = rows.astype(BF16)
    if not in_rows:
        gout_ref[...] = gout_in[...]
    hat, scale = norm_parts(h2_ref[...])
    n_ref[...] = (hat * gain_ref[...].astype(F32) + shift_ref[...].astype(F32)).astype(BF16)
    feed_back(idx_ref, gout_ref, h2_ref, gain_ref, wu_ref, wd_ref, a_ref, gd_ref, gh2_ref, keep_ref, send_ref, gz_ref,
              n_ref, gwu_ref, gwd_ref, vec_ref, sems, lambda step: wait_all(arriving.items[step]))


def attn_bwd(idx_ref, gh2_ref, tap_ref, w_in, q_in, kt_in, vt_in, ck_ref, cv_ref, p_in,
             gq_out, gk_out, gv_out, keep_ref, send_ref,
             w_ref, q_ref, kt_ref, vt_ref, p_ref, go_ref, gq_ref, gk_ref, gv_ref, gck_ref, gcv_ref, gw_ref, gs_ref, across_ref,
             in_sems, out_sems, sems):
    arriving = Moves(in_sems)
    arriving.start(w_in.at[pl.ds(0, 1)], w_ref.at[pl.ds(6, 1)])
    arriving.start(q_in, q_ref)
    arriving.start(p_in, p_ref)
    arriving.start(w_in.at[pl.ds(1, 3)], w_ref.at[pl.ds(0, 3)])
    arriving.start(w_in.at[pl.ds(4, 3)], w_ref.at[pl.ds(3, 3)])
    arriving.start(kt_in, kt_ref)
    arriving.start(vt_in, vt_ref)
    out = Moves(out_sems)
    parts, quarters = gw_ref.shape[1], keep_ref.shape[0]
    block = D // parts
    shaped = (parts, block, D)
    wait_all(arriving.items[:1])
    go_ref[...] = nt(gh2_ref[...].astype(BF16), w_ref[6].reshape(D, D)).astype(BF16)
    masks = head_mask(WIN)
    zero = jnp.zeros((WIN, 256), BF16)
    wait_all(arriving.items[1:3])

    def own_lanes(stacked):
        return sum(jnp.where(masks[i], stacked[i * WIN:(i + 1) * WIN, :], 0.0) for i in range(4))

    for g in range(2):
        cols = slice(g * 256, g * 256 + 256)
        for i in range(4):
            across_ref[:, i * WIN:i * WIN + WIN] = jnp.where(masks[i], ck_ref[:, cols], zero).T
        for i in range(4):
            gp = nt(jnp.where(masks[i], cv_ref[:, cols], zero), go_ref[:, cols])
            p = p_ref[g * 4 + i].astype(F32)
            pg = p * gp
            gs_ref[i * WIN:i * WIN + WIN, :] = (pg - p * jnp.sum(pg, axis=0, keepdims=True)).astype(BF16)
        stacked = p_ref[pl.ds(g * 4, 4)].reshape(4 * WIN, LEN)
        gcv_ref[:, cols] = own_lanes(nn(stacked, go_ref[:, cols])).astype(BF16)
        gck_ref[:, cols] = (own_lanes(nn(gs_ref[...], q_ref[:, cols])) * 0.125).astype(BF16)
        gq_ref[:, cols] = (nn(across_ref[...], gs_ref[...]) * 0.125).astype(BF16).T

    out.start(gq_ref, gq_out)
    gck, gcv = gck_ref[...], gcv_ref[...]
    wait_all(arriving.items[3:])
    for t in range(3):
        rows = slice(t * WIN, t * WIN + WIN)
        gw_ref[t] = tn(kt_ref[rows, :], gck).astype(BF16).reshape(shaped)
        gw_ref[3 + t] = tn(vt_ref[rows, :], gcv).astype(BF16).reshape(shaped)

    halves = [], []
    bits = quarters.bit_length() - 1
    for q in range(quarters):
        for half in range(2):
            slot = relative(q ^ idx_ref[0], half, bits)
            for u in range(3):
                halves[half].append((gw_ref.at[half * 3 + u, :, :, q * 128:q * 128 + 128],
                                     (slot, slice(None), pl.ds(u * block, block))))
    copies = send_halves(idx_ref, halves, keep_ref, send_ref, sems)
    for t in range(3):
        rows = slice(t * WIN, t * WIN + WIN)
        tap = tap_ref[rows, :]
        gk_ref[rows, :] = (nt(gck, w_ref[t].reshape(D, D)) * tap).astype(BF16)
        gv_ref[rows, :] = (nt(gcv, w_ref[3 + t].reshape(D, D)) * tap).astype(BF16)
    out.start(gk_ref, gk_out)
    out.start(gv_ref, gv_out)
    wait_all(copies)
    out.wait()


def proj_bwd(out_rows, idx_ref, gh2_ref, h_ref, gain_ref, shift_ref, w_in, gq_ref, gk_ref, gv_ref, ot_in,
             gh_ref, keep_ref, send_ref, w_ref, ot_ref, n_ref, gw_ref, vec_ref, staged_ref, in_sems, sems):
    arriving = Moves(in_sems)
    arriving.start(w_in, w_ref)
    arriving.start(ot_in, ot_ref)
    gain = gain_ref[...].astype(F32)
    parts, quarters = gw_ref.shape[1], keep_ref.shape[0]
    block = D // parts
    shaped = (parts, block, D)
    bits = quarters.bit_length() - 1
    slots = [[relative(q ^ idx_ref[0], half, bits) for half in range(2)] for q in range(quarters)]
    hat, scale = norm_parts(h_ref[...].astype(F32))
    n_ref[...] = (hat * gain + shift_ref[...].astype(F32)).astype(BF16)
    arriving.wait()
    gn = (nt(gq_ref[...], w_ref[0].reshape(D, D)) + nt(gk_ref[...], w_ref[1].reshape(D, D))
          + nt(gv_ref[...], w_ref[2].reshape(D, D)))
    fill_vectors(vec_ref, [jnp.sum(gn * hat, axis=0, keepdims=True), jnp.sum(gn, axis=0, keepdims=True)])
    vectors = [[(vec_ref, (slots[q][half], slice(None), pl.ds(2 * block, 16))) for q in range(quarters)]
               for half in range(2)]
    copies = send_halves(idx_ref, vectors, keep_ref, send_ref, sems)
    gh = gh2_ref[...] + norm_back(gn, hat, scale, gain)
    gh_ref[...] = (to_rows(gh, staged_ref) if out_rows else gh).astype(BF16)
    gw_ref[3] = nn(ot_ref[...], gh2_ref[...].astype(BF16)).astype(BF16).reshape(shaped)
    across = n_ref[...].T
    for u, grad in enumerate((gq_ref, gk_ref, gv_ref)):
        gw_ref[u] = nn(across, grad[...]).astype(BF16).reshape(shaped)
    weights = [[(gw_ref.at[half * 2 + u, :, :, q * 128:q * 128 + 128], (slots[q][half], slice(None), pl.ds(u * block, block)))
                for q in range(quarters) for u in range(2)] for half in range(2)]
    copies += send_halves(idx_ref, weights, keep_ref, send_ref, sems, len(copies))
    wait_all(copies)


def place_shards(n, idx_ref, *refs):
    pieces, outs, sems = refs[:n], refs[n:-1], refs[-1]
    moves = Moves(sems)
    for k, piece in enumerate(pieces):
        at = 0
        for out in outs:
            rows = out.shape[1]
            moves.start(piece.at[pl.ds(at, rows), :], out.at[lax.rem(idx_ref[2] + n - k, n)])
            at += rows
    moves.wait()


def add_kernel(jobs, idx_ref, *refs):
    outs = refs[sum(2 * groups * chunks for groups, chunks in jobs):]
    at_in = at_out = 0
    for groups, chunks in jobs:
        at = 0
        for _ in range(chunks):
            for g in range(groups):
                keep, recv = refs[at_in], refs[at_in + 1]
                at_in += 2
                rows = keep.shape[1]
                outs[at_out + g][:, at:at + rows, :] = (keep[...].astype(F32) + recv[...].astype(F32)).astype(BF16)
            at += rows
        at_out += groups


def add_parts(idx, jobs, deps=(), us=0.1):
    sizes = [chunks[0][0].shape[0] // groups for chunks, groups, _ in jobs]
    ordered = [each for (_, _, index), each in zip(jobs, sizes) if index]
    steps = ordered[0] if ordered else min(min(sizes), 4)
    in_specs, out_specs, shapes, args, plan = [], [], [], [], []
    for (chunks, groups, index), each in zip(jobs, sizes):
        lead = each // steps
        total = sum(keep.shape[1] for keep, _ in chunks)
        plan.append((groups, len(chunks)))
        for keep, recv in chunks:
            for g in range(groups):
                if index:
                    where = functools.partial(lambda index, g, i, s: (index(g, i, s), 0, 0), index, g)
                else:
                    where = functools.partial(lambda g, i, s: (i + g * steps, 0, 0), g)
                in_specs += [pl.BlockSpec((lead, keep.shape[1], 128), where)] * 2
                args += [keep, recv]
        out_specs += [pl.BlockSpec((lead, total, 128), lambda i, s: (i, 0, 0))] * groups
        shapes += [jax.ShapeDtypeStruct((each, total, 128), BF16)] * groups
    count = len(args)

    def with_deps(idx_ref, *refs):
        add_kernel(plan, idx_ref, *refs[:count], *refs[count + len(deps):])

    made = pl.pallas_call(
        with_deps,
        grid_spec=pltpu.PrefetchScalarGridSpec(
            num_scalar_prefetch=1, grid=(steps,), in_specs=in_specs + [ANY] * len(deps), out_specs=out_specs),
        out_shape=shapes,
        compiler_params=pltpu.CompilerParams(vmem_limit_bytes=24 * 2**20),
        cost_estimate=pl.CostEstimate(flops=int(us * 1.1e9), bytes_accessed=1024, transcendentals=0),
        name="add_parts",
    )(idx, *args, *deps)
    split, at = [], 0
    for groups, _ in plan:
        split.append(made[at:at + groups])
        at += groups
    return split


def unpack(quarters, starts, idx_ref, *refs):
    outs, held, sems = refs[2 * quarters:-2], refs[-2], refs[-1]
    core, replica = idx_ref[1], idx_ref[0]
    rows = held.shape[2]
    for here in range(2):
        @pl.when(core == here)
        def _():
            for k in range(quarters):
                for half in range(2):
                    source = refs[(1 - here) * quarters + k].at[pl.ds(0 if half == here else rows, rows), :]
                    pltpu.make_async_copy(source, held.at[half, replica ^ k], sems.at[half * quarters + k]).start()
    for k in range(quarters):
        for half in range(2):
            pltpu.make_async_copy(refs[k].at[pl.ds(0, rows), :], held.at[half, k], sems.at[half * quarters + k]).wait()
    down, up, key_conv, value_conv = outs[:4]
    block = up.shape[0]
    feed, conv, proj = starts
    for q in range(quarters):
        cols = slice(q * 128, q * 128 + 128)
        down[:, cols] = held[0, q, feed:feed + 4 * block, :].astype(F32)
        for i in range(4):
            at = q * 512 + i * 128
            up[:, at:at + 128] = held[1, q, feed + i * block:feed + (i + 1) * block, :].astype(F32)
        for t in range(3):
            key_conv[t, :, cols] = held[0, q, conv + t * block:conv + (t + 1) * block, :].astype(F32)
            value_conv[t, :, cols] = held[1, q, conv + t * block:conv + (t + 1) * block, :].astype(F32)
        for u in range(4):
            at = proj + u % 2 * block
            outs[4 + u][:, cols] = held[u // 2, q, at:at + block, :].astype(F32)


def plain(kernel, in_specs, outs, out_specs, scratch, name, us, *args, deps=(), mib=16):
    count = len(args)

    def with_deps(*refs):
        kernel(*refs[:count], *refs[count + len(deps):])

    return pl.pallas_call(
        with_deps,
        out_shape=[jax.ShapeDtypeStruct(s, d) for s, d in outs],
        in_specs=list(in_specs) + [ANY] * len(deps),
        out_specs=out_specs,
        scratch_shapes=scratch,
        compiler_params=pltpu.CompilerParams(vmem_limit_bytes=mib * 2**20),
        cost_estimate=pl.CostEstimate(flops=int(us * 1.1e9), bytes_accessed=1024, transcendentals=0),
        name=name,
    )(*args, *deps)


def geometry(segments, validity, block_len):
    seg = segments.reshape(WIN, 3)
    val = validity.reshape(WIN, 3)
    anchor_seg = seg[:, 2]
    tap = ((seg == anchor_seg[:, None]) & (val == 1)).astype(F32).T.reshape(LEN, 1)
    seg_t = seg.T.reshape(LEN)
    window = jnp.arange(WIN, dtype=jnp.int32)
    position = (window[None, :] * 3 + jnp.arange(3, dtype=jnp.int32)[:, None]).reshape(LEN)
    anchor = window * 3 + 2
    allowed = (anchor[:, None] <= position[None, :]) & (anchor_seg[:, None] == seg_t[None, :])
    allowed = allowed & (val[:, 2][:, None] == 1) & (anchor[:, None] // block_len == position[None, :] // block_len)
    return tap, jnp.where(allowed, 0.0, NEGATIVE).astype(F32)


def tie(value, *others):
    return lax.optimization_barrier((value,) + others)[0]


def swap_cores(value):
    return lax.ppermute(value, "section", [(0, 1), (1, 0)])


def dp_swap(value, step, bits):
    route = []
    for replica in range(2**bits):
        for core in range(2):
            bit = step if core == 0 else bits - 1 - step
            route.append((replica * 2 + core, (replica ^ (1 << bit)) * 2 + core))
    return lax.ppermute(value, ("dp", "section"), route)


def shard_gather(idx, piece, n, deps=(), parts=None):
    parts = parts or [piece.shape[0]]
    if n > 8:
        whole = lax.all_gather(piece, "shard", axis=0)
        return [whole[:, sum(parts[:i]):sum(parts[:i + 1])] for i in range(len(parts))]
    pieces = [piece] + [lax.ppermute(piece, "shard", [(i, (i + k) % n) for i in range(n)]) for k in range(1, n)]
    return plain(functools.partial(place_shards, n), [SMEM] + [ANY] * n, [((n, rows, 128), BF16) for rows in parts],
                 [VMEM] * len(parts), [DMA((n * len(parts),))], "place_shards", 1, idx, *pieces, deps=deps)


def shard_step(value, step, n):
    return lax.ppermute(value, "shard", [(i, i ^ (1 << step)) for i in range(n)])


def shard_order(bits):
    def index(g, i, idx_ref):
        place = i + g * (1 << (bits - 1))
        return sum(((place >> k) & 1) << (bits - 1 - k) for k in range(bits)) ^ idx_ref[2]
    return index


class Sums:
    def __init__(self, keep, recv):
        self.keep, self.recv = keep, recv


class Hops:
    def __init__(self, idx, n, bits):
        self.idx, self.n, self.bits, self.last = idx, n, bits, None

    def run(self, *jobs, beside=(), deps=(), us=0.1):
        n = self.n
        direct = n <= 8
        listed = []
        for chunks, what in jobs:
            pairs = [(c.keep, c.recv) for c in chunks]
            if isinstance(what, tuple):
                listed.append((pairs, 2, shard_order(n.bit_length() - 1) if what[1] == 0 else None))
            elif what == "shard" and direct:
                listed.append((pairs, n, lambda g, i, s: lax.rem(s[2] + g, n)))
            elif what == "shard":
                listed.append((pairs, 2, shard_order(n.bit_length() - 1)))
            else:
                listed.append((pairs, 2, None))
        made = add_parts(self.idx, listed, tuple(deps) + (() if self.last is None else (self.last,)), us)
        self.last = made[0][0]
        results = []
        for (chunks, what), parts in zip(jobs, made):
            if isinstance(what, tuple):
                results.append(Sums(parts[0], shard_step(parts[1], what[1], n)))
            elif what == "shard" and direct:
                got = [lax.ppermute(parts[k], "shard", [(i, (i + k) % n) for i in range(n)]) for k in range(1, n)]
                got = [tie(g, *beside) for g in got] if beside else got
                results.append(sum([parts[0].astype(F32)] + [g.astype(F32) for g in got])[0].astype(BF16))
            elif what == "shard":
                keep, recv = parts[0], shard_step(parts[1], 0, n)
                for step in range(1, n.bit_length() - 1):
                    (keep, send), = add_parts(self.idx, [([(keep, recv)], 2, None)])
                    recv = shard_step(send, step, n)
                results.append((keep[0].astype(F32) + recv[0].astype(F32)).astype(BF16))
            else:
                results.append(Sums(parts[0], dp_swap(parts[1], what, self.bits)))
        return results

    def shard_steps(self, chunks, first=0):
        for step in range(first, self.n.bit_length() - 1):
            chunks, = self.run((chunks if isinstance(chunks, list) else [chunks], ("shard", step)))
        return chunks

    def total(self, sums):
        sums = Sums(tie(sums.keep, self.last), tie(sums.recv, self.last))
        return (sums.keep[0].astype(F32) + sums.recv[0].astype(F32)).astype(BF16)

    def collect(self, total, owner):
        total = tie(total, self.last)
        both = jnp.concatenate([total, lax.ppermute(total, "section", [(1 - owner, owner)])])
        quarters = 2**self.bits
        return [both] + [lax.ppermute(both, ("dp", "section"),
                                      [(2 * i + owner, 2 * (i ^ k) + owner) for i in range(quarters)])
                         for k in range(1, quarters)]


def body(boundary, segment_ids, token_valid, attention_gain, attention_bias, query_weight, key_weight, value_weight,
         key_conv, value_conv, out_weight, feed_gain, feed_bias, up_weight, down_weight):
    core = lax.axis_index("section")
    replica = lax.axis_index("dp")
    first = core == 0
    quarters = lax.axis_size("dp")
    bits = quarters.bit_length() - 1
    n = lax.axis_size("shard")
    block = D // n
    idx = jnp.stack([replica, core, lax.axis_index("shard")]).astype(jnp.int32)

    def quarter(weight, width=128):
        return lax.dynamic_slice_in_dim(weight, replica * width, width, weight.ndim - 1)

    vectors = jnp.stack([attention_gain[0], attention_bias[0], feed_gain[0], feed_bias[0]])
    vectors = jnp.pad(vectors, ((0, 12), (0, 128 - block)))
    key_taps = quarter(key_conv[0]).transpose(1, 0, 2).reshape(3 * block, 128)
    value_taps = quarter(value_conv[0]).transpose(1, 0, 2).reshape(3 * block, 128)
    attn_halves = (jnp.concatenate([quarter(query_weight[0]), quarter(key_weight[0]), key_taps, vectors]),
                   jnp.concatenate([quarter(value_weight[0]), quarter(out_weight[0]), value_taps, vectors]))
    up_part = quarter(up_weight[0], 512).reshape(block, 4, 128).transpose(1, 0, 2).reshape(4 * block, 128)
    feed_halves = (quarter(down_weight[0]), up_part)
    pieces = []
    for halves in (attn_halves, feed_halves):
        kept = jnp.where(first, halves[0], halves[1])
        got = swap_cores(jnp.where(first, halves[1], halves[0]))
        pieces.append((jnp.where(first, kept, got), jnp.where(first, got, kept)))

    own_rows = boundary[0].reshape(2, LEN, D)
    mine = lax.dynamic_index_in_dim(own_rows, core, 0, keepdims=False)
    theirs = swap_cores(lax.dynamic_index_in_dim(own_rows, 1 - core, 0, keepdims=False))
    h = jnp.where(first, mine, theirs)
    cot = jnp.where(first, theirs, mine)
    segments = lax.dynamic_index_in_dim(segment_ids.reshape(2, LEN), core, 0, keepdims=False)
    validity = lax.dynamic_index_in_dim(token_valid.reshape(2, LEN), core, 0, keepdims=False)

    square = (n, block, D)
    saved = []

    def run_attn_fwd(length, h, here, own, other, deps):
        gains = here[:, 5 * block:5 * block + 4, :block].transpose(1, 0, 2).reshape(4, 1, D)
        tap, bias = geometry(segments, validity, length)
        outs = [(ROW, F32), (ROW, BF16), (ROW, BF16), (ROW, BF16), (ROW, BF16), ((WIN, D), BF16), ((WIN, D), BF16),
                ((H, WIN, LEN), BF16), ((D, LEN), BF16), ((7,) + square, BF16), ((3,) + square, BF16)]
        made = plain(
            functools.partial(attn_fwd, len(own), length == BLK), [SMEM] + [VMEM] * 5 + [ANY] * (2 * len(own)), outs,
            [VMEM] * 2 + [ANY] * 9,
            [pltpu.VMEM((10,) + square, BF16)] + [pltpu.VMEM(outs[i][0], BF16) for i in (2, 3, 4, 5, 6, 7, 8)]
            + [pltpu.VMEM(ROW, BF16), pltpu.VMEM((256, 4 * WIN), BF16), pltpu.VMEM((D // 128, LEN, 128), F32), DMA((10 * quarters,)), DMA((10,))],
            "attn_fwd", 13, idx, h, bias, tap, gains[0], gains[1], *own, *other, deps=deps, mib=56)
        return gains, tap, made

    def run_feed_fwd(h2, gains, own, other, at, deps):
        outs = [(ROW, BF16), ((LEN, FF), BF16), ((LEN, FF), BF16), ((n, block, FF), BF16), ((n, 4 * block, D), BF16)]
        y, act, slope, up, down = plain(
            functools.partial(feed_fwd, len(own), at, at > 0), [SMEM] + [VMEM] * 3 + [ANY] * (2 * len(own)), outs,
            [VMEM] + [ANY] * 4, [pltpu.VMEM(outs[i][0], BF16) for i in (3, 4, 1, 2)]
            + [pltpu.VMEM(ROW, BF16), pltpu.VMEM((D // 128, LEN, 128), F32), DMA((5 * quarters,)), DMA((10,))],
            "feed_fwd", 13, idx, h2, gains[2], gains[3], *own, *other, deps=deps, mib=56)
        return y, (act, slope, up.reshape(D, FF), down.reshape(FF, D))

    def spread(piece, last_after=None):
        pieces = [piece]
        for step in reversed(range(bits)):
            final = step == 0 and last_after is not None
            pieces += [dp_swap(tie(held, last_after) if final and at else held, step, bits)
                       for at, held in enumerate(list(pieces))]
        return pieces

    def between(own, after):
        return [swap_cores(held if mark is None else tie(held, mark)) for held, mark in zip(own, after)]

    attn_here, = shard_gather(idx, pieces[0][0], n)
    attn_own = spread(attn_here)
    feed_here, = shard_gather(idx, tie(pieces[1][0], attn_here), n, tuple(attn_own[1:3]))
    feed_own = spread(feed_here)
    attn_other = [swap_cores(held) for held in attn_own]
    next_piece = jnp.concatenate([pieces[0][1], pieces[1][1]])
    next_here, = shard_gather(idx, tie(next_piece, feed_here), n, tuple(attn_own[3:] + feed_own[1:3] + attn_other[:3]))
    gains, tap, made = run_attn_fwd(BLK, h, attn_here, attn_own, attn_other, (next_here,))
    h2 = made[0]
    next_own = spread(next_here, h2)
    feed_other = between(feed_own, [None] * 3 + [h2] * (quarters - 3))
    y, feed = run_feed_fwd(h2, gains, feed_own, feed_other, 0, ())
    saved.append((made[1], h2, gains, tap) + tuple(made[2:]) + feed)
    next_other = between(next_own, [h2] * 3 + [y] * (quarters - 3))
    gains, tap, made = run_attn_fwd(LEN, y, next_here, next_own, next_other, ())
    saved.append((made[1], made[0], gains, tap) + tuple(made[2:]) + (None,) * 4)

    rows_feed, rows_conv, rows_proj = 4 * block + 16, 3 * block, 2 * block + 16

    def halves_of(keep, send):
        recv = swap_cores(send)
        return Sums(keep.reshape((-1,) + keep.shape[2:]), recv.reshape((-1,) + recv.shape[2:]))

    def run_feed_bwd(layer, grad, deps=()):
        h, h2, gains, tap, q, kt, vt, ck, cv, p, ot, w, w_proj, act, slope, up, down = saved[layer]
        shape = (quarters, n, rows_feed, 128)
        gh2, keep, send = plain(
            functools.partial(feed_bwd, layer == 1), [SMEM] + [VMEM] * 4 + [ANY] * 4, [(ROW, F32), (shape, BF16), (shape, BF16)], [VMEM, ANY, ANY],
            [pltpu.VMEM((D, FF), BF16), pltpu.VMEM((FF, D), BF16), pltpu.VMEM((LEN, FF), BF16),
             pltpu.VMEM((LEN, FF), BF16), pltpu.VMEM((LEN, FF), BF16), pltpu.VMEM(ROW, BF16),
             pltpu.VMEM((n, block, FF), BF16), pltpu.VMEM((n, 4 * block, D), BF16), pltpu.VMEM((n, 16, 128), BF16),
             pltpu.VMEM(ROW, BF16), pltpu.VMEM((D // 128, LEN, 128), F32), DMA((4,)), DMA((quarters * 7,))],
            "feed_bwd", 7, idx, grad, h2, gains[2], gains[3], up, down, act, slope, deps=deps, mib=56)
        return gh2, halves_of(keep, send)

    def run_feed_both(h2, gains, grad, own, other, at):
        shape = (quarters, n, rows_feed, 128)
        result, gh2, keep, send = plain(
            functools.partial(feed_both, len(own), at), [SMEM] + [VMEM] * 4 + [ANY] * (2 * len(own)),
            [(ROW, BF16), (ROW, F32), (shape, BF16), (shape, BF16)], [VMEM, VMEM, ANY, ANY],
            [pltpu.VMEM((n, block, FF), BF16), pltpu.VMEM((n, 4 * block, D), BF16)] + [pltpu.VMEM((LEN, FF), BF16)] * 3
            + [pltpu.VMEM(ROW, BF16), pltpu.VMEM((n, block, FF), BF16), pltpu.VMEM((n, 4 * block, D), BF16),
               pltpu.VMEM((n, 16, 128), BF16), pltpu.VMEM(ROW, BF16), pltpu.VMEM((D // 128, LEN, 128), F32),
               DMA((5 * quarters,)), DMA((quarters * 7,))],
            "feed_both", 20, idx, h2, gains[2], gains[3], grad, *own, *other, mib=56)
        return result, gh2, halves_of(keep, send)

    def run_attn_bwd(layer, gh2, deps=()):
        h, h2, gains, tap, q, kt, vt, ck, cv, p, ot, w, w_proj, act, slope, up, down = saved[layer]
        shape = (quarters, n, rows_conv, 128)
        gq, gk, gv, keep, send = plain(
            attn_bwd, [SMEM, VMEM, VMEM] + [ANY] * 4 + [VMEM] * 2 + [ANY],
            [(ROW, BF16)] * 3 + [(shape, BF16), (shape, BF16)], [ANY] * 5,
            [pltpu.VMEM((7,) + square, BF16)] + [pltpu.VMEM(ROW, BF16)] * 3 + [pltpu.VMEM((H, WIN, LEN), BF16)]
            + [pltpu.VMEM(ROW, BF16)] * 4 + [pltpu.VMEM((WIN, D), BF16)] * 2
            + [pltpu.VMEM((6,) + square, BF16), pltpu.VMEM((4 * WIN, LEN), BF16), pltpu.VMEM((256, 4 * WIN), BF16), DMA((7,)), DMA((3,)), DMA((quarters * 6,))],
            "attn_bwd", 7, idx, gh2, tap, w, q, kt, vt, ck, cv, p, deps=deps, mib=50)
        return gq, gk, gv, halves_of(keep, send)

    def run_proj_bwd(layer, gh2, gq, gk, gv, deps=()):
        h, h2, gains, tap, q, kt, vt, ck, cv, p, ot, w, w_proj, act, slope, up, down = saved[layer]
        shape = (quarters, n, rows_proj, 128)
        grad, keep, send = plain(
            functools.partial(proj_bwd, layer == 0), [SMEM] + [VMEM] * 4 + [ANY] + [VMEM] * 3 + [ANY], [(ROW, BF16), (shape, BF16), (shape, BF16)],
            [VMEM, ANY, ANY],
            [pltpu.VMEM((3,) + square, BF16), pltpu.VMEM((D, LEN), BF16), pltpu.VMEM(ROW, BF16),
             pltpu.VMEM((4,) + square, BF16), pltpu.VMEM((n, 16, 128), BF16), pltpu.VMEM((D // 128, LEN, 128), F32), DMA((3,)), DMA((quarters * 6,))],
            "proj_bwd", 6, idx, gh2, h, gains[0], gains[1], w_proj, gq, gk, gv, ot, deps=deps, mib=50)
        return grad, halves_of(keep, send)

    hops = Hops(idx, n, bits)
    result, gh2, feed_two = run_feed_both(saved[1][1], saved[1][2], cot, next_own, next_other, 5 * block + 16)
    gq, gk, gv, conv_two = run_attn_bwd(1, gh2)
    hops.last = gq
    feed_two, = hops.run(([feed_two], 0))
    grad, proj_two = run_proj_bwd(1, gh2, gq, gk, gv, deps=(hops.last,))
    hops.last = grad
    conv_two, = hops.run(([conv_two], 0))
    gh2, feed_one = run_feed_bwd(0, grad, deps=(hops.last,))
    hops.last = gh2
    feed_two, conv_two = hops.run(([feed_two], 1), ([conv_two], 1), us=24)
    mixed, = hops.run(([feed_one, proj_two], 0))
    gq, gk, gv, conv_one = run_attn_bwd(0, gh2, deps=(hops.last,))
    hops.last = gq
    grad, proj_one = run_proj_bwd(0, gh2, gq, gk, gv)
    hops.last = grad
    two, mixed = hops.run(([feed_two, conv_two], ("shard", 0)), ([mixed], 1), us=12)
    attn_one, = hops.run(([conv_one, proj_one], 0))
    two, = hops.run(([two], ("shard", 1)))
    mixed, = hops.run(([mixed], ("shard", 0)), deps=(two.recv,))
    attn_one, = hops.run(([attn_one], 1))
    mark = hops.last
    mixed, = hops.run(([mixed], ("shard", 1)))
    attn_one, = hops.run(([attn_one], "shard"))
    two, mixed = [hops.total(hops.shard_steps(x, 2)) for x in (two, mixed)]
    two_all = hops.collect(jnp.concatenate([two, mixed[rows_feed:]]), 1)
    one_all = hops.collect(jnp.concatenate([mixed[:rows_feed], tie(attn_one, *two_all[1:])]), 0)

    result, grad = tie(result, mark), tie(grad, mark)
    other = swap_cores(jnp.where(first, result, grad))
    ours = jnp.where(first, grad, result)
    section_ends = jnp.stack([jnp.where(first, ours, other), jnp.where(first, other, ours)]).reshape(1, 2 * LEN, D)
    total = rows_feed + rows_conv + rows_proj
    shapes = [(4 * block, D), (block, FF), (3, block, D), (3, block, D)] + [(block, D)] * 4
    gdown, gup, gkc, gvc, gq, gk, gv, go = plain(
        functools.partial(unpack, quarters, (0, rows_feed, rows_feed + rows_conv)), [SMEM] + [ANY] * (2 * quarters),
        [(shape, F32) for shape in shapes], [VMEM] * 8,
        [pltpu.VMEM((2, quarters, total, 128), BF16), DMA((2 * quarters,))], "unpack", 4,
        idx, *two_all, *one_all, mib=20)

    def vectors_of(one, two):
        return jnp.where(first, one[:2, :block], two[:2, :block]).astype(F32)

    vec_feed = vectors_of(one_all[0][4 * block:], two_all[0][4 * block:])
    vec_attn = vectors_of(one_all[0][rows_feed + rows_conv + 2 * block:], two_all[0][rows_feed + rows_conv + 2 * block:])
    return (section_ends, vec_attn[0:1], vec_attn[1:2], gq[None], gk[None], gv[None], gkc.transpose(1, 0, 2)[None],
            gvc.transpose(1, 0, 2)[None], go[None], vec_feed[0:1], vec_feed[1:2], gup[None], gdown[None])


def solution(mesh):
    vector, matrix, conv = P("section", "shard"), P("section", "shard", None), P("section", "shard", None, None)
    rows, tokens = P("section", ("dp", "shard"), None), P(("dp", "shard"))
    weights = (vector, vector, matrix, matrix, matrix, conv, conv, matrix, vector, vector, matrix, matrix)
    return jax.shard_map(body, mesh=mesh, in_specs=(rows, tokens, tokens) + weights, out_specs=(rows,) + weights,
                         check_vma=False)
```

```python
import functools

import jax
import jax.numpy as jnp
from jax import lax
from jax.experimental import pallas as pl
from jax.experimental.pallas import tpu as pltpu
from jax.sharding import PartitionSpec as P

D = 512
H = 8
HD = 64
FF = 2048
BLK = 256
LEN = 768
WIN = LEN // 3
EPSILON = 1e-05
NEGATIVE = -1e30
F32 = jnp.float32
BF16 = jnp.bfloat16
LOG2E = 1.4426950408889634
VMEM = pl.BlockSpec(memory_space=pltpu.VMEM)
ANY = pl.BlockSpec(memory_space=pl.ANY)
SMEM = pl.BlockSpec(memory_space=pltpu.SMEM)
DMA = pltpu.SemaphoreType.DMA
ROW = (LEN, D)
Q, K, V, O, KC, VC = 0, 1, 2, 3, 4, 7
HALVES = (Q, K, KC, KC + 1, KC + 2), (V, O, VC, VC + 1, VC + 2)


def nn(a, b):
    return lax.dot_general(a, b, (((1,), (0,)), ((), ())), preferred_element_type=F32)


def nt(a, b):
    return lax.dot_general(a, b, (((1,), (1,)), ((), ())), preferred_element_type=F32)


def tn(a, b):
    return lax.dot_general(a, b, (((0,), (0,)), ((), ())), preferred_element_type=F32)


def norm_parts(hidden):
    centred = hidden - jnp.mean(hidden, axis=-1, keepdims=True)
    spread = jnp.mean(centred * centred, axis=-1, keepdims=True)
    scale = lax.rsqrt(spread + EPSILON)
    return centred * scale, scale


def norm_back(grad, hat, scale, gain):
    inner = grad * gain
    mean_one = jnp.mean(inner, axis=-1, keepdims=True)
    mean_two = jnp.mean(inner * hat, axis=-1, keepdims=True)
    return scale * (inner - mean_one - hat * mean_two)


def gelu_both(z):
    phi = 0.5 + 0.5 * lax.erf(z * 0.7071067811865476)
    density = jnp.exp2(z * z * (-0.5 * LOG2E)) * 0.3989422804014327
    return z * phi, phi + z * density


def head_mask(rows):
    lane = lax.broadcasted_iota(jnp.int32, (rows, 256), 1) // HD
    return [lane == i for i in range(4)]


def relative(index, core, bits):
    return sum(((index >> k) & 1) << (bits - 1 - k) for k in range(bits)) if core == 0 else index


def to_taps(rows, staged_ref):
    for c in range(D // 128):
        staged_ref[c] = rows[:, c * 128:c * 128 + 128].astype(F32)
    return [jnp.concatenate([staged_ref[c, pl.ds(t, WIN, stride=3), :] for c in range(D // 128)], axis=1)
            for t in range(3)]


def to_rows(value, staged_ref):
    for c in range(D // 128):
        for t in range(3):
            staged_ref[c, pl.ds(t, WIN, stride=3), :] = value[t * WIN:(t + 1) * WIN, c * 128:c * 128 + 128]
    return jnp.concatenate([staged_ref[c] for c in range(D // 128)], axis=1)


class Moves:
    def __init__(self, sems):
        self.sems, self.items = sems, []

    def start(self, src, dst):
        copy = pltpu.make_async_copy(src, dst, self.sems.at[len(self.items)])
        copy.start()
        self.items.append(copy)
        return copy

    def wait(self):
        for copy in self.items:
            copy.wait()


def fetch_pieces(idx_ref, own, other, units, sems):
    core, replica = idx_ref[1], idx_ref[0]
    ordered = len(own) == 1
    quarters = own[0].shape[0] if ordered else len(own)
    bits = quarters.bit_length() - 1
    for here in range(2):
        made = []
        for half in range(2):
            side = own if half == here else other
            for m in range(quarters):
                piece = side[0].at[m] if ordered else side[m]
                made += units(half, piece, m if ordered else replica ^ relative(m, half, bits))

        @pl.when(core == here)
        def _():
            for i, (src, dst) in enumerate(made):
                pltpu.make_async_copy(src, dst, sems.at[i]).start()
    return [pltpu.make_async_copy(src, dst, sems.at[i]) for i, (src, dst) in enumerate(made)]


def send_halves(idx_ref, halves, keep_ref, send_ref, sems, base=0):
    core = idx_ref[1]
    for here in range(2):
        @pl.when(core == here)
        def _():
            i = base
            for half in range(2):
                for src, dst in halves[half]:
                    out = keep_ref if here == half else send_ref
                    pltpu.make_async_copy(src, out.at[dst], sems.at[i]).start()
                    i += 1
    items = halves[0] + halves[1]
    return [pltpu.make_async_copy(src, keep_ref.at[dst], sems.at[base + i]) for i, (src, dst) in enumerate(items)]


def fill_vectors(vec_ref, rows):
    vec_ref[...] = jnp.zeros_like(vec_ref)
    parts, block = vec_ref.shape[0], D // vec_ref.shape[0]
    for z in range(parts):
        for i, row in enumerate(rows):
            vec_ref[z, i:i + 1, :block] = row[:, z * block:(z + 1) * block].astype(BF16)


def wait_all(copies):
    for copy in copies:
        copy.wait()


def attn_fwd(count, in_rows, idx_ref, h_in, bias_ref, tap_ref, gain_ref, shift_ref, *refs):
    own, other = refs[:count], refs[count:2 * count]
    (h2_ref, h_ref, q_out, kt_out, vt_out, ck_out, cv_out, p_out, ot_out, w_out, proj_out,
     w_ref, q_ref, kt_ref, vt_ref, ck_ref, cv_ref, p_ref, ot_ref, n_ref, across_ref, staged_ref, in_sems, out_sems) = refs[2 * count:]
    block = w_ref.shape[2]

    def units(half, piece, quarter):
        cols = pl.ds(pl.multiple_of(quarter * 128, 128), 128)
        return [(piece.at[:, pl.ds(u * block, block), :], w_ref.at[place, :, :, cols])
                for u, place in enumerate(HALVES[half])]

    fetched = fetch_pieces(idx_ref, own, other, units, in_sems)
    out = Moves(out_sems)

    def weight(u):
        return w_ref[u].reshape(D, D)

    for t, rows in enumerate(to_taps(h_in[...], staged_ref) if in_rows else []):
        h_ref[t * WIN:(t + 1) * WIN, :] = rows.astype(BF16)
    if not in_rows:
        h_ref[...] = h_in[...]
    hat, _s = norm_parts(h_ref[...].astype(F32))
    n_ref[...] = (hat * gain_ref[...].astype(F32) + shift_ref[...].astype(F32)).astype(BF16)
    wait_all(fetched)
    out.start(w_ref.at[pl.ds(O, 7)], w_out)
    out.start(w_ref.at[pl.ds(Q, 3)], proj_out)
    tap = tap_ref[...]
    kt_ref[...] = (nn(n_ref[...], weight(K)) * tap).astype(BF16)
    vt_ref[...] = (nn(n_ref[...], weight(V)) * tap).astype(BF16)
    q_ref[...] = nn(n_ref[...], weight(Q)).astype(BF16)
    out.start(q_ref, q_out)
    out.start(kt_ref, kt_out)
    out.start(vt_ref, vt_out)
    ck_ref[...] = sum(nn(kt_ref[t * WIN:(t + 1) * WIN, :], weight(KC + t)) for t in range(3)).astype(BF16)
    cv_ref[...] = sum(nn(vt_ref[t * WIN:(t + 1) * WIN, :], weight(VC + t)) for t in range(3)).astype(BF16)
    out.start(ck_ref, ck_out)
    out.start(cv_ref, cv_out)
    masks = head_mask(WIN)
    zero = jnp.zeros((WIN, 256), BF16)
    for g in range(2):
        cols = slice(g * 256, g * 256 + 256)
        for i in range(4):
            across_ref[:, i * WIN:i * WIN + WIN] = jnp.where(masks[i], cv_ref[:, cols], zero).T
        for i in range(4):
            s = nt(jnp.where(masks[i], ck_ref[:, cols], zero), q_ref[:, cols]) * (0.125 * LOG2E) + bias_ref[...]
            top = jnp.maximum(jnp.max(s, axis=0, keepdims=True), 0.0)
            num = jnp.exp2(s - top)
            den = jnp.exp2(-top) + jnp.sum(num, axis=0, keepdims=True)
            p_ref[g * 4 + i] = (num * (1.0 / den)).astype(BF16)
        heads = pl.ds(g * 4, 4)
        out.start(p_ref.at[heads], p_out.at[heads])
        ot_ref[cols, :] = nn(across_ref[...], p_ref[heads].reshape(4 * WIN, LEN)).astype(BF16)
    out.start(ot_ref, ot_out)
    h2_ref[...] = h_ref[...].astype(F32) + tn(ot_ref[...], weight(O))
    out.wait()


def feed_fwd(count, at, out_rows, idx_ref, h2_ref, gain_ref, shift_ref, *refs):
    own, other = refs[:count], refs[count:2 * count]
    (y_ref, a_out, gd_out, wu_out, wd_out, wu_ref, wd_ref, a_ref, gd_ref, n_ref, staged_ref, in_sems, out_sems) = refs[2 * count:]
    block = wu_ref.shape[1]

    def units(half, piece, quarter):
        if half == 0:
            return [(piece.at[:, pl.ds(at, 4 * block), :], wd_ref.at[:, :, pl.ds(pl.multiple_of(quarter * 128, 128), 128)])]
        return [(piece.at[:, pl.ds(at + i * block, block), :],
                 wu_ref.at[:, :, pl.ds(pl.multiple_of(quarter * 512 + i * 128, 128), 128)]) for i in range(4)]

    fetched = fetch_pieces(idx_ref, own, other, units, in_sems)
    hat, _s = norm_parts(h2_ref[...])
    n_ref[...] = (hat * gain_ref[...].astype(F32) + shift_ref[...].astype(F32)).astype(BF16)
    wait_all(fetched)
    out = Moves(out_sems)
    out.start(wu_ref, wu_out)
    out.start(wd_ref, wd_out)
    chunks = [slice(c * 512, c * 512 + 512) for c in range(4)]

    def up(c):
        return nn(n_ref[...], wu_ref[:, :, chunks[c]].reshape(D, 512))

    total = h2_ref[...]
    z = up(0)
    for c in range(4):
        later = up(c + 1) if c < 3 else None
        act, slope = gelu_both(z)
        act = act.astype(BF16)
        a_ref[:, chunks[c]] = act
        gd_ref[:, chunks[c]] = slope.astype(BF16)
        out.start(a_ref.at[:, chunks[c]], a_out.at[:, chunks[c]])
        out.start(gd_ref.at[:, chunks[c]], gd_out.at[:, chunks[c]])
        total = total + nn(act, wd_ref[...].reshape(FF, D)[chunks[c], :])
        z = later
    y_ref[...] = (to_rows(total, staged_ref) if out_rows else total).astype(BF16)
    out.wait()


def feed_back(idx_ref, gout_ref, h2_ref, gain_ref, wu, wd, a_ref, gd_ref, gh2_ref, keep_ref, send_ref, gz_ref,
              n_ref, gwu_ref, gwd_ref, vec_ref, sems, arrived):
    parts, quarters = gwu_ref.shape[0], keep_ref.shape[0]
    block = D // parts
    bits = quarters.bit_length() - 1
    wide = FF // quarters
    arrived(slice(0, 1))
    gwd_ref[...] = tn(a_ref[...], gout_ref[...]).astype(BF16).reshape(parts, 4 * block, D)
    slots = [[relative(q ^ idx_ref[0], half, bits) for half in range(2)] for q in range(quarters)]
    down = [(gwd_ref.at[:, :, q * 128:q * 128 + 128], (slots[q][0], slice(None), pl.ds(0, 4 * block)))
            for q in range(quarters)]
    copies = send_halves(idx_ref, (down, []), keep_ref, send_ref, sems)
    arrived(slice(1, 3))
    for c in range(4):
        cols = slice(c * 512, c * 512 + 512)
        gz_ref[:, cols] = (nt(gout_ref[...], wd[cols, :]) * gd_ref[:, cols].astype(F32)).astype(BF16)
    arrived(slice(3, 4))
    gwu_ref[...] = tn(n_ref[...], gz_ref[...]).astype(BF16).reshape(parts, block, FF)
    up = [(gwu_ref.at[:, :, q * wide + i * 128:q * wide + i * 128 + 128],
           (slots[q][1], slice(None), pl.ds(i * block, block))) for q in range(quarters) for i in range(wide // 128)]
    copies += send_halves(idx_ref, ([], up), keep_ref, send_ref, sems, len(copies))
    gn = nt(gz_ref[...], wu[...])
    hat, scale = norm_parts(h2_ref[...])
    fill_vectors(vec_ref, [jnp.sum(gn * hat, axis=0, keepdims=True), jnp.sum(gn, axis=0, keepdims=True)])
    vectors = [[(vec_ref, (slots[q][half], slice(None), pl.ds(4 * block, 16))) for q in range(quarters)]
               for half in range(2)]
    copies += send_halves(idx_ref, vectors, keep_ref, send_ref, sems, len(copies))
    gh2_ref[...] = gout_ref[...].astype(F32) + norm_back(gn, hat, scale, gain_ref[...].astype(F32))
    wait_all(copies)


def feed_both(count, at, idx_ref, h2_ref, gain_ref, shift_ref, gout_in, *refs):
    own, other = refs[:count], refs[count:2 * count]
    (y_ref, gh2_ref, keep_ref, send_ref, wu_ref, wd_ref, a_ref, gd_ref, gz_ref, n_ref, gwu_ref, gwd_ref, vec_ref,
     gout_ref, staged_ref, in_sems, sems) = refs[2 * count:]
    block = wu_ref.shape[1]

    def units(half, piece, quarter):
        if half == 0:
            return [(piece.at[:, pl.ds(at, 4 * block), :], wd_ref.at[:, :, pl.ds(pl.multiple_of(quarter * 128, 128), 128)])]
        return [(piece.at[:, pl.ds(at + i * block, block), :],
                 wu_ref.at[:, :, pl.ds(pl.multiple_of(quarter * 512 + i * 128, 128), 128)]) for i in range(4)]

    fetched = fetch_pieces(idx_ref, own, other, units, in_sems)
    for t, rows in enumerate(to_taps(gout_in[...], staged_ref)):
        gout_ref[t * WIN:(t + 1) * WIN, :] = rows.astype(BF16)
    hat, _s = norm_parts(h2_ref[...])
    n_ref[...] = (hat * gain_ref[...].astype(F32) + shift_ref[...].astype(F32)).astype(BF16)
    wait_all(fetched)
    chunks = [slice(c * 512, c * 512 + 512) for c in range(4)]

    def up(c):
        return nn(n_ref[...], wu_ref[:, :, chunks[c]].reshape(D, 512))

    total = h2_ref[...]
    z = up(0)
    for c in range(4):
        later = up(c + 1) if c < 3 else None
        act, slope = gelu_both(z)
        act = act.astype(BF16)
        a_ref[:, chunks[c]] = act
        gd_ref[:, chunks[c]] = slope.astype(BF16)
        total = total + nn(act, wd_ref[...].reshape(FF, D)[chunks[c], :])
        z = later
    y_ref[...] = to_rows(total, staged_ref).astype(BF16)
    feed_back(idx_ref, gout_ref, h2_ref, gain_ref, wu_ref[...].reshape(D, FF), wd_ref[...].reshape(FF, D), a_ref, gd_ref,
              gh2_ref, keep_ref, send_ref, gz_ref, n_ref, gwu_ref, gwd_ref, vec_ref, sems, lambda step: None)


def feed_bwd(in_rows, idx_ref, gout_in, h2_ref, gain_ref, shift_ref, wu_in, wd_in, a_in, gd_in,
             gh2_ref, keep_ref, send_ref, wu_ref, wd_ref, a_ref, gd_ref, gz_ref, n_ref, gwu_ref, gwd_ref, vec_ref,
             gout_ref, staged_ref, in_sems, sems):
    arriving = Moves(in_sems)
    for src, dst in ((a_in, a_ref), (wd_in, wd_ref), (gd_in, gd_ref), (wu_in, wu_ref)):
        arriving.start(src, dst)
    for t, rows in enumerate(to_taps(gout_in[...], staged_ref) if in_rows else []):
        gout_ref[t * WIN:(t + 1) * WIN, :] = rows.astype(BF16)
    if not in_rows:
        gout_ref[...] = gout_in[...]
    hat, scale = norm_parts(h2_ref[...])
    n_ref[...] = (hat * gain_ref[...].astype(F32) + shift_ref[...].astype(F32)).astype(BF16)
    feed_back(idx_ref, gout_ref, h2_ref, gain_ref, wu_ref, wd_ref, a_ref, gd_ref, gh2_ref, keep_ref, send_ref, gz_ref,
              n_ref, gwu_ref, gwd_ref, vec_ref, sems, lambda step: wait_all(arriving.items[step]))


def attn_bwd(idx_ref, gh2_ref, tap_ref, w_in, q_in, kt_in, vt_in, ck_ref, cv_ref, p_in,
             gq_out, gk_out, gv_out, keep_ref, send_ref,
             w_ref, q_ref, kt_ref, vt_ref, p_ref, go_ref, gq_ref, gk_ref, gv_ref, gck_ref, gcv_ref, gw_ref, gs_ref, across_ref,
             in_sems, out_sems, sems):
    arriving = Moves(in_sems)
    arriving.start(w_in.at[pl.ds(0, 1)], w_ref.at[pl.ds(6, 1)])
    arriving.start(q_in, q_ref)
    arriving.start(p_in, p_ref)
    arriving.start(w_in.at[pl.ds(1, 3)], w_ref.at[pl.ds(0, 3)])
    arriving.start(w_in.at[pl.ds(4, 3)], w_ref.at[pl.ds(3, 3)])
    arriving.start(kt_in, kt_ref)
    arriving.start(vt_in, vt_ref)
    out = Moves(out_sems)
    parts, quarters = gw_ref.shape[1], keep_ref.shape[0]
    block = D // parts
    shaped = (parts, block, D)
    wait_all(arriving.items[:1])
    go_ref[...] = nt(gh2_ref[...].astype(BF16), w_ref[6].reshape(D, D)).astype(BF16)
    masks = head_mask(WIN)
    zero = jnp.zeros((WIN, 256), BF16)
    wait_all(arriving.items[1:3])

    def own_lanes(stacked):
        return sum(jnp.where(masks[i], stacked[i * WIN:(i + 1) * WIN, :], 0.0) for i in range(4))

    for g in range(2):
        cols = slice(g * 256, g * 256 + 256)
        for i in range(4):
            across_ref[:, i * WIN:i * WIN + WIN] = jnp.where(masks[i], ck_ref[:, cols], zero).T
        for i in range(4):
            gp = nt(jnp.where(masks[i], cv_ref[:, cols], zero), go_ref[:, cols])
            p = p_ref[g * 4 + i].astype(F32)
            pg = p * gp
            gs_ref[i * WIN:i * WIN + WIN, :] = (pg - p * jnp.sum(pg, axis=0, keepdims=True)).astype(BF16)
        stacked = p_ref[pl.ds(g * 4, 4)].reshape(4 * WIN, LEN)
        gcv_ref[:, cols] = own_lanes(nn(stacked, go_ref[:, cols])).astype(BF16)
        gck_ref[:, cols] = (own_lanes(nn(gs_ref[...], q_ref[:, cols])) * 0.125).astype(BF16)
        gq_ref[:, cols] = (nn(across_ref[...], gs_ref[...]) * 0.125).astype(BF16).T

    out.start(gq_ref, gq_out)
    gck, gcv = gck_ref[...], gcv_ref[...]
    wait_all(arriving.items[3:])
    for t in range(3):
        rows = slice(t * WIN, t * WIN + WIN)
        gw_ref[t] = tn(kt_ref[rows, :], gck).astype(BF16).reshape(shaped)
        gw_ref[3 + t] = tn(vt_ref[rows, :], gcv).astype(BF16).reshape(shaped)

    halves = [], []
    bits = quarters.bit_length() - 1
    for q in range(quarters):
        for half in range(2):
            slot = relative(q ^ idx_ref[0], half, bits)
            for u in range(3):
                halves[half].append((gw_ref.at[half * 3 + u, :, :, q * 128:q * 128 + 128],
                                     (slot, slice(None), pl.ds(u * block, block))))
    copies = send_halves(idx_ref, halves, keep_ref, send_ref, sems)
    for t in range(3):
        rows = slice(t * WIN, t * WIN + WIN)
        tap = tap_ref[rows, :]
        gk_ref[rows, :] = (nt(gck, w_ref[t].reshape(D, D)) * tap).astype(BF16)
        gv_ref[rows, :] = (nt(gcv, w_ref[3 + t].reshape(D, D)) * tap).astype(BF16)
    out.start(gk_ref, gk_out)
    out.start(gv_ref, gv_out)
    wait_all(copies)
    out.wait()


def proj_bwd(out_rows, idx_ref, gh2_ref, h_ref, gain_ref, shift_ref, w_in, gq_ref, gk_ref, gv_ref, ot_in,
             gh_ref, keep_ref, send_ref, w_ref, ot_ref, n_ref, gw_ref, vec_ref, staged_ref, in_sems, sems):
    arriving = Moves(in_sems)
    arriving.start(w_in, w_ref)
    arriving.start(ot_in, ot_ref)
    gain = gain_ref[...].astype(F32)
    parts, quarters = gw_ref.shape[1], keep_ref.shape[0]
    block = D // parts
    shaped = (parts, block, D)
    bits = quarters.bit_length() - 1
    slots = [[relative(q ^ idx_ref[0], half, bits) for half in range(2)] for q in range(quarters)]
    hat, scale = norm_parts(h_ref[...].astype(F32))
    n_ref[...] = (hat * gain + shift_ref[...].astype(F32)).astype(BF16)
    arriving.wait()
    gn = (nt(gq_ref[...], w_ref[0].reshape(D, D)) + nt(gk_ref[...], w_ref[1].reshape(D, D))
          + nt(gv_ref[...], w_ref[2].reshape(D, D)))
    fill_vectors(vec_ref, [jnp.sum(gn * hat, axis=0, keepdims=True), jnp.sum(gn, axis=0, keepdims=True)])
    vectors = [[(vec_ref, (slots[q][half], slice(None), pl.ds(2 * block, 16))) for q in range(quarters)]
               for half in range(2)]
    copies = send_halves(idx_ref, vectors, keep_ref, send_ref, sems)
    gh = gh2_ref[...] + norm_back(gn, hat, scale, gain)
    gh_ref[...] = (to_rows(gh, staged_ref) if out_rows else gh).astype(BF16)
    gw_ref[3] = nn(ot_ref[...], gh2_ref[...].astype(BF16)).astype(BF16).reshape(shaped)
    across = n_ref[...].T
    for u, grad in enumerate((gq_ref, gk_ref, gv_ref)):
        gw_ref[u] = nn(across, grad[...]).astype(BF16).reshape(shaped)
    weights = [[(gw_ref.at[half * 2 + u, :, :, q * 128:q * 128 + 128], (slots[q][half], slice(None), pl.ds(u * block, block)))
                for q in range(quarters) for u in range(2)] for half in range(2)]
    copies += send_halves(idx_ref, weights, keep_ref, send_ref, sems, len(copies))
    wait_all(copies)


def place_shards(n, idx_ref, *refs):
    pieces, outs, sems = refs[:n], refs[n:-1], refs[-1]
    moves = Moves(sems)
    for k, piece in enumerate(pieces):
        at = 0
        for out in outs:
            rows = out.shape[1]
            moves.start(piece.at[pl.ds(at, rows), :], out.at[lax.rem(idx_ref[2] + n - k, n)])
            at += rows
    moves.wait()


def add_kernel(jobs, idx_ref, *refs):
    outs = refs[sum(2 * groups * chunks for groups, chunks in jobs):]
    at_in = at_out = 0
    for groups, chunks in jobs:
        at = 0
        for _ in range(chunks):
            for g in range(groups):
                keep, recv = refs[at_in], refs[at_in + 1]
                at_in += 2
                rows = keep.shape[1]
                outs[at_out + g][:, at:at + rows, :] = (keep[...].astype(F32) + recv[...].astype(F32)).astype(BF16)
            at += rows
        at_out += groups


def add_parts(idx, jobs, deps=(), us=0.1):
    sizes = [chunks[0][0].shape[0] // groups for chunks, groups, _ in jobs]
    ordered = [each for (_, _, index), each in zip(jobs, sizes) if index]
    steps = ordered[0] if ordered else min(min(sizes), 4)
    in_specs, out_specs, shapes, args, plan = [], [], [], [], []
    for (chunks, groups, index), each in zip(jobs, sizes):
        lead = each // steps
        total = sum(keep.shape[1] for keep, _ in chunks)
        plan.append((groups, len(chunks)))
        for keep, recv in chunks:
            for g in range(groups):
                if index:
                    where = functools.partial(lambda index, g, i, s: (index(g, i, s), 0, 0), index, g)
                else:
                    where = functools.partial(lambda g, i, s: (i + g * steps, 0, 0), g)
                in_specs += [pl.BlockSpec((lead, keep.shape[1], 128), where)] * 2
                args += [keep, recv]
        out_specs += [pl.BlockSpec((lead, total, 128), lambda i, s: (i, 0, 0))] * groups
        shapes += [jax.ShapeDtypeStruct((each, total, 128), BF16)] * groups
    count = len(args)

    def with_deps(idx_ref, *refs):
        add_kernel(plan, idx_ref, *refs[:count], *refs[count + len(deps):])

    made = pl.pallas_call(
        with_deps,
        grid_spec=pltpu.PrefetchScalarGridSpec(
            num_scalar_prefetch=1, grid=(steps,), in_specs=in_specs + [ANY] * len(deps), out_specs=out_specs),
        out_shape=shapes,
        compiler_params=pltpu.CompilerParams(vmem_limit_bytes=24 * 2**20),
        cost_estimate=pl.CostEstimate(flops=int(us * 1.1e9), bytes_accessed=1024, transcendentals=0),
        name="add_parts",
    )(idx, *args, *deps)
    split, at = [], 0
    for groups, _ in plan:
        split.append(made[at:at + groups])
        at += groups
    return split


def unpack(quarters, starts, idx_ref, *refs):
    outs, held, sems = refs[3 * quarters:-2], refs[-2], refs[-1]
    core, replica = idx_ref[1], idx_ref[0]
    rows = held.shape[2]
    for here in range(2):
        @pl.when(core == here)
        def _():
            for k in range(quarters):
                for half in range(2):
                    side = 0 if half == here else 1
                    source = refs[k].at[pl.ds(side * rows, rows), :] if here == 1 else refs[(1 + side) * quarters + k]
                    pltpu.make_async_copy(source, held.at[half, replica ^ k], sems.at[half * quarters + k]).start()
    for k in range(quarters):
        for half in range(2):
            pltpu.make_async_copy(refs[k].at[pl.ds(0, rows), :], held.at[half, k], sems.at[half * quarters + k]).wait()
    down, up, key_conv, value_conv = outs[:4]
    block = up.shape[0]
    feed, conv, proj = starts
    for q in range(quarters):
        cols = slice(q * 128, q * 128 + 128)
        down[:, cols] = held[0, q, feed:feed + 4 * block, :].astype(F32)
        for i in range(4):
            at = q * 512 + i * 128
            up[:, at:at + 128] = held[1, q, feed + i * block:feed + (i + 1) * block, :].astype(F32)
        for t in range(3):
            key_conv[t, :, cols] = held[0, q, conv + t * block:conv + (t + 1) * block, :].astype(F32)
            value_conv[t, :, cols] = held[1, q, conv + t * block:conv + (t + 1) * block, :].astype(F32)
        for u in range(4):
            at = proj + u % 2 * block
            outs[4 + u][:, cols] = held[u // 2, q, at:at + block, :].astype(F32)


def plain(kernel, in_specs, outs, out_specs, scratch, name, us, *args, deps=(), mib=16):
    count = len(args)

    def with_deps(*refs):
        kernel(*refs[:count], *refs[count + len(deps):])

    return pl.pallas_call(
        with_deps,
        out_shape=[jax.ShapeDtypeStruct(s, d) for s, d in outs],
        in_specs=list(in_specs) + [ANY] * len(deps),
        out_specs=out_specs,
        scratch_shapes=scratch,
        compiler_params=pltpu.CompilerParams(vmem_limit_bytes=mib * 2**20),
        cost_estimate=pl.CostEstimate(flops=int(us * 1.1e9), bytes_accessed=1024, transcendentals=0),
        name=name,
    )(*args, *deps)


def geometry(segments, validity, block_len):
    seg = segments.reshape(WIN, 3)
    val = validity.reshape(WIN, 3)
    anchor_seg = seg[:, 2]
    tap = ((seg == anchor_seg[:, None]) & (val == 1)).astype(F32).T.reshape(LEN, 1)
    seg_t = seg.T.reshape(LEN)
    window = jnp.arange(WIN, dtype=jnp.int32)
    position = (window[None, :] * 3 + jnp.arange(3, dtype=jnp.int32)[:, None]).reshape(LEN)
    anchor = window * 3 + 2
    allowed = (anchor[:, None] <= position[None, :]) & (anchor_seg[:, None] == seg_t[None, :])
    allowed = allowed & (val[:, 2][:, None] == 1) & (anchor[:, None] // block_len == position[None, :] // block_len)
    return tap, jnp.where(allowed, 0.0, NEGATIVE).astype(F32)


def tie(value, *others):
    return lax.optimization_barrier((value,) + others)[0]


def swap_cores(value):
    return lax.ppermute(value, "section", [(0, 1), (1, 0)])


def dp_swap(value, step, bits):
    route = []
    for replica in range(2**bits):
        for core in range(2):
            bit = step if core == 0 else bits - 1 - step
            route.append((replica * 2 + core, (replica ^ (1 << bit)) * 2 + core))
    return lax.ppermute(value, ("dp", "section"), route)


def shard_gather(idx, piece, n, deps=(), parts=None):
    parts = parts or [piece.shape[0]]
    if n > 8:
        whole = lax.all_gather(piece, "shard", axis=0)
        return [whole[:, sum(parts[:i]):sum(parts[:i + 1])] for i in range(len(parts))]
    pieces = [piece] + [lax.ppermute(piece, "shard", [(i, (i + k) % n) for i in range(n)]) for k in range(1, n)]
    return plain(functools.partial(place_shards, n), [SMEM] + [ANY] * n, [((n, rows, 128), BF16) for rows in parts],
                 [VMEM] * len(parts), [DMA((n * len(parts),))], "place_shards", 1, idx, *pieces, deps=deps)


def shard_step(value, step, n):
    return lax.ppermute(value, "shard", [(i, i ^ (1 << step)) for i in range(n)])


def shard_order(bits):
    def index(g, i, idx_ref):
        place = i + g * (1 << (bits - 1))
        return sum(((place >> k) & 1) << (bits - 1 - k) for k in range(bits)) ^ idx_ref[2]
    return index


class Sums:
    def __init__(self, keep, recv):
        self.keep, self.recv = keep, recv


class Hops:
    def __init__(self, idx, n, bits):
        self.idx, self.n, self.bits, self.last = idx, n, bits, None

    def run(self, *jobs, beside=(), deps=(), us=0.1):
        n = self.n
        direct = n <= 8
        listed = []
        for chunks, what in jobs:
            pairs = [(c.keep, c.recv) for c in chunks]
            if isinstance(what, tuple):
                listed.append((pairs, 2, shard_order(n.bit_length() - 1) if what[1] == 0 else None))
            elif what == "shard" and direct:
                listed.append((pairs, n, lambda g, i, s: lax.rem(s[2] + g, n)))
            elif what == "shard":
                listed.append((pairs, 2, shard_order(n.bit_length() - 1)))
            else:
                listed.append((pairs, 2, None))
        made = add_parts(self.idx, listed, tuple(deps) + (() if self.last is None else (self.last,)), us)
        self.last = made[0][0]
        results = []
        for (chunks, what), parts in zip(jobs, made):
            if isinstance(what, tuple):
                results.append(Sums(parts[0], shard_step(parts[1], what[1], n)))
            elif what == "shard" and direct:
                got = [lax.ppermute(parts[k], "shard", [(i, (i + k) % n) for i in range(n)]) for k in range(1, n)]
                got = [tie(g, *beside) for g in got] if beside else got
                results.append(sum([parts[0].astype(F32)] + [g.astype(F32) for g in got])[0].astype(BF16))
            elif what == "shard":
                keep, recv = parts[0], shard_step(parts[1], 0, n)
                for step in range(1, n.bit_length() - 1):
                    (keep, send), = add_parts(self.idx, [([(keep, recv)], 2, None)])
                    recv = shard_step(send, step, n)
                results.append((keep[0].astype(F32) + recv[0].astype(F32)).astype(BF16))
            else:
                results.append(Sums(parts[0], dp_swap(parts[1], what, self.bits)))
        return results

    def shard_steps(self, chunks, first=0):
        for step in range(first, self.n.bit_length() - 1):
            chunks, = self.run((chunks if isinstance(chunks, list) else [chunks], ("shard", step)))
        return chunks

    def total(self, sums):
        sums = Sums(tie(sums.keep, self.last), tie(sums.recv, self.last))
        return (sums.keep[0].astype(F32) + sums.recv[0].astype(F32)).astype(BF16)

    def collect(self, total, owner):
        total = tie(total, self.last)
        both = jnp.concatenate([total, lax.ppermute(total, "section", [(1 - owner, owner)])])
        quarters = 2**self.bits
        return [both] + [lax.ppermute(both, ("dp", "section"),
                                      [(2 * i + owner, 2 * (i ^ k) + owner) for i in range(quarters)])
                         for k in range(1, quarters)]

    def collect_each(self, total, owner):
        total = tie(total, self.last)
        quarters = 2**self.bits
        own, other = [total], [lax.ppermute(total, "section", [(1 - owner, owner)])]
        for k in range(1, quarters):
            for core, pieces in ((owner, own), (1 - owner, other)):
                route = [(2 * i + core, 2 * (i ^ k) + owner) for i in range(quarters)]
                pieces.append(lax.ppermute(total, ("dp", "section"), route))
        return own + other


def body(boundary, segment_ids, token_valid, attention_gain, attention_bias, query_weight, key_weight, value_weight,
         key_conv, value_conv, out_weight, feed_gain, feed_bias, up_weight, down_weight):
    core = lax.axis_index("section")
    replica = lax.axis_index("dp")
    first = core == 0
    quarters = lax.axis_size("dp")
    bits = quarters.bit_length() - 1
    n = lax.axis_size("shard")
    block = D // n
    idx = jnp.stack([replica, core, lax.axis_index("shard")]).astype(jnp.int32)

    def quarter(weight, width=128):
        return lax.dynamic_slice_in_dim(weight, replica * width, width, weight.ndim - 1)

    vectors = jnp.stack([attention_gain[0], attention_bias[0], feed_gain[0], feed_bias[0]])
    vectors = jnp.pad(vectors, ((0, 12), (0, 128 - block)))
    key_taps = quarter(key_conv[0]).transpose(1, 0, 2).reshape(3 * block, 128)
    value_taps = quarter(value_conv[0]).transpose(1, 0, 2).reshape(3 * block, 128)
    attn_halves = (jnp.concatenate([quarter(query_weight[0]), quarter(key_weight[0]), key_taps, vectors]),
                   jnp.concatenate([quarter(value_weight[0]), quarter(out_weight[0]), value_taps, vectors]))
    up_part = quarter(up_weight[0], 512).reshape(block, 4, 128).transpose(1, 0, 2).reshape(4 * block, 128)
    feed_halves = (quarter(down_weight[0]), up_part)
    pieces = []
    for halves in (attn_halves, feed_halves):
        kept = jnp.where(first, halves[0], halves[1])
        got = swap_cores(jnp.where(first, halves[1], halves[0]))
        pieces.append((jnp.where(first, kept, got), jnp.where(first, got, kept)))

    own_rows = boundary[0].reshape(2, LEN, D)
    mine = lax.dynamic_index_in_dim(own_rows, core, 0, keepdims=False)
    theirs = swap_cores(lax.dynamic_index_in_dim(own_rows, 1 - core, 0, keepdims=False))
    h = jnp.where(first, mine, theirs)
    cot = jnp.where(first, theirs, mine)
    segments = lax.dynamic_index_in_dim(segment_ids.reshape(2, LEN), core, 0, keepdims=False)
    validity = lax.dynamic_index_in_dim(token_valid.reshape(2, LEN), core, 0, keepdims=False)

    square = (n, block, D)
    saved = []

    def run_attn_fwd(length, h, here, own, other, deps):
        gains = here[:, 5 * block:5 * block + 4, :block].transpose(1, 0, 2).reshape(4, 1, D)
        tap, bias = geometry(segments, validity, length)
        outs = [(ROW, F32), (ROW, BF16), (ROW, BF16), (ROW, BF16), (ROW, BF16), ((WIN, D), BF16), ((WIN, D), BF16),
                ((H, WIN, LEN), BF16), ((D, LEN), BF16), ((7,) + square, BF16), ((3,) + square, BF16)]
        made = plain(
            functools.partial(attn_fwd, len(own), length == BLK), [SMEM] + [VMEM] * 5 + [ANY] * (2 * len(own)), outs,
            [VMEM] * 2 + [ANY] * 9,
            [pltpu.VMEM((10,) + square, BF16)] + [pltpu.VMEM(outs[i][0], BF16) for i in (2, 3, 4, 5, 6, 7, 8)]
            + [pltpu.VMEM(ROW, BF16), pltpu.VMEM((256, 4 * WIN), BF16), pltpu.VMEM((D // 128, LEN, 128), F32), DMA((10 * quarters,)), DMA((10,))],
            "attn_fwd", 13, idx, h, bias, tap, gains[0], gains[1], *own, *other, deps=deps, mib=56)
        return gains, tap, made

    def run_feed_fwd(h2, gains, own, other, at, deps):
        outs = [(ROW, BF16), ((LEN, FF), BF16), ((LEN, FF), BF16), ((n, block, FF), BF16), ((n, 4 * block, D), BF16)]
        y, act, slope, up, down = plain(
            functools.partial(feed_fwd, len(own), at, at > 0), [SMEM] + [VMEM] * 3 + [ANY] * (2 * len(own)), outs,
            [VMEM] + [ANY] * 4, [pltpu.VMEM(outs[i][0], BF16) for i in (3, 4, 1, 2)]
            + [pltpu.VMEM(ROW, BF16), pltpu.VMEM((D // 128, LEN, 128), F32), DMA((5 * quarters,)), DMA((10,))],
            "feed_fwd", 13, idx, h2, gains[2], gains[3], *own, *other, deps=deps, mib=56)
        return y, (act, slope, up.reshape(D, FF), down.reshape(FF, D))

    def spread(piece, last_after=None):
        pieces = [piece]
        for step in reversed(range(bits)):
            final = step == 0 and last_after is not None
            pieces += [dp_swap(tie(held, last_after) if final and at else held, step, bits)
                       for at, held in enumerate(list(pieces))]
        return pieces

    def between(own, after):
        return [swap_cores(held if mark is None else tie(held, mark)) for held, mark in zip(own, after)]

    attn_here, = shard_gather(idx, pieces[0][0], n)
    attn_own = spread(attn_here)
    feed_here, = shard_gather(idx, tie(pieces[1][0], attn_here), n, tuple(attn_own[1:3]))
    feed_own = spread(feed_here)
    attn_other = [swap_cores(held) for held in attn_own]
    next_piece = jnp.concatenate([pieces[0][1], pieces[1][1]])
    next_here, = shard_gather(idx, tie(next_piece, feed_here), n, tuple(attn_own[3:] + feed_own[1:3] + attn_other[:3]))
    gains, tap, made = run_attn_fwd(BLK, h, attn_here, attn_own, attn_other, (next_here,))
    h2 = made[0]
    next_own = spread(next_here, h2)
    feed_other = between(feed_own, [None] * 3 + [h2] * (quarters - 3))
    y, feed = run_feed_fwd(h2, gains, feed_own, feed_other, 0, ())
    saved.append((made[1], h2, gains, tap) + tuple(made[2:]) + feed)
    next_other = between(next_own, [h2] * 3 + [y] * (quarters - 3))
    gains, tap, made = run_attn_fwd(LEN, y, next_here, next_own, next_other, ())
    saved.append((made[1], made[0], gains, tap) + tuple(made[2:]) + (None,) * 4)

    rows_feed, rows_conv, rows_proj = 4 * block + 16, 3 * block, 2 * block + 16

    def halves_of(keep, send):
        recv = swap_cores(send)
        return Sums(keep.reshape((-1,) + keep.shape[2:]), recv.reshape((-1,) + recv.shape[2:]))

    def run_feed_bwd(layer, grad, deps=()):
        h, h2, gains, tap, q, kt, vt, ck, cv, p, ot, w, w_proj, act, slope, up, down = saved[layer]
        shape = (quarters, n, rows_feed, 128)
        gh2, keep, send = plain(
            functools.partial(feed_bwd, layer == 1), [SMEM] + [VMEM] * 4 + [ANY] * 4, [(ROW, F32), (shape, BF16), (shape, BF16)], [VMEM, ANY, ANY],
            [pltpu.VMEM((D, FF), BF16), pltpu.VMEM((FF, D), BF16), pltpu.VMEM((LEN, FF), BF16),
             pltpu.VMEM((LEN, FF), BF16), pltpu.VMEM((LEN, FF), BF16), pltpu.VMEM(ROW, BF16),
             pltpu.VMEM((n, block, FF), BF16), pltpu.VMEM((n, 4 * block, D), BF16), pltpu.VMEM((n, 16, 128), BF16),
             pltpu.VMEM(ROW, BF16), pltpu.VMEM((D // 128, LEN, 128), F32), DMA((4,)), DMA((quarters * 7,))],
            "feed_bwd", 7, idx, grad, h2, gains[2], gains[3], up, down, act, slope, deps=deps, mib=56)
        return gh2, halves_of(keep, send)

    def run_feed_both(h2, gains, grad, own, other, at):
        shape = (quarters, n, rows_feed, 128)
        result, gh2, keep, send = plain(
            functools.partial(feed_both, len(own), at), [SMEM] + [VMEM] * 4 + [ANY] * (2 * len(own)),
            [(ROW, BF16), (ROW, F32), (shape, BF16), (shape, BF16)], [VMEM, VMEM, ANY, ANY],
            [pltpu.VMEM((n, block, FF), BF16), pltpu.VMEM((n, 4 * block, D), BF16)] + [pltpu.VMEM((LEN, FF), BF16)] * 3
            + [pltpu.VMEM(ROW, BF16), pltpu.VMEM((n, block, FF), BF16), pltpu.VMEM((n, 4 * block, D), BF16),
               pltpu.VMEM((n, 16, 128), BF16), pltpu.VMEM(ROW, BF16), pltpu.VMEM((D // 128, LEN, 128), F32),
               DMA((5 * quarters,)), DMA((quarters * 7,))],
            "feed_both", 20, idx, h2, gains[2], gains[3], grad, *own, *other, mib=56)
        return result, gh2, halves_of(keep, send)

    def run_attn_bwd(layer, gh2, deps=()):
        h, h2, gains, tap, q, kt, vt, ck, cv, p, ot, w, w_proj, act, slope, up, down = saved[layer]
        shape = (quarters, n, rows_conv, 128)
        gq, gk, gv, keep, send = plain(
            attn_bwd, [SMEM, VMEM, VMEM] + [ANY] * 4 + [VMEM] * 2 + [ANY],
            [(ROW, BF16)] * 3 + [(shape, BF16), (shape, BF16)], [ANY] * 5,
            [pltpu.VMEM((7,) + square, BF16)] + [pltpu.VMEM(ROW, BF16)] * 3 + [pltpu.VMEM((H, WIN, LEN), BF16)]
            + [pltpu.VMEM(ROW, BF16)] * 4 + [pltpu.VMEM((WIN, D), BF16)] * 2
            + [pltpu.VMEM((6,) + square, BF16), pltpu.VMEM((4 * WIN, LEN), BF16), pltpu.VMEM((256, 4 * WIN), BF16), DMA((7,)), DMA((3,)), DMA((quarters * 6,))],
            "attn_bwd", 7, idx, gh2, tap, w, q, kt, vt, ck, cv, p, deps=deps, mib=50)
        return gq, gk, gv, halves_of(keep, send)

    def run_proj_bwd(layer, gh2, gq, gk, gv, deps=()):
        h, h2, gains, tap, q, kt, vt, ck, cv, p, ot, w, w_proj, act, slope, up, down = saved[layer]
        shape = (quarters, n, rows_proj, 128)
        grad, keep, send = plain(
            functools.partial(proj_bwd, layer == 0), [SMEM] + [VMEM] * 4 + [ANY] + [VMEM] * 3 + [ANY], [(ROW, BF16), (shape, BF16), (shape, BF16)],
            [VMEM, ANY, ANY],
            [pltpu.VMEM((3,) + square, BF16), pltpu.VMEM((D, LEN), BF16), pltpu.VMEM(ROW, BF16),
             pltpu.VMEM((4,) + square, BF16), pltpu.VMEM((n, 16, 128), BF16), pltpu.VMEM((D // 128, LEN, 128), F32), DMA((3,)), DMA((quarters * 6,))],
            "proj_bwd", 6, idx, gh2, h, gains[0], gains[1], w_proj, gq, gk, gv, ot, deps=deps, mib=50)
        return grad, halves_of(keep, send)

    hops = Hops(idx, n, bits)
    result, gh2, feed_two = run_feed_both(saved[1][1], saved[1][2], cot, next_own, next_other, 5 * block + 16)
    gq, gk, gv, conv_two = run_attn_bwd(1, gh2)
    hops.last = gq
    feed_two, = hops.run(([feed_two], 0))
    grad, proj_two = run_proj_bwd(1, gh2, gq, gk, gv, deps=(hops.last,))
    hops.last = grad
    conv_two, = hops.run(([conv_two], 0))
    gh2, feed_one = run_feed_bwd(0, grad, deps=(hops.last,))
    hops.last = gh2
    feed_two, conv_two = hops.run(([feed_two], 1), ([conv_two], 1), us=24)
    mixed, = hops.run(([feed_one, proj_two], 0))
    gq, gk, gv, conv_one = run_attn_bwd(0, gh2, deps=(hops.last,))
    hops.last = gq
    grad, proj_one = run_proj_bwd(0, gh2, gq, gk, gv)
    hops.last = grad
    two, mixed = hops.run(([feed_two, conv_two], ("shard", 0)), ([mixed], 1), us=12)
    attn_one, = hops.run(([conv_one, proj_one], 0))
    two, = hops.run(([two], ("shard", 1)))
    mixed, = hops.run(([mixed], ("shard", 0)), deps=(two.recv,))
    attn_one, = hops.run(([attn_one], 1))
    mark = hops.last
    mixed, = hops.run(([mixed], ("shard", 1)))
    attn_one, = hops.run(([attn_one], "shard"))
    two, mixed = [hops.total(hops.shard_steps(x, 2)) for x in (two, mixed)]
    two_all = hops.collect(jnp.concatenate([two, mixed[rows_feed:]]), 1)
    one_all = hops.collect_each(jnp.concatenate([mixed[:rows_feed], tie(attn_one, *two_all[1:])]), 0)

    result, grad = tie(result, mark), tie(grad, mark)
    other = swap_cores(jnp.where(first, result, grad))
    ours = jnp.where(first, grad, result)
    section_ends = jnp.stack([jnp.where(first, ours, other), jnp.where(first, other, ours)]).reshape(1, 2 * LEN, D)
    total = rows_feed + rows_conv + rows_proj
    shapes = [(4 * block, D), (block, FF), (3, block, D), (3, block, D)] + [(block, D)] * 4
    gdown, gup, gkc, gvc, gq, gk, gv, go = plain(
        functools.partial(unpack, quarters, (0, rows_feed, rows_feed + rows_conv)), [SMEM] + [ANY] * (3 * quarters),
        [(shape, F32) for shape in shapes], [VMEM] * 8,
        [pltpu.VMEM((2, quarters, total, 128), BF16), DMA((2 * quarters,))], "unpack", 4,
        idx, *two_all, *one_all, mib=20)

    def vectors_of(one, two):
        return jnp.where(first, one[:2, :block], two[:2, :block]).astype(F32)

    vec_feed = vectors_of(one_all[0][4 * block:], two_all[0][4 * block:])
    vec_attn = vectors_of(one_all[0][rows_feed + rows_conv + 2 * block:], two_all[0][rows_feed + rows_conv + 2 * block:])
    return (section_ends, vec_attn[0:1], vec_attn[1:2], gq[None], gk[None], gv[None], gkc.transpose(1, 0, 2)[None],
            gvc.transpose(1, 0, 2)[None], go[None], vec_feed[0:1], vec_feed[1:2], gup[None], gdown[None])


def solution(mesh):
    vector, matrix, conv = P("section", "shard"), P("section", "shard", None), P("section", "shard", None, None)
    rows, tokens = P("section", ("dp", "shard"), None), P(("dp", "shard"))
    weights = (vector, vector, matrix, matrix, matrix, conv, conv, matrix, vector, vector, matrix, matrix)
    return jax.shard_map(body, mesh=mesh, in_specs=(rows, tokens, tokens) + weights, out_specs=(rows,) + weights,
                         check_vma=False)
```
